32 devices in a mesh: dp: 16 (over z, y, x), seq: 2 (over core).
Axes of the slice: x: 2, y: 2, z: 4, core: 2. Of those that a mesh axis runs over, the one named last changes fastest.
Arguments:
- tokens: bfloat16 [32, 256, 1024], P('dp', 'seq'), may hold values from -6 to 6
- condition: bfloat16 [32, 768], P('dp'), may hold values from -6 to 6
- positions: int32 [32, 2, 256], P('dp', None, 'seq'), may hold values from 0 to 15, as said below
- weight_codes: int32 [32], P('dp'), may hold values from 0 to 31
- loss_table: float32 [32], replicated, may hold values from 0.25 to 4
- out_grad: bfloat16 [32, 256, 1024], P('dp', 'seq'), may hold values from -6 to 6
- mod_attn: bfloat16 [768, 1024], P('seq'), may hold values from -0.109375 to 0.109375
- qkv_weight: bfloat16 [1024, 3072], P('seq'), may hold values from -0.1875 to 0.1875
- attn_scale: float32 [16], replicated, may hold values from 8 to 24
- out_weight: bfloat16 [1024, 1024], P('seq'), may hold values from -1.5 to 1.5
- mod_ff: bfloat16 [768, 1024], P('seq'), may hold values from -0.109375 to 0.109375
- up_weight: bfloat16 [1024, 6144], P('seq'), may hold values from -0.1875 to 0.1875
- down_weight: bfloat16 [3072, 1024], P('seq'), may hold values from -0.109375 to 0.109375
Outputs:
- mixed: bfloat16 [32, 256, 1024], P('dp', 'seq')
- tokens_grad: float32 [32, 256, 1024], P('dp', 'seq')
- condition_grad: float32 [32, 768], P('dp')
- mod_attn_grad: float32 [768, 1024], P('seq', 'dp')
- qkv_grad: float32 [1024, 3072], P('seq', 'dp')
- scale_grad: float32 [16], replicated
- out_weight_grad: float32 [1024, 1024], P('seq', 'dp')
- mod_ff_grad: float32 [768, 1024], P('seq', 'dp')
- up_grad: float32 [1024, 6144], P('seq', 'dp')
- down_grad: float32 [3072, 1024], P('seq', 'dp')
The draws below stay inside these ranges and needn't reach their ends.
Inputs may be any that keep to these rules, and one draw needn't show every extreme that they name: `positions`: for each image the 256 pairs (row, column) along the middle dimension are the cells of a 16 x 16 grid, each exactly once.
All inputs are finite; a program needn't handle non-finite values.
Results may differ from the reference program's by a relative error of at most 0.023.
Values may be sent and summed in bfloat16 or wider, within the bound.
No kernel may reach another device: no remote copies, remote signals or barrier semaphores. Data moves between devices by JAX's collectives and lax.ppermute only.
A program may use at most 256 MiB of HBM per device.

```python
import math
import jax
import jax.numpy as jnp
import numpy as np
from jax import lax

D = 1024
HEADS = 16
HEAD_DIM = 64
FF = 3072
COND = 768
GRID = 16
LEVELS = 32
TOK_IMG = 256
IMAGES = 32


def draw_positions(key, part):
    key = jax.random.fold_in(key, 7)
    image_keys = jax.random.split(key, IMAGES)
    cells = jax.vmap(lambda image_key: jax.random.permutation(image_key, TOK_IMG))(image_keys).astype(jnp.int32)
    return jnp.stack([cells // GRID, cells % GRID], axis=1).astype(jnp.int32)


def with_ends(values, key, low, top_value):
    place = [jax.random.randint(jax.random.fold_in(key, axis), (), 0, length) for axis, length in enumerate(values.shape)]
    widest = values.shape.index(max(values.shape))
    next_to = place[:widest] + [(place[widest] + 1) % values.shape[widest]] + place[widest + 1:]
    return values.at[tuple(place)].set(low).at[tuple(next_to)].set(top_value)


def block_scale(stream_key, extent, shards, least, high):
    loudness = 1.0
    for axis_at, blocks in shards:
        steps = jax.random.uniform(jax.random.fold_in(jax.random.fold_in(stream_key, 6), axis_at), (blocks,), jnp.float32, least / len(shards), high / len(shards))
        loudness = loudness * jnp.repeat(jnp.exp(steps), extent[axis_at] // blocks).reshape((-1,) + (1,) * (len(extent) - 1 - axis_at))
    return loudness


def cumulative_ranks(count, skew):
    weights = [(1 << 20) // math.isqrt(grade ** skew) + 1 for grade in range(1, count + 1)]
    width = 1 + sum(weights) // (1 << 30)
    return np.cumsum(np.array([max(1, weight // width) for weight in weights]))


def ranked(rng, shape, number_of, slope):
    table = cumulative_ranks(number_of, slope)
    pick = jax.random.randint(jax.random.fold_in(rng, 1), shape, 0, int(table[number_of - 1]))
    rank = jnp.searchsorted(jnp.asarray(table, jnp.int32), pick, side="right")
    return jax.random.permutation(jax.random.fold_in(rng, 2), number_of)[rank].astype(jnp.int32)


def scatter_about(key, dims, deviation, limit, shards=(), kind=jnp.bfloat16):
    loudness = block_scale(key, dims, shards, -0.22, 0.18) if shards else 1.0
    drawn = jax.random.normal(key, dims, jnp.float32) * deviation * loudness
    return jnp.minimum(jnp.maximum(drawn, -limit), limit).astype(kind)


def setup_inputs(seed: int = 0) -> dict:
    seeds = jax.random.split(jax.random.key(seed), 14)
    return {
        "tokens": scatter_about(seeds[0], (IMAGES, TOK_IMG, D), 1.0, 6.0, ((0, 16), (1, 2))),
        "condition": scatter_about(seeds[1], (IMAGES, COND), 1.0, 6.0, ((0, 16),)),
        "positions": draw_positions(jax.random.fold_in(seeds[13], 71), 0),
        "weight_codes": with_ends(ranked(seeds[3], (IMAGES,), LEVELS, 2), jax.random.fold_in(seeds[3], 3), 0, LEVELS - 1).astype(jnp.int32),
        "loss_table": jnp.clip(jnp.exp(jax.random.uniform(seeds[4], (LEVELS,), jnp.float32, math.log(0.25), math.log(4.0))), 0.25, 4.0),
        "out_grad": scatter_about(seeds[5], (IMAGES, TOK_IMG, D), 1.0, 6.0, ((0, 16), (1, 2))),
        "mod_attn": scatter_about(seeds[6], (COND, D), (4 * COND) ** -0.5, 0.109375, ((0, 2),)),
        "qkv_weight": scatter_about(seeds[7], (D, 3 * D), D ** -0.5, 0.1875, ((0, 2),)),
        "attn_scale": jnp.clip(jax.random.uniform(seeds[8], (HEADS,), jnp.float32, 8.0, 24.0), 8.0, 24.0),
        "out_weight": scatter_about(seeds[9], (D, D), (D // 64) ** -0.5, 1.5, ((0, 2),)),
        "mod_ff": scatter_about(seeds[10], (COND, D), (4 * COND) ** -0.5, 0.109375, ((0, 2),)),
        "up_weight": scatter_about(seeds[11], (D, 2 * FF), D ** -0.5, 0.1875, ((0, 2),)),
        "down_weight": scatter_about(seeds[12], (FF, D), FF ** -0.5, 0.109375, ((0, 2),)),
    }


epsilon = 1e-06
finest = lax.Precision.HIGHEST

@jax.custom_vjp
def low(v):
    return lax.optimization_barrier(v.astype(jnp.bfloat16)).astype(jnp.float32)

@jax.custom_vjp
def low_back(v):
    return v

def low_keep(v):
    return (low(v), None)

def low_pass(kept, grad):
    return (grad,)

def back_keep(v):
    return (v, None)

def back_low(kept, grad):
    return (low(grad),)
low.defvjp(low_keep, low_pass)
low_back.defvjp(back_keep, back_low)

def norm_mod(values, modulation):
    return values * lax.rsqrt(lax.optimization_barrier(jnp.mean(values * values, axis=-1, keepdims=True)) + epsilon) * (1.0 + modulation[:, None, :])

def angle_tables(positions):
    quarter = HEAD_DIM // 8
    counter = jnp.arange(quarter)[None, :] * HEADS + jnp.arange(HEADS)[:, None]
    frequency = math.pi * jnp.power(10.0, counter.astype(jnp.float32) / (HEADS * quarter))
    coords = (2.0 * positions.astype(jnp.float32) + 1.0) / GRID - 1.0
    angles = jnp.concatenate([coords[:, 0, :, None, None] * frequency, coords[:, 1, :, None, None] * frequency], axis=-1)
    return (jnp.cos(angles), jnp.sin(angles))

def rotate(vectors, cosine_table, sine_table):
    rot_width = cosine_table.shape[-1]
    first = vectors[..., :rot_width]
    second = vectors[..., rot_width:2 * rot_width]
    return jnp.concatenate([first * cosine_table - second * sine_table, second * cosine_table + first * sine_table, vectors[..., 2 * rot_width:]], axis=-1)

def query_key(queries, keys_raw, attn_scale, cosine_table, sine_table):
    root_scale = jnp.sqrt(attn_scale)[:, None]
    queries = queries * lax.rsqrt(lax.optimization_barrier(jnp.sum(queries * queries, axis=-1, keepdims=True)) + epsilon) * root_scale
    keys_raw = keys_raw * lax.rsqrt(lax.optimization_barrier(jnp.sum(keys_raw * keys_raw, axis=-1, keepdims=True)) + epsilon) * root_scale
    return (rotate(queries, cosine_table, sine_table), rotate(keys_raw, cosine_table, sine_table))

def gated_gelu(projected):
    middle = projected.shape[-1] // 2
    return projected[..., :middle] * jax.nn.gelu(projected[..., middle:], approximate=False)

def layer_block(inputs, cond_rows, position_rows, weights):
    mod_attn, qkv_weight, attn_scale, out_weight, mod_ff, up_weight, down_weight = weights
    groups, length, model_width = inputs.shape
    head_shape = (groups, length, HEADS, model_width // HEADS)
    mod_one = jnp.dot(cond_rows, mod_attn, precision=finest)
    mod_two = jnp.dot(cond_rows, mod_ff, precision=finest)
    hidden_one = low(norm_mod(inputs, mod_one))
    projected = low_back(jnp.einsum('gtd,de->gte', hidden_one, qkv_weight, precision=finest))
    cosine_table, sine_table = angle_tables(position_rows)
    queries, keys_rot = query_key(projected[..., :model_width].reshape(head_shape), projected[..., model_width:2 * model_width].reshape(head_shape), attn_scale, cosine_table, sine_table)
    queries = low(queries)
    keys_rot = low(keys_rot)
    values = low(projected[..., 2 * model_width:].reshape(head_shape))
    scores = low_back(jnp.einsum('gthc,gshc->ghts', queries, keys_rot, precision=finest))
    prob_low = low(jax.nn.softmax(scores, axis=-1))
    attended = jnp.einsum('ghts,gshc->gthc', prob_low, values, precision=finest).reshape(groups, length, model_width)
    attended = low(low_back(attended))
    residual = inputs + low_back(jnp.einsum('gtd,de->gte', attended, out_weight, precision=finest))
    hidden_two = low(norm_mod(residual, mod_two))
    gate_up = low_back(jnp.einsum('gtd,de->gte', hidden_two, up_weight, precision=finest))
    activated = low(gated_gelu(gate_up))
    return residual + low_back(jnp.einsum('gtf,fd->gtd', activated, down_weight, precision=finest))

def reference(tokens, condition, positions, weight_codes, loss_table, out_grad, mod_attn, qkv_weight, attn_scale, out_weight, mod_ff, up_weight, down_weight):
    images, length, model_width = tokens.shape
    group_size = math.gcd(images, max(1, 4096 // length))
    group_count = images // group_size
    pos_groups = positions.reshape(group_count, group_size, 2, length)

    def forward(inputs, cond_rows, *weights):

        def scan_step(state_in, pieces):
            return (state_in, layer_block(pieces[0], pieces[1], pieces[2], weights))
        stacked = (inputs.reshape(group_count, group_size, length, model_width), cond_rows.reshape(group_count, group_size, cond_rows.shape[-1]), pos_groups)
        _, outputs = lax.scan(jax.checkpoint(scan_step), None, stacked)
        return outputs.reshape(images, length, model_width)
    floats = tuple((array.astype(jnp.float32) for array in (tokens, condition, mod_attn, qkv_weight, attn_scale, out_weight, mod_ff, up_weight, down_weight)))
    mixed, pullback = jax.vjp(forward, *floats)
    image_scale = loss_table[weight_codes]
    cotangent = out_grad.astype(jnp.float32) * image_scale[:, None, None]
    gradients = pullback(cotangent)
    return (mixed.astype(jnp.bfloat16), gradients[0], gradients[1], gradients[2], gradients[3], gradients[4], gradients[5], gradients[6], gradients[7], gradients[8])
```

```python
import math

import jax
import jax.numpy as jnp
import numpy as np
from jax import lax
from jax.experimental import pallas as pl
from jax.experimental.pallas import tpu as pltpu
from jax.sharding import PartitionSpec as P

HEAD_DIM = 64
GRID = 16
EPS = 1e-06
BF = jnp.bfloat16
F32 = jnp.float32
FINEST = lax.Precision.HIGHEST
LANES = 256
VMEM = 56 * 1024 * 1024


def nn(a, b):
    return lax.dot_general(a, b, (((1,), (0,)), ((), ())), preferred_element_type=F32)


def nt(a, b):
    return lax.dot_general(a, b, (((1,), (1,)), ((), ())), preferred_element_type=F32)


def tn(a, b):
    return lax.dot_general(a, b, (((0,), (0,)), ((), ())), preferred_element_type=F32)


def angle_constants(heads):
    quarter = HEAD_DIM // 8
    counter = np.arange(quarter)[None, :] * heads + np.arange(heads)[:, None]
    freq = (math.pi * np.power(10.0, counter / (heads * quarter))).astype(np.float32)
    coords = ((2.0 * np.arange(GRID) + 1.0) / GRID - 1.0).astype(np.float32)
    angles = (coords[:, None, None] * freq[None]).astype(np.float32).astype(np.float64)
    cos, sin = np.cos(angles), np.sin(angles)
    table = np.zeros((3, 2, GRID, heads, HEAD_DIM))
    q = quarter
    for part in range(2):
        lo = part * q
        table[0, part, :, :, lo : lo + q] = cos
        table[0, part, :, :, 2 * q + lo : 3 * q + lo] = cos
        table[1, part, :, :, lo : lo + q] = -sin
        table[2, part, :, :, 2 * q + lo : 3 * q + lo] = sin
    table[0, 0, :, :, 4 * q :] = 1.0
    return table.reshape(3, 2 * GRID, heads * HEAD_DIM).astype(np.float32)


def segment_matrix():
    rows = lax.broadcasted_iota(jnp.int32, (LANES, LANES), 0) // HEAD_DIM
    cols = lax.broadcasted_iota(jnp.int32, (LANES, LANES), 1) // HEAD_DIM
    return (rows == cols).astype(F32).astype(BF)


def segment_sum(values, ones):
    high = values.astype(BF)
    low = (values - high.astype(F32)).astype(BF)
    return nn(high, ones) + nn(low, ones)


def tables_of(onehot, table):
    return [
        lax.dot_general(
            onehot, table[i], (((1,), (0,)), ((), ())), precision=FINEST, preferred_element_type=F32
        )
        for i in range(3)
    ]


def spin(values, tabs, sign):
    cos, first, second = tabs
    q = HEAD_DIM // 4
    turned = pltpu.roll(values, LANES - q, 1) * first + pltpu.roll(values, q, 1) * second
    return values * cos + sign * turned


def head_masks():
    lane = lax.broadcasted_iota(jnp.int32, (1, LANES), 1) // HEAD_DIM
    return [lane == h for h in range(LANES // HEAD_DIM)]


def halves(core, values):
    half = values.shape[1] // 2
    a, b = values[:, :half], values[:, half:]
    return jnp.where(core == 0, a, b), jnp.where(core == 0, b, a)


def whole_of(core, own, other):
    return jnp.concatenate(
        [jnp.where(core == 0, own, other), jnp.where(core == 0, other, own)], axis=1
    )


def normed(values):
    scale = lax.rsqrt(jnp.mean(values * values, axis=-1, keepdims=True) + EPS)
    return values * scale, scale


def norm_back(unit, scale, mod, grad):
    inner = grad * (1.0 + mod)
    into = scale * (inner - unit * jnp.mean(inner * unit, axis=-1, keepdims=True))
    return into, jnp.sum(grad * unit, axis=0, keepdims=True)


def forward_kernel(
    place, x_ref, mod_ref, hot_ref, tab_ref, root_ref, qo, ko, vo, qp, kp, vp,
    q_out, k_out, v_out, att_out, own_out, other_out, own_ref, other_ref,
):
    core = place[0]

    @pl.when(pl.program_id(0) == 0)
    def _():
        unit, _ = normed(x_ref[...].astype(F32))
        own, other = halves(core, (unit * (1.0 + mod_ref[...])).astype(BF))
        own_ref[...] = own
        other_ref[...] = other
        own_out[...] = own
        other_out[...] = other

    own, other = own_ref[...], other_ref[...]
    q = nn(own, qo[...]) + nn(other, qp[...])
    k = nn(own, ko[...]) + nn(other, kp[...])
    v = (nn(own, vo[...]) + nn(other, vp[...])).astype(BF)
    q_out[...] = q
    k_out[...] = k
    v_out[...] = v
    ones = segment_matrix()
    tabs = tables_of(hot_ref[...], tab_ref)
    root = root_ref[...]
    qr = spin(q * (lax.rsqrt(segment_sum(q * q, ones) + EPS) * root), tabs, 1.0).astype(BF)
    kr = spin(k * (lax.rsqrt(segment_sum(k * k, ones) + EPS) * root), tabs, 1.0).astype(BF)
    total = jnp.zeros(q.shape, F32)
    zero = jnp.zeros_like(qr)
    for mask in head_masks():
        scores = nt(jnp.where(mask, qr, zero), kr)
        expo = jnp.exp(scores - jnp.max(scores, axis=-1, keepdims=True))
        prob = (expo / jnp.sum(expo, axis=-1, keepdims=True)).astype(BF)
        total = jnp.where(mask, nn(prob, v), total)
    att_out[...] = total.astype(BF)


def feed_kernel(
    place, scale_ref, x_ref, att_ref, mod_ref, og_ref, wo_ref, wp_ref, ao, ap, go, gp, do, dp,
    mixed_out, rgrad_out, rlow_out, mgrad_out, own_out, other_out, act_out, gu_out,
    res_ref, own_ref, other_ref, cot_ref, mix_ref, hgo_ref, hgp_ref,
):
    core = place[0]
    step = pl.program_id(0)
    steps = pl.num_programs(0)
    block = ao.shape[1]

    @pl.when(step == 0)
    def _():
        att_own, att_other = halves(core, att_ref[...])
        residual = (
            x_ref[...].astype(F32) + nn(att_own, wo_ref[...]) + nn(att_other, wp_ref[...])
        )
        res_ref[...] = residual
        unit, _ = normed(residual)
        own, other = halves(core, (unit * (1.0 + mod_ref[...])).astype(BF))
        own_ref[...] = own
        other_ref[...] = other
        own_out[...] = own
        other_out[...] = other
        cot_ref[...] = (og_ref[...].astype(F32) * scale_ref[0, 0]).astype(BF)
        mix_ref[...] = jnp.zeros_like(mix_ref)
        hgo_ref[...] = jnp.zeros_like(hgo_ref)
        hgp_ref[...] = jnp.zeros_like(hgp_ref)

    own, other = own_ref[...], other_ref[...]
    a = nn(own, ao[...]) + nn(other, ap[...])
    g = nn(own, go[...]) + nn(other, gp[...])
    down = jnp.where((step * 2 >= steps) == (core == 1), do[...], dp[...])
    phi = 0.5 * (1.0 + lax.erf(g * (1.0 / math.sqrt(2.0))))
    gelu = g * phi
    act = (a * gelu).astype(BF)
    act_out[...] = act
    mix_ref[...] += nn(act, down)
    act_grad = nt(cot_ref[...], down)
    a_grad = (act_grad * gelu).astype(BF)
    slope = phi + g * (jnp.exp(-0.5 * g * g) * (1.0 / math.sqrt(2.0 * math.pi)))
    g_grad = (act_grad * a * slope).astype(BF)
    at = pl.multiple_of(step * block, block)
    gu_out[:, pl.ds(at, block)] = a_grad
    gu_out[:, pl.ds(pl.multiple_of(steps * block + step * block, block), block)] = g_grad
    hgo_ref[...] += nt(a_grad, ao[...]) + nt(g_grad, go[...])
    hgp_ref[...] += nt(a_grad, ap[...]) + nt(g_grad, gp[...])

    @pl.when(step == steps - 1)
    def _():
        residual = res_ref[...]
        mixed_out[...] = (residual + mix_ref[...]).astype(BF)
        unit, scale = normed(residual)
        into, mgrad = norm_back(
            unit, scale, mod_ref[...], whole_of(core, hgo_ref[...], hgp_ref[...])
        )
        mgrad_out[...] = mgrad
        total = og_ref[...].astype(F32) * scale_ref[0, 0] + into
        rgrad_out[...] = total
        rlow_out[...] = total.astype(BF)


def backward_kernel(
    place, x_ref, mod_ref, hot_ref, tab_ref, root_ref, rgrad_ref, rlow_ref, wo_ref, wp_ref,
    q_ref, k_ref, v_ref, qo, ko, vo, qp, kp, vp,
    qkv_out, scale_out, tgrad_out, mgrad_out, hgo_ref, hgp_ref,
):
    core = place[0]
    step = pl.program_id(0)
    steps = pl.num_programs(0)

    @pl.when(step == 0)
    def _():
        hgo_ref[...] = jnp.zeros_like(hgo_ref)
        hgp_ref[...] = jnp.zeros_like(hgp_ref)

    weight = jnp.where((step * 2 >= steps) == (core == 1), wo_ref[...], wp_ref[...])
    grad = nt(rlow_ref[...], weight).astype(BF)
    ones = segment_matrix()
    tabs = tables_of(hot_ref[...], tab_ref)
    root = root_ref[...]
    q, k, v = q_ref[...], k_ref[...], v_ref[...]
    q_inv = lax.rsqrt(segment_sum(q * q, ones) + EPS)
    k_inv = lax.rsqrt(segment_sum(k * k, ones) + EPS)
    qr = spin(q * (q_inv * root), tabs, 1.0).astype(BF)
    kr = spin(k * (k_inv * root), tabs, 1.0).astype(BF)
    dq = jnp.zeros(q.shape, F32)
    dk = jnp.zeros(q.shape, F32)
    dv = jnp.zeros(q.shape, F32)
    zero = jnp.zeros_like(qr)
    for mask in head_masks():
        scores = nt(kr, jnp.where(mask, qr, zero))
        expo = jnp.exp(scores - jnp.max(scores, axis=0, keepdims=True))
        prob = expo / jnp.sum(expo, axis=0, keepdims=True)
        pgrad = nt(v, jnp.where(mask, grad, zero))
        sgrad = (prob * (pgrad - jnp.sum(prob * pgrad, axis=0, keepdims=True))).astype(BF)
        dq = jnp.where(mask, tn(sgrad, kr), dq)
        dk = jnp.where(mask, nn(sgrad, qr), dk)
        dv = jnp.where(mask, nn(prob.astype(BF), grad), dv)
    dq = spin(dq, tabs, -1.0)
    dk = spin(dk, tabs, -1.0)
    q_scale, k_scale = q_inv * root, k_inv * root
    q_dot, k_dot = dq * q, dk * k
    scale_out[...] = jnp.sum(q_dot * q_scale + k_dot * k_scale, axis=0, keepdims=True)
    gq = (q_scale * (dq - q * (segment_sum(q_dot, ones) * (q_inv * q_inv)))).astype(BF)
    gk = (k_scale * (dk - k * (segment_sum(k_dot, ones) * (k_inv * k_inv)))).astype(BF)
    gv = dv.astype(BF)
    for i, part in enumerate((gq, gk, gv)):
        at = pl.multiple_of((i * steps + step) * LANES, LANES)
        qkv_out[:, pl.ds(at, LANES)] = part
    hgo_ref[...] += nt(gq, qo[...]) + nt(gk, ko[...]) + nt(gv, vo[...])
    hgp_ref[...] += nt(gq, qp[...]) + nt(gk, kp[...]) + nt(gv, vp[...])

    @pl.when(step == steps - 1)
    def _():
        unit, scale = normed(x_ref[...].astype(F32))
        into, mgrad = norm_back(
            unit, scale, mod_ref[...], whole_of(core, hgo_ref[...], hgp_ref[...])
        )
        mgrad_out[...] = mgrad
        tgrad_out[...] = rgrad_ref[...] + into


def weight_kernel(place, bo, bp, ao, ap, send_a, keep_a, send_b, keep_b):
    one, two = place[1], place[2]
    total = tn(bo[...], ao[...]) + tn(bp[...], ap[...])
    cell = total.shape[0] // 4
    half = total.shape[1] // 2
    cells = [total[i * cell : (i + 1) * cell] for i in range(4)]
    for i in range(2):
        zero, unit = cells[2 * i][:, :half], cells[2 * i + 1][:, :half]
        send_a[0, i] = jnp.where(one == 0, unit, zero).astype(BF)
        keep_a[0, i] = jnp.where(one == 0, zero, unit).astype(BF)
        zero, unit = cells[i][:, half:], cells[2 + i][:, half:]
        send_b[0, i] = jnp.where(two == 0, unit, zero).astype(BF)
        keep_b[0, i] = jnp.where(two == 0, zero, unit).astype(BF)


def full(shape):
    return pl.BlockSpec(shape, lambda *_: (0,) * len(shape))


def call(kernel, grid, place, args, specs, outs, out_specs, scratch, flops, moved, exps=0):
    return pl.pallas_call(
        kernel,
        out_shape=outs,
        grid_spec=pltpu.PrefetchScalarGridSpec(
            num_scalar_prefetch=1,
            grid=grid,
            in_specs=specs,
            out_specs=out_specs,
            scratch_shapes=scratch,
        ),
        compiler_params=pltpu.CompilerParams(vmem_limit_bytes=VMEM),
        cost_estimate=pl.CostEstimate(
            flops=int(flops), bytes_accessed=int(moved), transcendentals=int(exps)
        ),
    )(place, *args)


def struct(shape, dtype):
    return jax.ShapeDtypeStruct(shape, dtype)


def shards(n, tokens, condition, positions, weight_codes, loss_table, out_grad, mod_attn,
           qkv_weight, attn_scale, out_weight, mod_ff, up_weight, down_weight):
    images, part, width = tokens.shape
    rows = images * part
    heads = attn_scale.shape[0]
    ff = 2 * down_weight.shape[0]
    low = 1 if n <= 16 else n // 4
    high = n // (4 * low)
    me = lax.axis_index("dp")
    core = lax.axis_index("seq")
    one = (me // low) % 2
    two = (me // (2 * low)) % 2
    place = jnp.stack([core, one, two]).astype(jnp.int32)

    def swap(values):
        return lax.ppermute(values, "seq", [(0, 1), (1, 0)])

    def cross(values, stride):
        return lax.ppermute(
            values, "dp", [(i, i + stride - 2 * stride * ((i // stride) % 2)) for i in range(n)]
        )

    def pick(values, index, axis=0):
        return lax.dynamic_index_in_dim(values, index, axis, keepdims=False)

    x = jnp.concatenate([pick(tokens, core), swap(pick(tokens, 1 - core))], axis=0)
    pos = jnp.concatenate([pick(positions, core), swap(pick(positions, 1 - core))], axis=1)
    mods = jnp.concatenate([mod_attn, mod_ff], axis=1)
    cond_rows = mod_attn.shape[0]
    cond_own = lax.dynamic_slice_in_dim(condition, core * cond_rows, cond_rows, 1)
    mod_part = jnp.dot(cond_own, mods, preferred_element_type=F32)
    mod_mine = pick(mod_part, core) + swap(pick(mod_part, 1 - core))
    mod_one, mod_two = mod_mine[None, :width], mod_mine[None, width:]
    qkv_other = swap(qkv_weight)
    out_other = swap(out_weight)
    og = jnp.concatenate([pick(out_grad, core), swap(pick(out_grad, 1 - core))], axis=0)
    late_up, late_down, qkv_other = lax.optimization_barrier((up_weight, down_weight, qkv_other))
    up_other = swap(late_up)
    down_other = swap(late_down)

    cells = lax.broadcasted_iota(jnp.int32, (rows, GRID), 1)
    onehot = jnp.concatenate(
        [(pos[0][:, None] == cells).astype(F32), (pos[1][:, None] == cells).astype(F32)], axis=1
    )
    table = jnp.asarray(angle_constants(heads))
    root = jnp.repeat(jnp.sqrt(attn_scale), HEAD_DIM)[None, :]

    steps = width // LANES
    half = width // 2
    col = pl.BlockSpec((rows, LANES), lambda j, p: (0, j))
    shared = [
        full((rows, width)),
        full((1, width)),
        full((rows, 2 * GRID)),
        pl.BlockSpec((3, 2 * GRID, LANES), lambda j, p: (0, 0, j)),
        pl.BlockSpec((1, LANES), lambda j, p: (0, j)),
    ]
    qkv_specs = [
        pl.BlockSpec((half, LANES), lambda j, p, i=i: (0, i * steps + j)) for i in (0, 1, 2, 0, 1, 2)
    ]
    qkv_args = [qkv_weight] * 3 + [qkv_other] * 3
    q_raw, k_raw, value, attended, h1_own, h1_other = call(
        forward_kernel,
        (steps,),
        place,
        [x, mod_one, onehot, table, root] + qkv_args,
        shared + qkv_specs,
        [struct((rows, width), F32)] * 2 + [struct((rows, width), BF)] * 2 + [struct((rows, half), BF)] * 2,
        [col] * 4 + [full((rows, half))] * 2,
        [pltpu.VMEM((rows, half), BF)] * 2,
        8 * rows * width * width,
        8 * width * width + 8 * rows * width * 2,
        heads * rows * rows,
    )

    levels = loss_table.shape[0]
    picked = (weight_codes[:, None] == jnp.arange(levels)[None, :]).astype(F32)
    image_scale = pick(jnp.sum(picked * loss_table[None, :], axis=1), core)
    cot_low = (og.astype(F32) * image_scale).astype(BF)
    block = 512
    count = ff // block
    up_specs = [
        pl.BlockSpec((half, block), lambda j, p, i=i: (0, i * count + j)) for i in (0, 0, 1, 1)
    ]
    down_specs = [
        pl.BlockSpec(
            (block, width),
            lambda j, p: (jnp.clip(j - p[0] * (count // 2), 0, count // 2 - 1), 0),
        ),
        pl.BlockSpec(
            (block, width),
            lambda j, p: (jnp.clip(j - (1 - p[0]) * (count // 2), 0, count // 2 - 1), 0),
        ),
    ]
    mixed_mine, res_grad, res_low, mod_two_grad, h2_own, h2_other, act, gate_up = call(
        feed_kernel,
        (count,),
        place,
        [image_scale.reshape(1, 1), x, attended, mod_two, og, out_weight, out_other]
        + [up_weight, up_other, up_weight, up_other, down_weight, down_other],
        [
            pl.BlockSpec(memory_space=pltpu.SMEM),
            full((rows, width)),
            full((rows, width)),
            full((1, width)),
            full((rows, width)),
            full((half, width)),
            full((half, width)),
        ]
        + up_specs
        + down_specs,
        [
            struct((rows, width), BF),
            struct((rows, width), F32),
            struct((rows, width), BF),
            struct((1, width), F32),
            struct((rows, half), BF),
            struct((rows, half), BF),
            struct((rows, ff), BF),
            struct((rows, 2 * ff), BF),
        ],
        [
            full((rows, width)),
            full((rows, width)),
            full((rows, width)),
            full((1, width)),
            full((rows, half)),
            full((rows, half)),
            pl.BlockSpec((rows, block), lambda j, p: (0, j)),
            full((rows, 2 * ff)),
        ],
        [
            pltpu.VMEM((rows, width), F32),
            pltpu.VMEM((rows, half), BF),
            pltpu.VMEM((rows, half), BF),
            pltpu.VMEM((rows, width), BF),
            pltpu.VMEM((rows, width), F32),
            pltpu.VMEM((rows, half), F32),
            pltpu.VMEM((rows, half), F32),
        ],
        2 * rows * width * (width + 6 * ff),
        2 * width * (width + 3 * ff) + 12 * rows * ff,
        2 * rows * ff,
    )

    def weight_grad(cols_own, cols_other, rows_own, rows_other):
        cols = cols_own.shape[1]
        depth = rows_other.shape[1]
        cell = cols // (4 * high)
        at = 0 if rows_own.shape[1] == depth else 1
        outs = [struct((high, 2, cell, depth // 2), BF)] * 4
        return call(
            weight_kernel,
            (high,),
            place,
            [cols_own, cols_other, rows_own, rows_other],
            [pl.BlockSpec((rows, 4 * cell), lambda j, p: (0, j))] * 2
            + [
                pl.BlockSpec((rows, depth), lambda j, p: (0, at * p[0])),
                full((rows, depth)),
            ],
            outs,
            [pl.BlockSpec((1, 2, cell, depth // 2), lambda j, p: (j, 0, 0, 0))] * 4,
            [],
            4 * rows * cols * depth,
            4 * rows * (cols + depth) + 2 * cols * depth,
        )

    def plane_sum(parts):
        send_a, keep_a, send_b, keep_b = parts
        got_a, got_b = cross(send_a, low), cross(send_b, 2 * low)

        def take(values, index):
            return lax.dynamic_index_in_dim(values, index, 1, keepdims=False).astype(F32)

        next_a = (take(keep_a, 1 - two) + take(got_a, 1 - two)).astype(BF)
        next_b = (take(keep_b, 1 - one) + take(got_b, 1 - one)).astype(BF)
        last_a, last_b = cross(next_a, 2 * low), cross(next_b, low)
        sum_a = take(keep_a, two) + take(got_a, two) + last_a.astype(F32)
        sum_b = take(keep_b, one) + take(got_b, one) + last_b.astype(F32)
        both = jnp.concatenate([sum_a, sum_b], axis=-1).astype(BF)
        return both.reshape(high * low, -1, both.shape[-1])

    lines = [
        [h * 4 * low + s * low + i for h in range(high) for i in range(low)] for s in range(4)
    ]

    def line_sum(values):
        return lax.psum_scatter(
            values, "dp", scatter_dimension=0, axis_index_groups=lines, tiled=False
        )

    def other_half(values):
        size = values.shape[1] // 2
        return swap(lax.dynamic_slice_in_dim(values, (1 - core) * size, size, 1))

    down_parts = weight_grad(cot_low, swap(cot_low), act, other_half(act))
    up_parts = weight_grad(gate_up, swap(gate_up), h2_own, swap(h2_other))
    out_parts = weight_grad(res_low, swap(res_low), attended, other_half(attended))

    weight_specs = [
        pl.BlockSpec(
            (LANES, width),
            lambda j, p: (jnp.clip(j - p[0] * (steps // 2), 0, steps // 2 - 1), 0),
        ),
        pl.BlockSpec(
            (LANES, width),
            lambda j, p: (jnp.clip(j - (1 - p[0]) * (steps // 2), 0, steps // 2 - 1), 0),
        ),
    ]
    qkv_grad, scale_lanes, tokens_mine, mod_one_grad = call(
        backward_kernel,
        (steps,),
        place,
        [x, mod_one, onehot, table, root, res_grad, res_low, out_weight, out_other]
        + [q_raw, k_raw, value]
        + qkv_args,
        shared
        + [full((rows, width)), full((rows, width))]
        + weight_specs
        + [col] * 3
        + qkv_specs,
        [
            struct((rows, 3 * width), BF),
            struct((1, width), F32),
            struct((rows, width), F32),
            struct((1, width), F32),
        ],
        [
            full((rows, 3 * width)),
            pl.BlockSpec((1, LANES), lambda j, p: (0, j)),
            full((rows, width)),
            full((1, width)),
        ],
        [pltpu.VMEM((rows, half), F32)] * 2,
        10 * rows * width * width,
        8 * width * width + 20 * rows * width,
        heads * rows * rows,
    )
    qkv_parts = weight_grad(qkv_grad, swap(qkv_grad), h1_own, swap(h1_other))

    down_sum = line_sum(plane_sum(down_parts))
    up_sum = line_sum(plane_sum(up_parts))
    out_plane, qkv_plane = plane_sum(out_parts), plane_sum(qkv_parts)
    last_sum = line_sum(jnp.concatenate([out_plane, qkv_plane], axis=1))
    out_cols = out_plane.shape[1]

    scale_term = jnp.sum(scale_lanes.reshape(heads, HEAD_DIM), axis=1) / (2.0 * attn_scale)
    both_rows = jnp.concatenate([mod_one_grad, mod_two_grad, scale_term[None, :]], axis=1)
    got_rows = swap(both_rows)
    pair = jnp.where(
        core == 0,
        jnp.concatenate([both_rows, got_rows], axis=0),
        jnp.concatenate([got_rows, both_rows], axis=0),
    )
    cond_part = jnp.dot(pair[:, : 2 * width], mods.astype(F32).T, precision=FINEST)
    cond_got = swap(cond_part)
    condition_grad = jnp.where(
        core == 0,
        jnp.concatenate([cond_part, cond_got], axis=1),
        jnp.concatenate([cond_got, cond_part], axis=1),
    )
    grads = pair[:, : 2 * width].reshape(images, 2, width)
    rest = jnp.concatenate([cond_own.astype(F32), pair[:, 2 * width :]], axis=1)
    stride = n // 2
    while stride:
        bit = (me // stride) % 2
        split = grads.reshape(grads.shape[0], 2, 2, -1)
        message = jnp.concatenate(
            [pick(split, 1 - bit, 2).reshape(grads.shape[0], -1), rest], axis=1
        )
        got = cross(message, stride)
        mine = pick(split, bit, 2).reshape(grads.shape[0], -1)
        wide = mine.shape[1]
        mine = jnp.concatenate([mine, rest], axis=1)
        every = jnp.where(
            bit == 0,
            jnp.concatenate([mine, got], axis=0),
            jnp.concatenate([got, mine], axis=0),
        )
        grads = every[:, :wide].reshape(every.shape[0], 2, -1)
        rest = every[:, wide:]
        stride //= 2
    cond_all = rest[:, :cond_rows]
    mod_attn_grad = jnp.dot(cond_all.T, grads[:, 0], precision=FINEST)
    mod_ff_grad = jnp.dot(cond_all.T, grads[:, 1], precision=FINEST)
    scale_grad = jnp.sum(rest[:, cond_rows:], axis=0)

    def home(values):
        got = swap(values[part:])
        own = values[:part]
        return jnp.where(core == 0, jnp.stack([own, got]), jnp.stack([got, own]))

    def turned(values):
        return values.astype(F32).T

    return (
        home(mixed_mine),
        home(tokens_mine),
        condition_grad,
        mod_attn_grad,
        turned(last_sum[out_cols:]),
        scale_grad,
        turned(last_sum[:out_cols]),
        mod_ff_grad,
        turned(up_sum),
        turned(down_sum),
    )


def solution(mesh):
    n = mesh.shape["dp"]

    def body(*args):
        return shards(n, *args)

    return jax.shard_map(
        body,
        mesh=mesh,
        in_specs=(
            P("dp", "seq", None),
            P("dp", None),
            P("dp", None, "seq"),
            P("dp"),
            P(),
            P("dp", "seq", None),
            P("seq", None),
            P("seq", None),
            P(),
            P("seq", None),
            P("seq", None),
            P("seq", None),
            P("seq", None),
        ),
        out_specs=(
            P("dp", "seq", None),
            P("dp", "seq", None),
            P("dp", None),
            P("seq", "dp"),
            P("seq", "dp"),
            P(),
            P("seq", "dp"),
            P("seq", "dp"),
            P("seq", "dp"),
            P("seq", "dp"),
        ),
        check_vma=False,
    )
```

```python
import functools
import math

import jax
import jax.numpy as jnp
import ml_dtypes
import numpy as np
from jax import lax
from jax.experimental import pallas as pl
from jax.experimental.pallas import tpu as pltpu
from jax.sharding import PartitionSpec as P

HEAD_DIM = 64
GRID = 16
EPS = 1e-06
BF = jnp.bfloat16
F32 = jnp.float32
FINEST = lax.Precision.HIGHEST
LANES = 256
VMEM = 63 * 1024 * 1024


def nn(a, b):
    return lax.dot_general(a, b, (((1,), (0,)), ((), ())), preferred_element_type=F32)


def nt(a, b):
    return lax.dot_general(a, b, (((1,), (1,)), ((), ())), preferred_element_type=F32)


def tn(a, b):
    return lax.dot_general(a, b, (((0,), (0,)), ((), ())), preferred_element_type=F32)


def angle_constants(heads):
    quarter = HEAD_DIM // 8
    counter = np.arange(quarter)[None, :] * heads + np.arange(heads)[:, None]
    freq = (math.pi * np.power(10.0, counter / (heads * quarter))).astype(np.float32)
    coords = ((2.0 * np.arange(GRID) + 1.0) / GRID - 1.0).astype(np.float32)
    angles = (coords[:, None, None] * freq[None]).astype(np.float32).astype(np.float64)
    cos, sin = np.cos(angles), np.sin(angles)
    table = np.zeros((3, 2, GRID, heads, HEAD_DIM))
    q = quarter
    for part in range(2):
        lo = part * q
        table[0, part, :, :, lo : lo + q] = cos
        table[0, part, :, :, 2 * q + lo : 3 * q + lo] = cos
        table[1, part, :, :, lo : lo + q] = -sin
        table[2, part, :, :, 2 * q + lo : 3 * q + lo] = sin
    table[0, 0, :, :, 4 * q :] = 1.0
    rest = table.reshape(3, 2 * GRID, heads * HEAD_DIM).astype(np.float32)
    terms = []
    for _ in range(3):
        terms.append(rest.astype(ml_dtypes.bfloat16))
        rest = rest - terms[-1].astype(np.float32)
    return np.concatenate(terms, axis=1)


def segment_matrix():
    rows = lax.broadcasted_iota(jnp.int32, (LANES, LANES), 0) // HEAD_DIM
    cols = lax.broadcasted_iota(jnp.int32, (LANES, LANES), 1) // HEAD_DIM
    return (rows == cols).astype(F32).astype(BF)


def segment_sum(values, ones):
    high = values.astype(BF)
    low = (values - high.astype(F32)).astype(BF)
    return nn(high, ones) + nn(low, ones)


def onehot_of(places):
    cells = lax.broadcasted_iota(jnp.int32, (GRID, places.shape[1]), 0)
    hot = [(places[i : i + 1] == cells).astype(F32) for i in range(2)]
    return jnp.concatenate(hot * 3, axis=0).astype(BF)


def tables_of(onehot, tab_ref, at):
    return [tn(onehot, tab_ref[i, :, at : at + LANES]) for i in range(3)]


def spin(values, tabs, sign):
    cos, first, second = tabs
    q = HEAD_DIM // 4
    turned = pltpu.roll(values, LANES - q, 1) * first + pltpu.roll(values, q, 1) * second
    return values * cos + sign * turned


def head_masks():
    lane = lax.broadcasted_iota(jnp.int32, (1, LANES), 1) // HEAD_DIM
    return [lane == h for h in range(LANES // HEAD_DIM)]


def root_of(scale_ref, group):
    masks = head_masks()
    value = jnp.zeros((1, LANES), F32)
    for h, mask in enumerate(masks):
        value = jnp.where(mask, scale_ref[group * len(masks) + h], value)
    return jnp.sqrt(value)


def normed(values):
    scale = lax.rsqrt(jnp.mean(values * values, axis=-1, keepdims=True) + EPS)
    return values * scale, scale


def norm_back(unit, scale, mod, grad):
    inner = grad * (1.0 + mod)
    into = scale * (inner - unit * jnp.mean(inner * unit, axis=-1, keepdims=True))
    return into, jnp.sum(grad * unit, axis=0, keepdims=True)


def half_of(core, values):
    half = values.shape[1] // 2
    return jnp.where(core == 0, values[:, :half], values[:, half:])


def stacked(masks, values):
    zero = jnp.zeros_like(values)
    return jnp.concatenate([jnp.where(mask, values, zero) for mask in masks], axis=0)


def abreast(values, count):
    size = values.shape[0] // count
    return jnp.concatenate([values[i * size : (i + 1) * size] for i in range(count)], axis=1)


def struct(shape, dtype):
    return jax.ShapeDtypeStruct(shape, dtype)


class In:
    def __init__(self, *arrays, shape=None, plan=None):
        self.arrays, self.shape = arrays, shape or arrays[0].shape
        whole = tuple(slice(None) for _ in self.shape)
        self.plan = plan or (lambda core: [[(0, whole, whole)]])


class Out:
    def __init__(self, shape, dtype, count=1):
        self.struct, self.count = struct(shape, dtype), count


class Held:
    def __init__(self, ref, pieces):
        self.ref, self.shape, self.pieces, self.waited = ref, ref.shape, pieces, set()

    def start(self, piece):
        if piece < len(self.pieces):
            for copy in self.pieces[piece]:
                copy.start()

    def need(self, piece):
        if piece not in self.waited:
            self.waited.add(piece)
            for copy in self.pieces[piece]:
                copy.wait()

    def __getitem__(self, where):
        for piece in range(len(self.pieces)):
            self.need(piece)
        return self.ref[where]


class Made:
    def __init__(self, ref, copies):
        self.ref, self.copies, self.sent = ref, copies, False

    def __setitem__(self, where, values):
        self.ref[where] = values

    def __getitem__(self, where):
        return self.ref[where]

    def send(self):
        if not self.sent:
            self.sent = True
            for copy in self.copies:
                copy.start()


def call(kernel, tables, inputs, outputs, scratch=()):
    arrays = [a for i in inputs for a in i.arrays]
    structs = [o.struct for o in outputs for _ in range(o.count)]

    def body(*refs):
        refs = list(refs)

        def some(count):
            taken = refs[:count]
            del refs[:count]
            return taken

        scalars, sources, targets = some(len(tables)), some(len(arrays)), some(len(structs))
        held, made = some(len(inputs)), some(len(outputs))
        in_sems, out_sems = some(len(inputs)), some(1)[0]
        extra = refs
        ins, outs = [], []
        for i, ref, sems in zip(inputs, held, in_sems):
            from_refs = [sources.pop(0) for _ in i.arrays]
            pieces, count = [], 0
            for piece in i.plan(scalars[0][0]):
                copies = []
                for which, a, b in piece:
                    copies.append(
                        pltpu.make_async_copy(from_refs[which].at[a], ref.at[b], sems.at[count])
                    )
                    count += 1
                pieces.append(copies)
            ins.append(Held(ref, pieces))
        for piece in range(max(len(i.pieces) for i in ins)):
            for i in ins:
                i.start(piece)
        count = 0
        for o, ref in zip(outputs, made):
            copies = []
            for k in range(o.count):
                copies.append(
                    pltpu.make_async_copy(
                        ref if o.count == 1 else ref.at[k], targets.pop(0), out_sems.at[count]
                    )
                )
                count += 1
            outs.append(Made(ref, copies))
        kernel(*scalars, *ins, *outs, *extra)
        for o in outs:
            o.send()
        for i in ins:
            for piece in range(len(i.pieces)):
                i.need(piece)
        for o in outs:
            for copy in o.copies:
                copy.wait()

    results = pl.pallas_call(
        body,
        out_shape=structs,
        in_specs=[pl.BlockSpec(memory_space=pltpu.SMEM)] * len(tables)
        + [pl.BlockSpec(memory_space=pltpu.HBM)] * len(arrays),
        out_specs=[pl.BlockSpec(memory_space=pltpu.HBM)] * len(structs),
        scratch_shapes=[pltpu.VMEM(i.shape, i.arrays[0].dtype) for i in inputs]
        + [
            pltpu.VMEM(o.struct.shape if o.count == 1 else (o.count, *o.struct.shape), o.struct.dtype)
            for o in outputs
        ]
        + [pltpu.SemaphoreType.DMA((sum(len(p) for p in i.plan(0)),)) for i in inputs]
        + [pltpu.SemaphoreType.DMA((len(structs),))]
        + list(scratch),
        compiler_params=pltpu.CompilerParams(vmem_limit_bytes=VMEM),
    )(*tables, *arrays)
    return list(results)


def at_half(core, which, size):
    part = core if which == 0 else 1 - core
    return pl.ds(pl.multiple_of(part * size, size), size)


def by_rows(own, got, parts=1, block=None):
    rows, cols = own.shape
    block = block or cols // parts

    def plan(core):
        for j in range(cols // parts // block):
            piece = []
            for p in range(parts):
                where = slice(p * (cols // parts) + j * block, p * (cols // parts) + (j + 1) * block)
                for k in range(2):
                    piece.append((k, (slice(None), where), (at_half(core, k, rows), where)))
            yield piece

    return In(own, got, shape=(2 * rows, cols), plan=plan)


def by_rows_order(own, got, parts, block, order):
    made = by_rows(own, got, parts, block)
    pieces = made.plan

    def plan(core):
        every = list(pieces(core))
        return [every[i] for i in order]

    made.plan = plan
    return made


def by_row_blocks(own, got, block):
    rows, cols = own.shape

    def plan(core):
        for j in range(rows // block):
            piece = []
            for k in range(2):
                part = core if k == 0 else 1 - core
                there = pl.ds(pl.multiple_of(part * rows + j * block, block), block)
                piece.append((k, (slice(j * block, (j + 1) * block),), (there,)))
            yield piece

    return In(own, got, shape=(2 * rows, cols), plan=plan)


def by_columns(own, other):
    rows, cols = own.shape
    return In(
        own,
        other,
        shape=(rows, 2 * cols),
        plan=lambda core: [
            [(k, (slice(None),), (slice(None), at_half(core, k, cols))) for k in range(2)]
        ],
    )


def image(own, got, mine=True):
    part, width = own.shape[1:]

    def plan(core):
        which = core if mine else 1 - core
        first, second = (0, 1) if mine else (1, 0)
        return [
            [
                (first, (which,), (slice(0, part),)),
                (second, (which,), (slice(part, 2 * part),)),
            ]
        ]

    return In(own, got, shape=(2 * part, width), plan=plan)


def pile(*arrays):
    starts = np.cumsum([0] + [a.shape[0] for a in arrays])

    def plan(core):
        return [
            [
                (i, (slice(None),), (slice(int(starts[i]), int(starts[i + 1])),))
                for i in range(len(arrays))
            ]
        ]

    return In(*arrays, shape=(int(starts[-1]), arrays[0].shape[1]), plan=plan)


def mod_row(core, cond, mod):
    rows = nn(cond[...], mod[...])
    return jnp.where(core == 0, rows[0:1], rows[1:2]), jnp.where(core == 0, rows[1:2], rows[0:1])


def forward_kernel(
    place, scales, x, cond, mod, weight, xs, pos, posg, tab, q_out, k_out, v_out, att, h1, mod_out
):
    core = place[0]
    width = x.shape[1]
    row, row_sib = mod_row(core, cond, mod)
    mod_out[...] = row
    unit, _ = normed(x[...].astype(F32))
    hidden = (unit * (1.0 + row)).astype(BF)
    h1[0] = half_of(core, hidden)
    unit, _ = normed(xs[...].astype(F32))
    h1[1] = half_of(core, (unit * (1.0 + row_sib)).astype(BF))
    h1.send()
    onehot = onehot_of(jnp.concatenate([pos[core], posg[core]], axis=1))
    ones = segment_matrix()
    masks = head_masks()
    heads = len(masks)
    spread = stacked(masks, jnp.ones((LANES, LANES), BF))
    steps = width // LANES
    for j in range(steps):
        here = slice(j * LANES, (j + 1) * LANES)
        weight.need(j)
        q, k, v = [
            nn(hidden, weight.ref[:, i * width + j * LANES : i * width + (j + 1) * LANES])
            for i in range(3)
        ]
        v = v.astype(BF)
        q_out[:, here] = q
        k_out[:, here] = k
        v_out[:, here] = v
        tabs = tables_of(onehot, tab, j * LANES)
        root = root_of(scales, j)
        qr = spin(q * (lax.rsqrt(segment_sum(q * q, ones) + EPS) * root), tabs, 1.0).astype(BF)
        kr = spin(k * (lax.rsqrt(segment_sum(k * k, ones) + EPS) * root), tabs, 1.0).astype(BF)
        expo = abreast(jnp.exp(nt(stacked(masks, qr), kr)).astype(BF), heads)
        total = nn(expo, stacked(masks, v)) / nn(expo, spread)
        lane = (j % (steps // 2)) * LANES
        att[jnp.where(core == j // (steps // 2), 0, 1), :, lane : lane + LANES] = total.astype(BF)


def middle_kernel(place, x, att, weight, cond, mod, h2, hid_out, mod_out, res_out):
    core = place[0]
    row, _ = mod_row(core, cond, mod)
    mod_out[...] = row
    residual = x[...].astype(F32) + nn(att[...], weight[...])
    res_out[...] = residual
    unit, _ = normed(residual)
    hidden = (unit * (1.0 + row)).astype(BF)
    hid_out[...] = hidden
    h2[0] = half_of(core, hidden)
    h2[1] = half_of(1 - core, hidden)


def feed_kernel(
    high, place, codes, losses, hid, up, og, down, ogs, res, mod,
    gu_a, gu_g, act, cots, rlow_out, mixed_out, rgrad_out, mgrad_out, grad_ref, mix_ref,
):
    core, one, two = place[0], place[1], place[2]
    ff = up.shape[1] // 2
    block = ff // 4
    unit_cols = ff // (2 * high)
    half = high // 2
    scale = losses[codes[core]]
    hidden = hid[...]
    cot = (og[...].astype(F32) * scale).astype(BF)
    cots[0] = cot
    cots[1] = (ogs[...].astype(F32) * losses[codes[1 - core]]).astype(BF)
    cots.send()
    for order, b in enumerate((0, 2, 1, 3)):
        here = slice(b * block, (b + 1) * block)
        there = slice(ff + b * block, ff + (b + 1) * block)
        up.need(order)
        down.need(b % 2)
        a = nn(hidden, up.ref[:, here])
        g = nn(hidden, up.ref[:, there])
        phi = 0.5 + 0.5 * lax.erf(g * (1.0 / math.sqrt(2.0)))
        gelu = g * phi
        active = (a * gelu).astype(BF)
        slope = a * (phi + g * (jnp.exp(-0.5 * g * g) * (1.0 / math.sqrt(2.0 * math.pi))))
        act[jnp.where(core == b // 2, 0, 1), :, (b % 2) * block : (b % 2 + 1) * block] = active
        act_grad = nt(cot, down.ref[here])
        a_grad = (act_grad * gelu).astype(BF)
        g_grad = (act_grad * slope).astype(BF)
        for c in range(block // unit_cols):
            cell = b * (block // unit_cols) + c
            cols = slice(c * unit_cols, (c + 1) * unit_cols)
            z, y, x = cell // 4, cell // 2 % 2, cell % 2
            at = (2 * z + y) * unit_cols
            gu_a[jnp.where(one == x, 0, 1), :, at : at + unit_cols] = a_grad[:, cols]
            at = (2 * z + x) * unit_cols
            gu_g[jnp.where(two == y, 0, 1), :, at : at + unit_cols] = g_grad[:, cols]
        mixed = nn(active, down.ref[here])
        grad = nt(a_grad, up.ref[:, here]) + nt(g_grad, up.ref[:, there])
        mix_ref[...] = mixed if order == 0 else mix_ref[...] + mixed
        grad_ref[...] = grad if order == 0 else grad_ref[...] + grad
    for out in (gu_a, gu_g, act):
        out.send()
    residual = res[...]
    mixed_out[...] = (residual + mix_ref[...]).astype(BF)
    mixed_out.send()
    unit, size = normed(residual)
    into, mgrad = norm_back(unit, size, mod[...], grad_ref[...])
    mgrad_out[...] = mgrad
    total = og[...].astype(F32) * scale + into
    rlow_out[...] = total.astype(BF)
    rgrad_out[...] = total


def backward_kernel(
    place, scales, rlow, weight, q_in, k_in, v_in, pos, posg, tab, qkv, x, mod, rgrad,
    qkv_out, scale_out, tgrad_out, mgrad_out,
):
    core = place[0]
    width = x.shape[1]
    onehot = onehot_of(jnp.concatenate([pos[core], posg[core]], axis=1))
    ones = segment_matrix()
    masks = head_masks()
    heads = len(masks)
    low = rlow[...]
    for j in range(width // LANES):
        here = slice(j * LANES, (j + 1) * LANES)
        weight.need(j % 2)
        grad = nt(low, weight.ref[here]).astype(BF)
        tabs = tables_of(onehot, tab, j * LANES)
        root = root_of(scales, j)
        q, k, v = q_in[:, here], k_in[:, here], v_in[:, here]
        q_inv = lax.rsqrt(segment_sum(q * q, ones) + EPS)
        k_inv = lax.rsqrt(segment_sum(k * k, ones) + EPS)
        q_scale, k_scale = q_inv * root, k_inv * root
        qr = spin(q * q_scale, tabs, 1.0).astype(BF)
        kr = spin(k * k_scale, tabs, 1.0).astype(BF)
        q_heads, g_heads = stacked(masks, qr), stacked(masks, grad)
        expo = jnp.exp(nt(kr, q_heads))
        prob = expo * (1.0 / jnp.sum(expo, axis=0, keepdims=True))
        weighted = prob * nt(v, g_heads)
        sgrad = (weighted - prob * jnp.sum(weighted, axis=0, keepdims=True)).astype(BF)
        dv = nn(prob.astype(BF), g_heads).astype(BF)
        dk = spin(nn(sgrad, q_heads), tabs, -1.0)
        size = qr.shape[0]
        turned = jnp.concatenate(
            [sgrad[:, i * size : (i + 1) * size] for i in range(heads)], axis=0
        )
        dq = spin(tn(turned, stacked(masks, kr)), tabs, -1.0)
        q_dot, k_dot = dq * q, dk * k
        scale_out[:, here] = jnp.sum(q_dot * q_scale + k_dot * k_scale, axis=0, keepdims=True)
        gq = (q_scale * (dq - q * (segment_sum(q_dot, ones) * (q_inv * q_inv)))).astype(BF)
        gk = (k_scale * (dk - k * (segment_sum(k_dot, ones) * (k_inv * k_inv)))).astype(BF)
        for i, part in enumerate((gq, gk, dv)):
            qkv_out[:, i * width + j * LANES : i * width + (j + 1) * LANES] = part
    qkv_out.send()
    unit, size = normed(x[...].astype(F32))
    into, mgrad = norm_back(unit, size, mod[...], nt(qkv_out[...], qkv[...]))
    mgrad_out[...] = mgrad
    tgrad_out[...] = rgrad[...] + into


def weight_kernel(cuts, place, *refs):
    one, two = place[1], place[2]
    out_a, out_b = refs[2 * len(cuts) :]
    high = out_a.ref.shape[2]
    start = 0
    for p, cell in enumerate(cuts):
        cols_in, rows_in = refs[2 * p : 2 * p + 2]
        rows = slice(start, start + cell)
        start += cell
        for j in range(high):
            total = tn(cols_in[:, j * 4 * cell : (j + 1) * 4 * cell], rows_in[...]).astype(BF)
            half = total.shape[1] // 2
            for y in range(2):
                for x in range(2):
                    part = total[(2 * y + x) * cell : (2 * y + x + 1) * cell]
                    out_a[jnp.where(one == x, 0, 1), y, j, rows] = part[:, :half]
                    out_b[jnp.where(two == y, 0, 1), x, j, rows] = part[:, half:]


def gate_weight_kernel(place, cols_a, rows_a, cols_g, rows_g, out_a, out_g):
    one, two = place[1], place[2]
    parts, size = out_a.ref.shape[1], out_a.ref.shape[2]
    for cols_in, rows_in, out, mine in ((cols_a, rows_a, out_a, two), (cols_g, rows_g, out_g, one)):
        for z in range(parts):
            total = tn(cols_in[:, 2 * z * size : 2 * (z + 1) * size], rows_in[...]).astype(BF)
            for i in range(2):
                out[jnp.where(mine == i, 0, 1), z] = total[i * size : (i + 1) * size]


def shards(n, tokens, condition, positions, weight_codes, loss_table, out_grad, mod_attn,
           qkv_weight, attn_scale, out_weight, mod_ff, up_weight, down_weight):
    images, part, width = tokens.shape
    rows = images * part
    half = width // 2
    heads = attn_scale.shape[0]
    ff = 2 * down_weight.shape[0]
    low = 1 if n <= 16 else n // 8
    high = n // (4 * low)
    me = lax.axis_index("dp")
    core = lax.axis_index("seq")
    one = (me // low) % 2
    two = (me // (2 * low)) % 2
    place = jnp.stack([core, one, two]).astype(jnp.int32)

    def swap(values):
        return lax.ppermute(values, "seq", [(0, 1), (1, 0)])

    def cross(values, stride):
        return lax.ppermute(
            values, "dp", [(i, i + stride - 2 * stride * ((i // stride) % 2)) for i in range(n)]
        )

    def pick(values, index, axis=0):
        return lax.dynamic_index_in_dim(values, index, axis, keepdims=False)

    def tie(*values):
        return lax.optimization_barrier(values)

    tokens_got, mod_attn_got, pos_got = swap(tokens), swap(mod_attn), swap(positions)
    qkv_got = swap(qkv_weight)
    tokens_got, mod_attn_got, pos_got, qkv_got, *later = tie(
        tokens_got, mod_attn_got, pos_got, qkv_got,
        out_weight, mod_ff, out_grad, up_weight, down_weight,
    )
    out_w, mod_ff_w, og_w, up_w, down_w = later
    out_got, mod_ff_got, og_got = swap(out_w), swap(mod_ff_w), swap(og_w)
    up_got, down_got = swap(up_w), swap(down_w)

    table = In(jnp.asarray(angle_constants(heads)))
    pos_in = [In(positions), In(pos_got)]
    x_in = image(tokens, tokens_got)
    q_raw, k_raw, value, att_own, att_other, h1_own, h1_sib, mod_one = call(
        forward_kernel,
        [place, attn_scale],
        [x_in, In(condition), by_rows(mod_attn, mod_attn_got)]
        + [by_rows(qkv_weight, qkv_got, 3, LANES), image(tokens, tokens_got, False)]
        + pos_in
        + [table],
        [Out((rows, width), F32), Out((rows, width), F32), Out((rows, width), BF)]
        + [Out((rows, half), BF, 2), Out((rows, half), BF, 2), Out((1, width), F32)],
    )
    att_sib = swap(att_other)

    h2_own, h2_other, hidden_two, mod_two, res = call(
        middle_kernel,
        [place],
        [x_in, by_columns(att_own, att_other), by_rows(out_weight, out_got)]
        + [In(condition), by_rows(mod_ff, mod_ff_got)],
        [Out((rows, half), BF, 2), Out((rows, width), BF)]
        + [Out((1, width), F32), Out((rows, width), F32)],
    )
    h2_pair = jnp.concatenate([h2_own, swap(h2_other)], axis=0)
    h2_one, h2_two = cross(h2_pair, low), cross(h2_pair, 2 * low)
    hidden_two, h2_pair = tie(hidden_two, h2_pair)

    block = ff // 4
    gate = call(
        functools.partial(feed_kernel, high),
        [place, weight_codes, loss_table],
        [In(hidden_two), by_rows_order(up_weight, up_got, 2, block, (0, 2, 1, 3))]
        + [image(out_grad, og_got), by_row_blocks(down_weight, down_got, block)]
        + [image(out_grad, og_got, False), In(res), In(mod_two)],
        [Out((rows, ff // 2), BF, 2)] * 3
        + [Out((rows, width), BF, 2), Out((rows, width), BF), Out((rows, width), BF)]
        + [Out((rows, width), F32), Out((1, width), F32)],
        [pltpu.VMEM((rows, width), F32)] * 2,
    )
    keep_a, send_a, keep_g, send_g, act_own, act_other, *rest = gate
    cot, cot_sib, res_low, mixed_mine, res_grad, mod_two_grad = rest
    send_a, send_g, h2_one, h2_two = tie(send_a, send_g, h2_one, h2_two)
    pair_a, pair_g = cross(send_a, low), cross(send_g, 2 * low)
    act_sib, res_sib = swap(act_other), swap(res_low)
    sib_a, sib_g = swap(keep_a), swap(keep_g)

    qkv_grad, scale_lanes, tokens_mine, mod_one_grad = call(
        backward_kernel,
        [place, attn_scale],
        [In(res_low), by_row_blocks(out_weight, out_got, LANES), In(q_raw), In(k_raw), In(value)]
        + pos_in
        + [table, by_rows(qkv_weight, qkv_got), x_in, In(mod_one), In(res_grad)],
        [Out((rows, 3 * width), BF), Out((1, width), F32)]
        + [Out((rows, width), F32), Out((1, width), F32)],
    )
    qkv_grad, cot = tie(qkv_grad, cot)

    def weight_grad(*pairs):
        cuts = [cols.shape[1] // (4 * high) for cols, _ in pairs]
        depth = pairs[0][1].shape[1]
        return call(
            functools.partial(weight_kernel, cuts),
            [place],
            [i for pair in pairs for i in pair],
            [Out((2, high, sum(cuts), depth // 2), BF, 2)] * 2,
        )

    def take(values, index, axis=0):
        return pick(values, index, axis).astype(F32)

    def first_step(parts):
        return cross(parts[1], low), cross(parts[3], 2 * low)

    def second_sent(parts, got):
        next_a = (take(parts[0], 1 - two) + take(got[0], 1 - two)).astype(BF)
        next_b = (take(parts[2], 1 - one) + take(got[1], 1 - one)).astype(BF)
        return next_a, next_b

    def second_step(sent):
        return cross(sent[0], 2 * low), cross(sent[1], low)

    def plane_sum(parts, got, last):
        sum_a = take(parts[0], two) + take(got[0], two) + last[0].astype(F32)
        sum_b = take(parts[2], one) + take(got[1], one) + last[1].astype(F32)
        return jnp.concatenate([sum_a, sum_b], axis=-1).astype(BF)

    high_bits, low_bits = high.bit_length() - 1, low.bit_length() - 1

    def line_start(values):
        cells = values.reshape((2,) * (high_bits + low_bits) + (-1, values.shape[-1]))
        bits = [4 * low << (high_bits - 1 - i) for i in range(high_bits)]
        bits += [1 << (low_bits - 1 - i) for i in range(low_bits)]
        return [cells], bits

    def line_sent(terms, bits):
        axis = max(sum(b >= 4 * low for b in bits) - 1, 0)
        bit = (me // bits[axis]) % 2
        sent = sum(take(t, 1 - bit, axis) for t in terms).astype(BF)
        kept = [pick(t, bit, axis) for t in terms]
        return sent, kept, bits[axis], bits[:axis] + bits[axis + 1 :]

    def line_step(state):
        sent, kept, stride, bits = line_sent(*state)
        return kept + [cross(sent, stride)], bits

    def line_sum(values):
        state = line_start(values)
        while state[1]:
            state = line_step(state)
        return sum(t.astype(F32) for t in state[0])

    down_parts = weight_grad((pile(cot, cot_sib), pile(act_own, act_sib)))
    pair_a, pair_g, down_parts[1], down_parts[3] = tie(
        pair_a, pair_g, down_parts[1], down_parts[3]
    )
    down_got = first_step(down_parts)
    up_parts = call(
        gate_weight_kernel,
        [place],
        [pile(keep_a, sib_a, pair_a, swap(pair_a)), pile(h2_pair, h2_one)]
        + [pile(keep_g, sib_g, pair_g, swap(pair_g)), pile(h2_pair, h2_two)],
        [Out((high // 2, ff // (2 * high), half), BF, 2)] * 2,
    )
    *down_got, up_parts[1], up_parts[3], qkv_grad = tie(
        *down_got, up_parts[1], up_parts[3], qkv_grad
    )
    up_last = cross(up_parts[1], 2 * low), cross(up_parts[3], low)
    down_sent = second_sent(down_parts, down_got)
    qkv_sib = swap(qkv_grad)
    qkv_sib, *down_sent = tie(qkv_sib, *down_sent)
    down_last = second_step(down_sent)
    last_parts = weight_grad(
        (pile(res_low, res_sib), pile(att_own, att_sib)),
        (pile(qkv_grad, qkv_sib), pile(h1_own, h1_sib)),
    )
    last_got = first_step(last_parts)
    *up_last, last_parts[1] = tie(*up_last, last_parts[1])

    up_plane = jnp.concatenate(
        [
            (up_parts[0].astype(F32) + up_last[0].astype(F32)).astype(BF),
            (up_parts[2].astype(F32) + up_last[1].astype(F32)).astype(BF),
        ],
        axis=0,
    )
    up_sum = line_sum(up_plane)
    down_sum = line_sum(plane_sum(down_parts, down_got, down_last))
    last_last = second_step(second_sent(last_parts, last_got))
    last_sum = line_sum(plane_sum(last_parts, last_got, last_last))
    out_cols = last_sum.shape[0] // 4

    cond_rows = mod_attn.shape[0]
    cond_own = lax.dynamic_slice_in_dim(condition, core * cond_rows, cond_rows, 1)
    mods = jnp.concatenate([mod_attn, mod_ff], axis=1)
    scale_term = jnp.sum(scale_lanes.reshape(heads, HEAD_DIM), axis=1) / (2.0 * attn_scale)
    both_rows = jnp.concatenate([mod_one_grad, mod_two_grad, scale_term[None, :]], axis=1)
    got_rows = swap(both_rows)
    pair = jnp.where(
        core == 0,
        jnp.concatenate([both_rows, got_rows], axis=0),
        jnp.concatenate([got_rows, both_rows], axis=0),
    )
    cond_part = jnp.dot(pair[:, : 2 * width], mods.astype(F32).T, precision=FINEST)
    cond_got = swap(cond_part)
    condition_grad = jnp.where(
        core == 0,
        jnp.concatenate([cond_part, cond_got], axis=1),
        jnp.concatenate([cond_got, cond_part], axis=1),
    )
    grads = pair[:, : 2 * width].reshape(images, 2, width)
    rest = jnp.concatenate([cond_own.astype(F32), pair[:, 2 * width :]], axis=1)
    stride = n // 2
    while stride:
        bit = (me // stride) % 2
        split = grads.reshape(grads.shape[0], 2, 2, -1)
        message = jnp.concatenate(
            [pick(split, 1 - bit, 2).reshape(grads.shape[0], -1), rest], axis=1
        )
        got = cross(message, stride)
        mine = pick(split, bit, 2).reshape(grads.shape[0], -1)
        wide = mine.shape[1]
        mine = jnp.concatenate([mine, rest], axis=1)
        every = jnp.where(
            bit == 0,
            jnp.concatenate([mine, got], axis=0),
            jnp.concatenate([got, mine], axis=0),
        )
        grads = every[:, :wide].reshape(every.shape[0], 2, -1)
        rest = every[:, wide:]
        stride //= 2
    cond_all = rest[:, :cond_rows]
    mod_attn_grad = jnp.dot(cond_all.T, grads[:, 0], precision=FINEST)
    mod_ff_grad = jnp.dot(cond_all.T, grads[:, 1], precision=FINEST)
    scale_grad = jnp.sum(rest[:, cond_rows:], axis=0)

    def home(values):
        got = swap(values[part:])
        own = values[:part]
        return jnp.where(core == 0, jnp.stack([own, got]), jnp.stack([got, own]))

    def turned(values):
        return values.astype(F32).T

    return (
        home(mixed_mine),
        home(tokens_mine),
        condition_grad,
        mod_attn_grad,
        turned(last_sum[out_cols:]),
        scale_grad,
        turned(last_sum[:out_cols]),
        mod_ff_grad,
        turned(up_sum),
        turned(down_sum),
    )


def solution(mesh):
    n = mesh.shape["dp"]

    def body(*args):
        return shards(n, *args)

    return jax.shard_map(
        body,
        mesh=mesh,
        in_specs=(
            P("dp", "seq", None),
            P("dp", None),
            P("dp", None, "seq"),
            P("dp"),
            P(),
            P("dp", "seq", None),
            P("seq", None),
            P("seq", None),
            P(),
            P("seq", None),
            P("seq", None),
            P("seq", None),
            P("seq", None),
        ),
        out_specs=(
            P("dp", "seq", None),
            P("dp", "seq", None),
            P("dp", None),
            P("seq", "dp"),
            P("seq", "dp"),
            P(),
            P("seq", "dp"),
            P("seq", "dp"),
            P("seq", "dp"),
            P("seq", "dp"),
        ),
        check_vma=False,
    )
```

```python
import functools
import math

import jax
import jax.numpy as jnp
import ml_dtypes
import numpy as np
from jax import lax
from jax.experimental import pallas as pl
from jax.experimental.pallas import tpu as pltpu
from jax.sharding import PartitionSpec as P

HEAD_DIM = 64
GRID = 16
EPS = 1e-06
BF = jnp.bfloat16
F32 = jnp.float32
FINEST = lax.Precision.HIGHEST
LANES = 256
VMEM = 63 * 1024 * 1024


def nn(a, b):
    return lax.dot_general(a, b, (((1,), (0,)), ((), ())), preferred_element_type=F32)


def nt(a, b):
    return lax.dot_general(a, b, (((1,), (1,)), ((), ())), preferred_element_type=F32)


def tn(a, b):
    return lax.dot_general(a, b, (((0,), (0,)), ((), ())), preferred_element_type=F32)


def angle_constants(heads):
    quarter = HEAD_DIM // 8
    counter = np.arange(quarter)[None, :] * heads + np.arange(heads)[:, None]
    freq = (math.pi * np.power(10.0, counter / (heads * quarter))).astype(np.float32)
    coords = ((2.0 * np.arange(GRID) + 1.0) / GRID - 1.0).astype(np.float32)
    angles = (coords[:, None, None] * freq[None]).astype(np.float32).astype(np.float64)
    cos, sin = np.cos(angles), np.sin(angles)
    table = np.zeros((3, 2, GRID, heads, HEAD_DIM))
    q = quarter
    for part in range(2):
        lo = part * q
        table[0, part, :, :, lo : lo + q] = cos
        table[0, part, :, :, 2 * q + lo : 3 * q + lo] = cos
        table[1, part, :, :, lo : lo + q] = -sin
        table[2, part, :, :, 2 * q + lo : 3 * q + lo] = sin
    table[0, 0, :, :, 4 * q :] = 1.0
    rest = table.reshape(3, 2 * GRID, heads * HEAD_DIM).astype(np.float32)
    terms = []
    for _ in range(3):
        terms.append(rest.astype(ml_dtypes.bfloat16))
        rest = rest - terms[-1].astype(np.float32)
    return np.concatenate(terms, axis=1)


def segment_matrix():
    rows = lax.broadcasted_iota(jnp.int32, (LANES, LANES), 0) // HEAD_DIM
    cols = lax.broadcasted_iota(jnp.int32, (LANES, LANES), 1) // HEAD_DIM
    return (rows == cols).astype(F32).astype(BF)


def segment_sum(values, ones):
    high = values.astype(BF)
    low = (values - high.astype(F32)).astype(BF)
    return nn(high, ones) + nn(low, ones)


def onehot_of(places):
    cells = lax.broadcasted_iota(jnp.int32, (GRID, places.shape[1]), 0)
    hot = [(places[i : i + 1] == cells).astype(F32) for i in range(2)]
    return jnp.concatenate(hot * 3, axis=0).astype(BF)


def tables_of(onehot, tab_ref, at):
    return [tn(onehot, tab_ref[i, :, at : at + LANES]) for i in range(3)]


def spin(values, tabs, sign):
    cos, first, second = tabs
    q = HEAD_DIM // 4
    turned = pltpu.roll(values, LANES - q, 1) * first + pltpu.roll(values, q, 1) * second
    return values * cos + sign * turned


def head_masks():
    lane = lax.broadcasted_iota(jnp.int32, (1, LANES), 1) // HEAD_DIM
    return [lane == h for h in range(LANES // HEAD_DIM)]


def root_of(scale_ref, group):
    masks = head_masks()
    value = jnp.zeros((1, LANES), F32)
    for h, mask in enumerate(masks):
        value = jnp.where(mask, scale_ref[group * len(masks) + h], value)
    return jnp.sqrt(value)


def normed(values):
    scale = lax.rsqrt(jnp.mean(values * values, axis=-1, keepdims=True) + EPS)
    return values * scale, scale


def norm_back(unit, scale, mod, grad):
    inner = grad * (1.0 + mod)
    into = scale * (inner - unit * jnp.mean(inner * unit, axis=-1, keepdims=True))
    return into, jnp.sum(grad * unit, axis=0, keepdims=True)


def half_of(core, values):
    half = values.shape[1] // 2
    return jnp.where(core == 0, values[:, :half], values[:, half:])


def stacked(masks, values):
    zero = jnp.zeros_like(values)
    return jnp.concatenate([jnp.where(mask, values, zero) for mask in masks], axis=0)


def abreast(values, count):
    size = values.shape[0] // count
    return jnp.concatenate([values[i * size : (i + 1) * size] for i in range(count)], axis=1)


def struct(shape, dtype):
    return jax.ShapeDtypeStruct(shape, dtype)


class In:
    def __init__(self, *arrays, shape=None, plan=None, late=False):
        self.arrays, self.shape, self.late = arrays, shape or arrays[0].shape, late
        whole = tuple(slice(None) for _ in self.shape)
        self.plan = plan or (lambda core: [[(0, whole, whole)]])


class Out:
    def __init__(self, shape, dtype, count=1, pieces=1, axis=1, into=()):
        self.struct, self.count, self.pieces = struct(shape, dtype), count, pieces
        self.axis, self.size = axis, shape[axis] // pieces
        self.into = dict(into)

    def where(self, piece):
        if self.pieces == 1:
            return ...
        return (slice(None),) * self.axis + (slice(piece * self.size, (piece + 1) * self.size),)


class Held:
    def __init__(self, ref, pieces):
        self.ref, self.shape, self.pieces = ref, ref.shape, pieces
        self.started, self.waited = set(), set()

    def start(self, piece):
        if piece < len(self.pieces) and piece not in self.started:
            self.started.add(piece)
            for copy in self.pieces[piece]:
                copy.start()

    def need(self, piece):
        self.start(piece)
        if piece not in self.waited:
            self.waited.add(piece)
            for copy in self.pieces[piece]:
                copy.wait()

    def start_all(self):
        for piece in range(len(self.pieces)):
            self.start(piece)

    def __getitem__(self, where):
        for piece in range(len(self.pieces)):
            self.need(piece)
        return self.ref[where]


class Made:
    def __init__(self, ref, copies):
        self.ref, self.copies, self.sent = ref, copies, set()

    def __setitem__(self, where, values):
        self.ref[where] = values

    def __getitem__(self, where):
        return self.ref[where]

    def send(self, piece=None):
        for i in range(len(self.copies)) if piece is None else (piece,):
            if i not in self.sent:
                self.sent.add(i)
                for copy in self.copies[i]:
                    copy.start()


def call(kernel, tables, inputs, outputs, scratch=()):
    arrays = [a for i in inputs for a in i.arrays]
    names, structs = [], []
    for i, o in enumerate(outputs):
        for k in range(o.count):
            name, column = o.into.get(k, ((i, k), 0))
            if name not in names:
                names.append(name)
                structs.append(o.struct)
            at = names.index(name)
            wide = max(structs[at].shape[-1], column + o.struct.shape[-1])
            structs[at] = struct((*o.struct.shape[:-1], wide), o.struct.dtype)

    def body(*refs):
        refs = list(refs)

        def some(count):
            taken = refs[:count]
            del refs[:count]
            return taken

        scalars, sources, targets = some(len(tables)), some(len(arrays)), some(len(structs))
        held, made = some(len(inputs)), some(len(outputs))
        in_sems, out_sems = some(len(inputs)), some(1)[0]
        extra = refs
        ins, outs = [], []
        for i, ref, sems in zip(inputs, held, in_sems):
            from_refs = [sources.pop(0) for _ in i.arrays]
            pieces, count = [], 0
            for piece in i.plan(scalars[0][0]):
                copies = []
                for which, a, b in piece:
                    copies.append(
                        pltpu.make_async_copy(from_refs[which].at[a], ref.at[b], sems.at[count])
                    )
                    count += 1
                pieces.append(copies)
            ins.append(Held(ref, pieces))
        for i, given in zip(ins, inputs):
            if not given.late:
                i.start(0)
        count = 0
        for o, ref in zip(outputs, made):
            copies = [[] for _ in range(o.pieces)]
            for k in range(o.count):
                name, column = o.into.get(k, ((len(outs), k), 0))
                target, source = targets[names.index(name)], ref if o.count == 1 else ref.at[k]
                if k in o.into:
                    target = target.at[:, column : column + o.struct.shape[-1]]
                for p in range(o.pieces):
                    where = o.where(p)
                    copies[p].append(
                        pltpu.make_async_copy(source.at[where], target.at[where], out_sems.at[count])
                    )
                    count += 1
            outs.append(Made(ref, copies))
        kernel(*scalars, *ins, *outs, *extra)
        for o in outs:
            o.send()
        for i in ins:
            for piece in range(len(i.pieces)):
                i.need(piece)
        for o in outs:
            for piece in o.copies:
                for copy in piece:
                    copy.wait()

    results = pl.pallas_call(
        body,
        out_shape=structs,
        in_specs=[pl.BlockSpec(memory_space=pltpu.SMEM)] * len(tables)
        + [pl.BlockSpec(memory_space=pltpu.HBM)] * len(arrays),
        out_specs=[pl.BlockSpec(memory_space=pltpu.HBM)] * len(structs),
        scratch_shapes=[pltpu.VMEM(i.shape, i.arrays[0].dtype) for i in inputs]
        + [
            pltpu.VMEM(o.struct.shape if o.count == 1 else (o.count, *o.struct.shape), o.struct.dtype)
            for o in outputs
        ]
        + [pltpu.SemaphoreType.DMA((sum(len(p) for p in i.plan(0)),)) for i in inputs]
        + [pltpu.SemaphoreType.DMA((sum(o.count * o.pieces for o in outputs),))]
        + list(scratch),
        compiler_params=pltpu.CompilerParams(vmem_limit_bytes=VMEM),
    )(*tables, *arrays)
    return list(results)


def at_half(core, which, size):
    part = core if which == 0 else 1 - core
    return pl.ds(pl.multiple_of(part * size, size), size)


def by_rows(own, got, parts=1, block=None, late=False):
    rows, cols = own.shape
    block = block or cols // parts

    def plan(core):
        for j in range(cols // parts // block):
            piece = []
            for p in range(parts):
                where = slice(p * (cols // parts) + j * block, p * (cols // parts) + (j + 1) * block)
                for k in range(2):
                    piece.append((k, (slice(None), where), (at_half(core, k, rows), where)))
            yield piece

    return In(own, got, shape=(2 * rows, cols), plan=plan, late=late)


def by_pieces(array, pieces, late=False):
    size = array.shape[-1] // pieces
    wheres = [
        (slice(None),) * (len(array.shape) - 1) + (slice(p * size, (p + 1) * size),)
        for p in range(pieces)
    ]
    return In(array, plan=lambda core: [[(0, where, where)] for where in wheres], late=late)


def by_rows_order(own, got, parts, block, order):
    made = by_rows(own, got, parts, block)
    pieces = made.plan

    def plan(core):
        every = list(pieces(core))
        return [every[i] for i in order]

    made.plan = plan
    return made


def by_row_blocks(own, got, block, late=False):
    rows, cols = own.shape

    def plan(core):
        for j in range(rows // block):
            piece = []
            for k in range(2):
                part = core if k == 0 else 1 - core
                there = pl.ds(pl.multiple_of(part * rows + j * block, block), block)
                piece.append((k, (slice(j * block, (j + 1) * block),), (there,)))
            yield piece

    return In(own, got, shape=(2 * rows, cols), plan=plan, late=late)


def image(own, got, mine=True, late=False):
    part, width = own.shape[1:]

    def plan(core):
        which = core if mine else 1 - core
        first, second = (0, 1) if mine else (1, 0)
        return [
            [
                (first, (which,), (slice(0, part),)),
                (second, (which,), (slice(part, 2 * part),)),
            ]
        ]

    return In(own, got, shape=(2 * part, width), plan=plan, late=late)


def pile(*arrays, width=None, pieces=1, halved=False, late=False):
    arrays = [a if isinstance(a, tuple) else (a, 0) for a in arrays]
    rows, cols = arrays[0][0].shape
    cols = (width or cols) // (2 if halved else 1)
    size = cols // pieces

    def plan(core):
        for p in range(pieces):
            there = slice(p * size, (p + 1) * size)
            piece = []
            for i, (_, first) in enumerate(arrays):
                at = first + p * size
                here = slice(at, at + size)
                if halved:
                    here = pl.ds(pl.multiple_of(core * cols + at, 128), size)
                piece.append((i, (slice(None), here), (slice(i * rows, (i + 1) * rows), there)))
            yield piece

    return In(*[a for a, _ in arrays], shape=(len(arrays) * rows, cols), plan=plan, late=late)


def norm_kernel(place, x, cond, mod, xs, mod_ff, hid_out, h1, row_one, row_two):
    core = place[0]
    rows = nn(cond[...], mod[...])
    first, second = rows[0:1], rows[1:2]
    row, row_sib = jnp.where(core == 0, first, second), jnp.where(core == 0, second, first)
    row_one[...] = row
    unit, _ = normed(x[...].astype(F32))
    hidden = (unit * (1.0 + row)).astype(BF)
    hid_out[...] = hidden
    hid_out.send()
    count = hidden.shape[0]
    h1[:count] = half_of(core, hidden)
    unit, _ = normed(xs[...].astype(F32))
    h1[count:] = half_of(core, (unit * (1.0 + row_sib)).astype(BF))
    h1.send()
    rows = nn(cond[...], mod_ff[...])
    row_two[...] = jnp.where(core == 0, rows[0:1], rows[1:2])


def forward_kernel(
    place, scales, hid, weight, pos, posg, tab, x, out_weight, mod,
    q_out, k_out, v_out, att, hid_out, res_out,
):
    core = place[0]
    width = x.shape[1]
    hidden = hid[...]
    onehot = onehot_of(jnp.concatenate([pos[core], posg[core]], axis=1))
    ones = segment_matrix()
    masks = head_masks()
    heads = len(masks)
    spread = stacked(masks, jnp.ones((LANES, LANES), BF))
    steps = width // LANES
    weight.need(0)
    for j in range(1, steps):
        weight.start(j)
    tab[...]
    for j in range(steps):
        here = slice(j * LANES, (j + 1) * LANES)
        if j == 1:
            for i in (out_weight, x, mod):
                i.start(0)
            weight[...]
            for out in (q_out, k_out, v_out):
                out.send(0)
        q, k, v = [
            nn(hidden, weight.ref[:, i * width + j * LANES : i * width + (j + 1) * LANES])
            for i in range(3)
        ]
        v = v.astype(BF)
        q_out[:, here] = q
        k_out[:, here] = k
        v_out[:, here] = v
        tabs = tables_of(onehot, tab.ref, j * LANES)
        root = root_of(scales, j)
        qr = spin(q * (lax.rsqrt(segment_sum(q * q, ones) + EPS) * root), tabs, 1.0).astype(BF)
        kr = spin(k * (lax.rsqrt(segment_sum(k * k, ones) + EPS) * root), tabs, 1.0).astype(BF)
        expo = abreast(jnp.exp(nt(stacked(masks, qr), kr)).astype(BF), heads)
        total = (nn(expo, stacked(masks, v)) / nn(expo, spread)).astype(BF)
        att[:, here] = total
    for out in (q_out, k_out, v_out, att):
        out.send()
    residual = x[...].astype(F32) + nn(att[...], out_weight[...])
    res_out[...] = residual
    unit, _ = normed(residual)
    hid_out[...] = (unit * (1.0 + mod[...])).astype(BF)


def dealt(values, high, bit, axis):
    size = values.shape[1] // (2 * high)
    kept, sent = [], []
    for cell in range(2 * high):
        if not cell & axis:
            zero = values[:, cell * size : (cell + 1) * size]
            unit = values[:, (cell + axis) * size : (cell + axis + 1) * size]
            kept.append(jnp.where(bit == 0, zero, unit))
            sent.append(jnp.where(bit == 0, unit, zero))
    return jnp.concatenate(kept, axis=1), jnp.concatenate(sent, axis=1)


def feed_kernel(
    high, place, codes, losses, hid, up, og, down, ogs, res, mod,
    gu_a, gu_g, act, rlow_out, cots, mixed_out, rgrad_out, mgrad_out, grad_ref, mix_ref,
):
    core, one, two = place[0], place[1], place[2]
    ff = up.shape[1] // 2
    block = ff // 4
    unit_cols = ff // (2 * high)
    half = high // 2
    scale = losses[codes[core]]
    hidden = hid[...]
    up.need(0)
    for i in (down, og, up):
        i.start(0 if i is not up else 1)
    order = (0, 2, 1, 3)

    def gates(b):
        a = nn(hidden, up.ref[:, b * block : (b + 1) * block])
        return a, nn(hidden, up.ref[:, ff + b * block : ff + (b + 1) * block])

    def finish(b, a, g, first):
        here = slice(b * block, (b + 1) * block)
        there = slice(ff + b * block, ff + (b + 1) * block)
        phi = 0.5 + 0.5 * lax.erf(g * (1.0 / math.sqrt(2.0)))
        gelu = g * phi
        active = (a * gelu).astype(BF)
        slope = a * (phi + g * (jnp.exp(-0.5 * g * g) * (1.0 / math.sqrt(2.0 * math.pi))))
        act[jnp.where(core == b // 2, 0, 1), :, (b % 2) * block : (b % 2 + 1) * block] = active
        act_grad = nt(cot, down.ref[here])
        a_grad = (act_grad * gelu).astype(BF)
        g_grad = (act_grad * slope).astype(BF)
        for c in range(block // unit_cols):
            cell = b * (block // unit_cols) + c
            cols = slice(c * unit_cols, (c + 1) * unit_cols)
            z, y, x = cell // 4, cell // 2 % 2, cell % 2
            at = (2 * z + y) * unit_cols
            gu_a[jnp.where(one == x, 0, 1), :, at : at + unit_cols] = a_grad[:, cols]
            at = (2 * z + x) * unit_cols
            gu_g[jnp.where(two == y, 0, 1), :, at : at + unit_cols] = g_grad[:, cols]
        mixed = nn(active, down.ref[here])
        grad = nt(a_grad, up.ref[:, here]) + nt(g_grad, up.ref[:, there])
        mix_ref[...] = mixed if first else mix_ref[...] + mixed
        grad_ref[...] = grad if first else grad_ref[...] + grad

    gate = gates(order[0])
    up.need(1)
    down.need(0)
    cot = (og[...].astype(F32) * scale).astype(BF)
    cots[0] = cot
    for i in (up, down, ogs, res, mod):
        i.start_all()
    later = gates(order[1])
    finish(order[0], *gate, True)
    for i in (up, down, ogs, res, mod):
        i[...]
    cots[1] = (ogs[...].astype(F32) * losses[codes[1 - core]]).astype(BF)
    for i, b in enumerate(order[1:]):
        gate = later
        if i < 2:
            later = gates(order[i + 2])
        finish(b, *gate, False)
    for out in (act, cots):
        out.send()
    residual = res[...]
    mixed_out[...] = (residual + mix_ref[...]).astype(BF)
    unit, size = normed(residual)
    into, mgrad = norm_back(unit, size, mod[...], grad_ref[...])
    mgrad_out[...] = mgrad
    total = og[...].astype(F32) * scale + into
    low = total.astype(BF)
    rlow_out[...] = low
    middle, end = low.shape[1] // 2, ff // 2
    for out, values, bit, axis in ((gu_a, low[:, :middle], one, 1), (gu_g, low[:, middle:], two, 2)):
        kept, sent = dealt(values, high, bit, axis)
        out[0, :, end:] = kept
        out[1, :, end:] = sent
        out.send()
    rgrad_out[...] = total


def backward_kernel(
    high, place, scales, rlow, weight, q_in, k_in, v_in, pos, posg, tab, qkv, x, mod, rgrad, row_two, cond,
    cells_a, cells_g, mgrad_out, row_out, cond_out, scale_out, tgrad_out, qkv_out,
):
    core, one, two = place[0], place[1], place[2]
    width = x.shape[1]
    onehot = onehot_of(jnp.concatenate([pos[core], posg[core]], axis=1))
    ones = segment_matrix()
    masks = head_masks()
    heads = len(masks)
    low = rlow[...]
    for j in range(width // LANES):
        here = slice(j * LANES, (j + 1) * LANES)
        if j == 0:
            for i in (weight, q_in, k_in, v_in, tab):
                i.need(0)
                i.start_all()
        if j == 1:
            for i in (qkv, x, mod, rgrad, row_two, cond):
                i.start_all()
            for i in (weight, q_in, k_in, v_in, tab):
                i[...]
        grad = nt(low, weight.ref[here]).astype(BF)
        tabs = tables_of(onehot, tab.ref, j * LANES)
        root = root_of(scales, j)
        q, k, v = q_in.ref[:, here], k_in.ref[:, here], v_in.ref[:, here]
        q_inv = lax.rsqrt(segment_sum(q * q, ones) + EPS)
        k_inv = lax.rsqrt(segment_sum(k * k, ones) + EPS)
        q_scale, k_scale = q_inv * root, k_inv * root
        qr = spin(q * q_scale, tabs, 1.0).astype(BF)
        kr = spin(k * k_scale, tabs, 1.0).astype(BF)
        q_heads, g_heads = stacked(masks, qr), stacked(masks, grad)
        expo = jnp.exp(nt(kr, q_heads))
        prob = expo * (1.0 / jnp.sum(expo, axis=0, keepdims=True))
        weighted = prob * nt(v, g_heads)
        sgrad = (weighted - prob * jnp.sum(weighted, axis=0, keepdims=True)).astype(BF)
        dv = nn(prob.astype(BF), g_heads).astype(BF)
        dk = spin(nn(sgrad, q_heads), tabs, -1.0)
        size = qr.shape[0]
        turned = jnp.concatenate(
            [sgrad[:, i * size : (i + 1) * size] for i in range(heads)], axis=0
        )
        dq = spin(tn(turned, stacked(masks, kr)), tabs, -1.0)
        q_dot, k_dot = dq * q, dk * k
        scale_out[:, here] = jnp.sum(q_dot * q_scale + k_dot * k_scale, axis=0, keepdims=True)
        gq = (q_scale * (dq - q * (segment_sum(q_dot, ones) * (q_inv * q_inv)))).astype(BF)
        gk = (k_scale * (dk - k * (segment_sum(k_dot, ones) * (k_inv * k_inv)))).astype(BF)
        for i, part in enumerate((gq, gk, dv)):
            qkv_out[:, i * width + j * LANES : i * width + (j + 1) * LANES] = part
    row_out[...] = row_two[...]
    every = cond[...].astype(F32)
    cond_out[...] = jnp.where(core == 0, every[0:1], every[1:2])
    middle = qkv_out.shape[1] // 2
    for out, at, bit, axis in ((cells_a, 0, one, 1), (cells_g, middle, two, 2)):
        kept, sent = dealt(qkv_out[:, at : at + middle], high, bit, axis)
        out[0] = kept
        out[1] = sent
        out.send()
    unit, size = normed(x[...].astype(F32))
    into, mgrad = norm_back(unit, size, mod[...], nt(qkv_out[...], qkv[...]))
    mgrad_out[...] = mgrad
    tgrad_out[...] = rgrad[...] + into


def down_weight_kernel(place, cols_in, rows_in, out_a, out_b):
    parts, size, half = out_a.ref.shape[1:]
    for j in range(2 * parts):
        total = tn(cols_in[:, j * size : (j + 1) * size], rows_in[...]).astype(BF)
        slot = jnp.where(place[3] == j % 2, 0, 1)
        out_a[slot, j // 2] = total[:, :half]
        out_b[slot, j // 2] = total[:, half:]
        if j % 2:
            out_a.send(j // 2)
            out_b.send(j // 2)


def gate_weight_kernel(cuts, place, *refs):
    one, two = place[1], place[2]
    out_a, out_g = refs[4 * len(cuts) :]
    ins_a, ins_g = refs[: 2 * len(cuts)], refs[2 * len(cuts) : 4 * len(cuts)]
    for ins, out, mine in ((ins_a, out_a, two), (ins_g, out_g, one)):
        if out is out_a:
            for i in ins_a:
                i[...]
            for i in ins_g:
                i.start_all()
        for z in range(out_a.ref.shape[1]):
            start = 0
            for p, size in enumerate(cuts):
                cols_in, rows_in = ins[2 * p : 2 * p + 2]
                total = tn(cols_in[:, 2 * z * size : 2 * (z + 1) * size], rows_in[...]).astype(BF)
                for i in range(2):
                    out[jnp.where(mine == i, 0, 1), z, start : start + size] = total[
                        i * size : (i + 1) * size
                    ]
                start += size
            out.send(z)


def shards(n, tokens, condition, positions, weight_codes, loss_table, out_grad, mod_attn,
           qkv_weight, attn_scale, out_weight, mod_ff, up_weight, down_weight):
    images, part, width = tokens.shape
    rows = images * part
    half = width // 2
    heads = attn_scale.shape[0]
    ff = 2 * down_weight.shape[0]
    low = 1 if n <= 16 else n // 8
    high = n // (4 * low)
    me = lax.axis_index("dp")
    core = lax.axis_index("seq")
    one = (me // low) % 2
    two = (me // (2 * low)) % 2
    three = (me // (4 * low)) % 2
    place = jnp.stack([core, one, two, three]).astype(jnp.int32)

    def swap(values):
        return lax.ppermute(values, "seq", [(0, 1), (1, 0)])

    def cross(values, stride):
        return lax.ppermute(
            values, "dp", [(i, i + stride - 2 * stride * ((i // stride) % 2)) for i in range(n)]
        )

    def pick(values, index, axis=0):
        return lax.dynamic_index_in_dim(values, index, axis, keepdims=False)

    def tie(*values):
        return lax.optimization_barrier(values)

    first = swap(tokens), swap(mod_attn), swap(mod_ff), swap(positions)
    tokens_got, mod_attn_got, mod_ff_got, pos_got, qkv_w, out_w = tie(
        *first, qkv_weight, out_weight
    )
    qkv_got, out_got = swap(qkv_w), swap(out_w)
    hidden_one, h1, mod_one, mod_two = call(
        norm_kernel,
        [place],
        [image(tokens, tokens_got), In(condition), by_rows(mod_attn, mod_attn_got)]
        + [image(tokens, tokens_got, False), by_rows(mod_ff, mod_ff_got)],
        [Out((rows, width), BF), Out((2 * rows, half), BF), Out((1, width), F32)]
        + [Out((1, width), F32)],
    )
    qkv_got, out_got, hidden_one, og_w, up_w, down_w = tie(
        qkv_got, out_got, hidden_one, out_grad, up_weight, down_weight
    )
    og_got, up_got, down_got = swap(og_w), swap(up_w), swap(down_w)
    h1_one, h1_two = cross(h1, low), cross(h1, 2 * low)

    table = In(jnp.asarray(angle_constants(heads)))
    pos_in = [In(positions), In(pos_got)]
    q_raw, k_raw, value, both, res = call(
        forward_kernel,
        [place, attn_scale],
        [In(hidden_one), by_rows(qkv_weight, qkv_got, 3, LANES)]
        + pos_in
        + [table, image(tokens, tokens_got, late=True)]
        + [by_rows(out_weight, out_got, late=True), In(mod_two, late=True)],
        [Out((rows, width), dtype, 1, width // LANES) for dtype in (F32, F32, BF)]
        + [Out((rows, width), BF, into={0: ("both", width)})]
        + [Out((rows, width), BF, into={0: ("both", 0)}), Out((rows, width), F32)],
    )
    both, h1_one, h1_two = tie(both, h1_one, h1_two)
    both_one, both_two, both_sib = cross(both, low), cross(both, 2 * low), swap(both)

    block = ff // 4
    wide = ff // 2 + width // 4
    gate = call(
        functools.partial(feed_kernel, high),
        [place, weight_codes, loss_table],
        [pile((both, 0), width=width), by_rows_order(up_weight, up_got, 2, block, (0, 2, 1, 3))]
        + [image(out_grad, og_got, late=True), by_row_blocks(down_weight, down_got, block, True)]
        + [image(out_grad, og_got, False, True), In(res, late=True), In(mod_two, late=True)],
        [Out((rows, wide), BF, 2, into={0: ("pack", 0)})]
        + [Out((rows, wide), BF, 2, into={0: ("pack", wide)})]
        + [Out((rows, ff // 2), BF, 2, into={1: ("pack", 2 * wide)})]
        + [Out((rows, width), BF), Out((rows, width), BF, 2), Out((rows, width), BF)]
        + [Out((rows, width), F32), Out((1, width), F32)],
        [pltpu.VMEM((rows, width), F32)] * 2,
    )
    pack, send_a, send_g, act_own, res_low, cot, cot_sib, *rest = gate
    mixed_mine, res_grad, mod_two_grad = rest
    send_a, send_g, pack, res_low, both_one, both_two, both_sib = tie(
        send_a, send_g, pack, res_low, both_one, both_two, both_sib
    )
    pair_a, pair_g = cross(send_a, low), cross(send_g, 2 * low)
    pack_sib, both_one_sib, both_two_sib = swap(pack), swap(both_one), swap(both_two)

    third = 3 * width // 4
    cond_cols = condition.shape[1]
    keep_q, send_qa, send_qg, line, tokens_mine = call(
        functools.partial(backward_kernel, high),
        [place, attn_scale],
        [In(res_low), by_row_blocks(out_weight, out_got, LANES)]
        + [by_pieces(a, width // LANES) for a in (q_raw, k_raw, value)]
        + pos_in
        + [table, by_rows(qkv_weight, qkv_got, late=True), image(tokens, tokens_got, True, True)]
        + [In(a, late=True) for a in (mod_one, res_grad, mod_two_grad, condition)],
        [Out((rows, third), BF, 2, into={0: ("keep", 0)})]
        + [Out((rows, third), BF, 2, into={0: ("keep", third)})]
        + [Out((1, width), F32, into={0: ("line", 0)})]
        + [Out((1, width), F32, into={0: ("line", width)})]
        + [Out((1, cond_cols), F32, into={0: ("line", 2 * width)})]
        + [Out((1, width), F32, into={0: ("line", 2 * width + cond_cols)})]
        + [Out((rows, width), F32)],
        [pltpu.VMEM((rows, 3 * width), BF)],
    )
    cot, keep_q, send_qa, send_qg, pack_sib, both_one_sib, both_two_sib = tie(
        cot, keep_q, send_qa, send_qg, pack_sib, both_one_sib, both_two_sib
    )

    def take(values, index, axis=0):
        return pick(values, index, axis).astype(F32)

    high_bits, low_bits = high.bit_length() - 1, low.bit_length() - 1
    high_strides = [4 * low << (high_bits - 1 - i) for i in range(high_bits)]
    low_strides = [1 << (low_bits - 1 - i) for i in range(low_bits)]
    line_strides, line_order = high_strides + low_strides, high_strides[::-1] + low_strides

    def cells_of(values, strides):
        return values.reshape((2,) * len(strides) + (-1, values.shape[-1]))

    def deal(terms, strides, stride):
        axis = strides.index(stride)
        bit = (me // stride) % 2
        sent = sum(take(t, 1 - bit, axis) for t in terms).astype(BF)
        return sent, [pick(t, bit, axis) for t in terms], [s for s in strides if s != stride]

    def finish(terms, strides, order):
        for stride in order:
            sent, terms, strides = deal(terms, strides, stride)
            terms = terms + [cross(sent, stride)]
        return sum(t.astype(F32) for t in terms)

    def hand_on(grads, rest, stride):
        bit = (me // stride) % 2
        split = grads.reshape(grads.shape[0], 2, 2, -1)
        sent = pick(split, 1 - bit, 2).reshape(grads.shape[0], -1)
        got = cross(jnp.concatenate([sent, rest], axis=1), stride)
        return pick(split, bit, 2).reshape(grads.shape[0], -1), rest, got, bit

    def taken(mine, rest, got, bit):
        mine = jnp.concatenate([mine, rest], axis=1)
        every = jnp.where(
            bit == 0,
            jnp.concatenate([mine, got], axis=0),
            jnp.concatenate([got, mine], axis=0),
        )
        wide = mine.shape[1] - rest.shape[1]
        return every[:, :wide].reshape(every.shape[0], 2, -1), every[:, wide:]

    line_steps = [n >> (i + 1) for i in range(n.bit_length() - 1)]
    keep_q_sib = swap(keep_q)
    pair_qa, pair_qg = cross(send_qa, low), cross(send_qg, 2 * low)

    down = call(
        down_weight_kernel,
        [place],
        [pile(cot, cot_sib), pile(act_own, (pack_sib, 2 * wide), width=ff // 2)],
        [Out((high // 2, width // high, ff // 4), BF, 2, high // 2, 0)] * 2,
    )
    pair_a, pair_g, down[0] = tie(pair_a, pair_g, down[0])
    down_got_a = cross(down[1], 4 * low)
    line, down[2] = tie(line, down[2])
    small = hand_on(line[:, : 2 * width].reshape(1, 2, width), line[:, 2 * width :], line_steps[0])

    def rows_of(first, far, far_sib):
        return pile(
            (both, first), (both_sib, first), (far, first), (far_sib, first), width=width, halved=True
        )

    def late(value):
        value.late = True
        return value

    def gate_weight(cuts, ins_a, ins_g):
        return call(
            functools.partial(gate_weight_kernel, cuts),
            [place],
            ins_a + [late(i) for i in ins_g],
            [Out((high // 2, sum(cuts), half), BF, 2, high // 2, 0)] * 2,
        )

    pair_a_sib, pair_g_sib = swap(pair_a), swap(pair_g)
    up_parts = gate_weight(
        [ff // (2 * high)],
        [
            pile(pack, pack_sib, pair_a, pair_a_sib, width=ff // 2),
            rows_of(0, both_one, both_one_sib),
        ],
        [
            pile((pack, wide), (pack_sib, wide), pair_g, pair_g_sib, width=ff // 2),
            rows_of(0, both_two, both_two_sib),
        ],
    )
    small = list(small)
    up_parts[0], down_got_a, pair_qa, pair_qg, keep_q_sib, small[2] = tie(
        up_parts[0], down_got_a, pair_qa, pair_qg, keep_q_sib, small[2]
    )
    up_last = cross(up_parts[1], 2 * low), cross(up_parts[3], low)
    down_got_b = cross(down[3], 4 * low)
    strides = high_strides[:-1] + [2 * low, low] + low_strides
    down_order = high_strides[:-1][::-1] + [low, 2 * low] + low_strides
    sent, down_a, strides_down = deal(
        [cells_of(down[0], strides), cells_of(down_got_a, strides)], strides, down_order[0]
    )
    down_a.append(cross(sent, down_order[0]))
    small = list(hand_on(*taken(*small), line_steps[1]))
    pair_qa_sib, pair_qg_sib = swap(pair_qa), swap(pair_qg)
    at = ff // 2
    last_parts = gate_weight(
        [width // (4 * high), 3 * width // (4 * high)],
        [
            pile((pack, at), (pack_sib, at), (pair_a, at), (pair_a_sib, at), width=width // 4),
            rows_of(width, both_one, both_one_sib),
            pile(keep_q, keep_q_sib, pair_qa, pair_qa_sib, width=third),
            pile(h1, h1_one),
        ],
        [
            pile(
                *((pack, wide + at), (pack_sib, wide + at), (pair_g, at), (pair_g_sib, at)),
                width=width // 4,
            ),
            rows_of(width, both_two, both_two_sib),
            pile((keep_q, third), (keep_q_sib, third), pair_qg, pair_qg_sib, width=third),
            pile(h1, h1_two),
        ],
    )
    last_last = cross(last_parts[1], 2 * low), cross(last_parts[3], low)
    last_parts[0], down_got_b, *up_last = tie(last_parts[0], down_got_b, *up_last)

    def plane(parts, got):
        sums = [parts[2 * i].astype(F32) + got[i].astype(F32) for i in range(2)]
        return cells_of(jnp.concatenate(sums, axis=0).astype(BF), line_strides)

    up_plane = plane(up_parts, up_last)
    sent, up_terms, strides_up = deal([up_plane], line_strides, line_order[0])
    up_terms.append(cross(sent, line_order[0]))
    sent, down_b, _ = deal(
        [cells_of(down[2], strides), cells_of(down_got_b, strides)], strides, down_order[0]
    )
    down_b.append(cross(sent, down_order[0]))
    last_last = list(last_last)
    last_last[0], last_last[1], up_terms[-1], down_a[-1], small[2], mixed_mine, tokens_mine = tie(
        last_last[0], last_last[1], up_terms[-1], down_a[-1], small[2], mixed_mine, tokens_mine
    )
    last_terms = [plane(last_parts, last_last)]
    sent, last_terms, strides_last = deal(last_terms, line_strides, line_order[0])
    last_terms.append(cross(sent, line_order[0]))
    sent, up_terms, strides_up = deal(up_terms, strides_up, line_order[1])
    up_terms.append(cross(sent, line_order[1]))
    grads, rest = taken(*small)
    small = list(hand_on(grads, rest, line_steps[2]))
    down_b[-1], small[2] = tie(down_b[-1], small[2])
    down_terms = [jnp.concatenate([a, b], axis=-1) for a, b in zip(down_a, down_b)]
    sent, down_terms, strides_down = deal(down_terms, strides_down, down_order[1])
    down_terms.append(cross(sent, down_order[1]))
    for step in line_steps[3:]:
        small = hand_on(*taken(*small), step)
    grads, rest = taken(*small)
    last_sum = finish(last_terms, strides_last, line_order[1:])
    up_sum = finish(up_terms, strides_up, line_order[2:])
    down_sum = finish(down_terms, strides_down, down_order[2:])

    cond_rows = mod_attn.shape[0]
    grads = grads.reshape(grads.shape[0], -1)
    wide = grads.shape[1]
    every = jnp.concatenate([grads, rest], axis=1)
    every = jnp.concatenate([every, swap(every)], axis=0)
    cond_all = lax.dynamic_slice_in_dim(every, wide + core * cond_rows, cond_rows, 1)
    mod_attn_grad = jnp.dot(cond_all.T, every[:, : wide // 2], precision=FINEST)
    mod_ff_grad = jnp.dot(cond_all.T, every[:, wide // 2 : wide], precision=FINEST)
    lanes = jnp.sum(every[:, wide + cond_cols :].reshape(2, -1, width), axis=1)
    lanes = jnp.sum((lanes[0] + lanes[1]).reshape(heads, HEAD_DIM), axis=1)
    scale_grad = lanes / (2.0 * attn_scale)

    mods = jnp.concatenate([mod_attn, mod_ff], axis=1)
    mine = line[:, : 2 * width]
    got = swap(mine)
    pair = jnp.where(
        core == 0, jnp.concatenate([mine, got], axis=0), jnp.concatenate([got, mine], axis=0)
    )
    cond_part = jnp.dot(pair, mods.astype(F32).T, precision=FINEST)
    cond_got = swap(cond_part)
    condition_grad = jnp.where(
        core == 0,
        jnp.concatenate([cond_part, cond_got], axis=1),
        jnp.concatenate([cond_got, cond_part], axis=1),
    )

    out_cols = last_sum.shape[0] // 4

    def home(values):
        got = swap(values[part:])
        own = values[:part]
        return jnp.where(core == 0, jnp.stack([own, got]), jnp.stack([got, own]))

    def turned(values):
        return values.astype(F32).T

    return (
        home(mixed_mine),
        home(tokens_mine),
        condition_grad,
        mod_attn_grad,
        turned(last_sum[out_cols:]),
        scale_grad,
        turned(last_sum[:out_cols]),
        mod_ff_grad,
        turned(up_sum),
        turned(down_sum),
    )


def solution(mesh):
    n = mesh.shape["dp"]

    def body(*args):
        return shards(n, *args)

    return jax.shard_map(
        body,
        mesh=mesh,
        in_specs=(
            P("dp", "seq", None),
            P("dp", None),
            P("dp", None, "seq"),
            P("dp"),
            P(),
            P("dp", "seq", None),
            P("seq", None),
            P("seq", None),
            P(),
            P("seq", None),
            P("seq", None),
            P("seq", None),
            P("seq", None),
        ),
        out_specs=(
            P("dp", "seq", None),
            P("dp", "seq", None),
            P("dp", None),
            P("seq", "dp"),
            P("seq", "dp"),
            P(),
            P("seq", "dp"),
            P("seq", "dp"),
            P("seq", "dp"),
            P("seq", "dp"),
        ),
        check_vma=False,
    )
```

```python
import functools
import math

import jax
import jax.numpy as jnp
import ml_dtypes
import numpy as np
from jax import lax
from jax.experimental import pallas as pl
from jax.experimental.pallas import tpu as pltpu
from jax.sharding import PartitionSpec as P

HEAD_DIM = 64
GRID = 16
EPS = 1e-06
BF = jnp.bfloat16
F32 = jnp.float32
FINEST = lax.Precision.HIGHEST
LANES = 256
VMEM = 63 * 1024 * 1024


def nn(a, b):
    return lax.dot_general(a, b, (((1,), (0,)), ((), ())), preferred_element_type=F32)


def nt(a, b):
    return lax.dot_general(a, b, (((1,), (1,)), ((), ())), preferred_element_type=F32)


def tn(a, b):
    return lax.dot_general(a, b, (((0,), (0,)), ((), ())), preferred_element_type=F32)


def angle_constants(heads):
    quarter = HEAD_DIM // 8
    counter = np.arange(quarter)[None, :] * heads + np.arange(heads)[:, None]
    freq = (math.pi * np.power(10.0, counter / (heads * quarter))).astype(np.float32)
    coords = ((2.0 * np.arange(GRID) + 1.0) / GRID - 1.0).astype(np.float32)
    angles = (coords[:, None, None] * freq[None]).astype(np.float32).astype(np.float64)
    cos, sin = np.cos(angles), np.sin(angles)
    table = np.zeros((3, 2, GRID, heads, HEAD_DIM))
    q = quarter
    for part in range(2):
        lo = part * q
        table[0, part, :, :, lo : lo + q] = cos
        table[0, part, :, :, 2 * q + lo : 3 * q + lo] = cos
        table[1, part, :, :, lo : lo + q] = -sin
        table[2, part, :, :, 2 * q + lo : 3 * q + lo] = sin
    table[0, 0, :, :, 4 * q :] = 1.0
    rest = table.reshape(3, 2 * GRID, heads * HEAD_DIM).astype(np.float32)
    terms = []
    for _ in range(3):
        terms.append(rest.astype(ml_dtypes.bfloat16))
        rest = rest - terms[-1].astype(np.float32)
    return np.concatenate(terms, axis=1)


def segment_matrix():
    rows = lax.broadcasted_iota(jnp.int32, (LANES, LANES), 0) // HEAD_DIM
    cols = lax.broadcasted_iota(jnp.int32, (LANES, LANES), 1) // HEAD_DIM
    return (rows == cols).astype(F32).astype(BF)


def segment_sum(values, ones):
    high = values.astype(BF)
    low = (values - high.astype(F32)).astype(BF)
    return nn(high, ones) + nn(low, ones)


def onehot_of(places):
    cells = lax.broadcasted_iota(jnp.int32, (GRID, places.shape[1]), 0)
    hot = [(places[i : i + 1] == cells).astype(F32) for i in range(2)]
    return jnp.concatenate(hot * 3, axis=0).astype(BF)


def tables_of(onehot, tab_ref, at):
    return [tn(onehot, tab_ref[i, :, at : at + LANES]) for i in range(3)]


def spin(values, tabs, sign):
    cos, first, second = tabs
    q = HEAD_DIM // 4
    turned = pltpu.roll(values, LANES - q, 1) * first + pltpu.roll(values, q, 1) * second
    return values * cos + sign * turned


def head_masks():
    lane = lax.broadcasted_iota(jnp.int32, (1, LANES), 1) // HEAD_DIM
    return [lane == h for h in range(LANES // HEAD_DIM)]


def root_of(scale_ref, group):
    masks = head_masks()
    value = jnp.zeros((1, LANES), F32)
    for h, mask in enumerate(masks):
        value = jnp.where(mask, scale_ref[group * len(masks) + h], value)
    return jnp.sqrt(value)


def normed(values):
    scale = lax.rsqrt(jnp.mean(values * values, axis=-1, keepdims=True) + EPS)
    return values * scale, scale


def norm_back(unit, scale, mod, grad):
    inner = grad * (1.0 + mod)
    into = scale * (inner - unit * jnp.mean(inner * unit, axis=-1, keepdims=True))
    return into, jnp.sum(grad * unit, axis=0, keepdims=True)


def half_of(core, values):
    half = values.shape[1] // 2
    return jnp.where(core == 0, values[:, :half], values[:, half:])


def stacked(masks, values):
    zero = jnp.zeros_like(values)
    return jnp.concatenate([jnp.where(mask, values, zero) for mask in masks], axis=0)


def abreast(values, count):
    size = values.shape[0] // count
    return jnp.concatenate([values[i * size : (i + 1) * size] for i in range(count)], axis=1)


def struct(shape, dtype):
    return jax.ShapeDtypeStruct(shape, dtype)


class In:
    def __init__(self, *arrays, shape=None, plan=None, late=False, which=0):
        self.which = which
        self.arrays, self.shape, self.late = arrays, shape or arrays[0].shape, late
        whole = tuple(slice(None) for _ in self.shape)
        self.plan = plan or (lambda core: [[(0, whole, whole)]])


class Out:
    def __init__(self, shape, dtype, count=1, pieces=1, axis=1, into=(), cuts=None):
        self.struct, self.count, self.axis = struct(shape, dtype), count, axis
        self.cuts = cuts or [shape[axis] * i // pieces for i in range(pieces + 1)]
        self.pieces = len(self.cuts) - 1
        self.into = dict(into)

    def where(self, piece):
        if self.pieces == 1:
            return ...
        return (slice(None),) * self.axis + (slice(self.cuts[piece], self.cuts[piece + 1]),)


class Held:
    def __init__(self, ref, pieces):
        self.ref, self.shape, self.pieces = ref, ref.shape, pieces
        self.started, self.waited = set(), set()

    def start(self, piece):
        if piece < len(self.pieces) and piece not in self.started:
            self.started.add(piece)
            for copy in self.pieces[piece]:
                copy.start()

    def need(self, piece):
        self.start(piece)
        if piece not in self.waited:
            self.waited.add(piece)
            for copy in self.pieces[piece]:
                copy.wait()

    def start_all(self):
        for piece in range(len(self.pieces)):
            self.start(piece)

    def __getitem__(self, where):
        for piece in range(len(self.pieces)):
            self.need(piece)
        return self.ref[where]


class Made:
    def __init__(self, ref, copies):
        self.ref, self.copies, self.sent = ref, copies, set()

    def __setitem__(self, where, values):
        self.ref[where] = values

    def __getitem__(self, where):
        return self.ref[where]

    def send(self, piece=None):
        for i in range(len(self.copies)) if piece is None else (piece,):
            if i not in self.sent:
                self.sent.add(i)
                for copy in self.copies[i]:
                    copy.start()


def call(kernel, tables, inputs, outputs, scratch=()):
    arrays = [a for i in inputs for a in i.arrays]
    names, structs = [], []
    for i, o in enumerate(outputs):
        for k in range(o.count):
            name, column = o.into.get(k, ((i, k), 0))
            if name not in names:
                names.append(name)
                structs.append(o.struct)
            at = names.index(name)
            wide = max(structs[at].shape[-1], column + o.struct.shape[-1])
            structs[at] = struct((*o.struct.shape[:-1], wide), o.struct.dtype)

    def body(*refs):
        refs = list(refs)

        def some(count):
            taken = refs[:count]
            del refs[:count]
            return taken

        scalars, sources, targets = some(len(tables)), some(len(arrays)), some(len(structs))
        held, made = some(len(inputs)), some(len(outputs))
        in_sems, out_sems = some(len(inputs)), some(1)[0]
        extra = refs
        ins, outs = [], []
        for i, ref, sems in zip(inputs, held, in_sems):
            from_refs = [sources.pop(0) for _ in i.arrays]
            pieces, count = [], 0
            for piece in i.plan(scalars[0][i.which]):
                copies = []
                for which, a, b in piece:
                    copies.append(
                        pltpu.make_async_copy(from_refs[which].at[a], ref.at[b], sems.at[count])
                    )
                    count += 1
                pieces.append(copies)
            ins.append(Held(ref, pieces))
        for i, given in zip(ins, inputs):
            if not given.late:
                i.start(0)
        count = 0
        for o, ref in zip(outputs, made):
            copies = [[] for _ in range(o.pieces)]
            for k in range(o.count):
                name, column = o.into.get(k, ((len(outs), k), 0))
                target, source = targets[names.index(name)], ref if o.count == 1 else ref.at[k]
                if k in o.into:
                    target = target.at[:, column : column + o.struct.shape[-1]]
                for p in range(o.pieces):
                    where = o.where(p)
                    copies[p].append(
                        pltpu.make_async_copy(source.at[where], target.at[where], out_sems.at[count])
                    )
                    count += 1
            outs.append(Made(ref, copies))
        kernel(*scalars, *ins, *outs, *extra)
        for o in outs:
            o.send()
        for i in ins:
            for piece in range(len(i.pieces)):
                i.need(piece)
        for o in outs:
            for piece in o.copies:
                for copy in piece:
                    copy.wait()

    results = pl.pallas_call(
        body,
        out_shape=structs,
        in_specs=[pl.BlockSpec(memory_space=pltpu.SMEM)] * len(tables)
        + [pl.BlockSpec(memory_space=pltpu.HBM)] * len(arrays),
        out_specs=[pl.BlockSpec(memory_space=pltpu.HBM)] * len(structs),
        scratch_shapes=[pltpu.VMEM(i.shape, i.arrays[0].dtype) for i in inputs]
        + [
            pltpu.VMEM(o.struct.shape if o.count == 1 else (o.count, *o.struct.shape), o.struct.dtype)
            for o in outputs
        ]
        + [pltpu.SemaphoreType.DMA((sum(len(p) for p in i.plan(0)),)) for i in inputs]
        + [pltpu.SemaphoreType.DMA((sum(o.count * o.pieces for o in outputs),))]
        + list(scratch),
        compiler_params=pltpu.CompilerParams(vmem_limit_bytes=VMEM),
    )(*tables, *arrays)
    return list(results)


def at_half(core, which, size):
    part = core if which == 0 else 1 - core
    return pl.ds(pl.multiple_of(part * size, size), size)


def by_rows(own, got, parts=1, block=None, late=False):
    rows, cols = own.shape
    block = block or cols // parts

    def plan(core):
        for j in range(cols // parts // block):
            piece = []
            for p in range(parts):
                where = slice(p * (cols // parts) + j * block, p * (cols // parts) + (j + 1) * block)
                for k in range(2):
                    piece.append((k, (slice(None), where), (at_half(core, k, rows), where)))
            yield piece

    return In(own, got, shape=(2 * rows, cols), plan=plan, late=late)


def by_pieces(array, pieces, late=False):
    size = array.shape[-1] // pieces
    wheres = [
        (slice(None),) * (len(array.shape) - 1) + (slice(p * size, (p + 1) * size),)
        for p in range(pieces)
    ]
    return In(array, plan=lambda core: [[(0, where, where)] for where in wheres], late=late)


def by_rows_order(own, got, parts, block, order):
    made = by_rows(own, got, parts, block)
    pieces = made.plan

    def plan(core):
        every = list(pieces(core))
        return [every[i] for i in order]

    made.plan = plan
    return made


def by_row_blocks(own, got, block, late=False):
    rows, cols = own.shape

    def plan(core):
        for j in range(rows // block):
            piece = []
            for k in range(2):
                part = core if k == 0 else 1 - core
                there = pl.ds(pl.multiple_of(part * rows + j * block, block), block)
                piece.append((k, (slice(j * block, (j + 1) * block),), (there,)))
            yield piece

    return In(own, got, shape=(2 * rows, cols), plan=plan, late=late)


def image(own, got, mine=True, late=False):
    part, width = own.shape[1:]

    def plan(core):
        which = core if mine else 1 - core
        first, second = (0, 1) if mine else (1, 0)
        return [
            [
                (first, (which,), (slice(0, part),)),
                (second, (which,), (slice(part, 2 * part),)),
            ]
        ]

    return In(own, got, shape=(2 * part, width), plan=plan, late=late)


def pile(*arrays, width=None, pieces=1, halved=False, late=False):
    arrays = [a if isinstance(a, tuple) else (a, 0) for a in arrays]
    rows, cols = arrays[0][0].shape
    cols = (width or cols) // (2 if halved else 1)
    size = cols // pieces

    def plan(core):
        for p in range(pieces):
            there = slice(p * size, (p + 1) * size)
            piece = []
            for i, (_, first) in enumerate(arrays):
                at = first + p * size
                here = slice(at, at + size)
                if halved:
                    here = pl.ds(pl.multiple_of(core * cols + at, 128), size)
                piece.append((i, (slice(None), here), (slice(i * rows, (i + 1) * rows), there)))
            yield piece

    return In(*[a for a, _ in arrays], shape=(len(arrays) * rows, cols), plan=plan, late=late)


def norm_kernel(place, x, cond, mod, xs, mod_ff, hid_out, h1, row_one, row_two):
    core = place[0]
    rows = nn(cond[...], mod[...])
    first, second = rows[0:1], rows[1:2]
    row, row_sib = jnp.where(core == 0, first, second), jnp.where(core == 0, second, first)
    row_one[...] = row
    unit, _ = normed(x[...].astype(F32))
    hidden = (unit * (1.0 + row)).astype(BF)
    hid_out[...] = hidden
    hid_out.send()
    half = hidden.shape[1] // 2
    h1[:, :half] = half_of(core, hidden)
    unit, _ = normed(xs[...].astype(F32))
    h1[:, half:] = half_of(core, (unit * (1.0 + row_sib)).astype(BF))
    h1.send()
    rows = nn(cond[...], mod_ff[...])
    row_two[...] = jnp.where(core == 0, rows[0:1], rows[1:2])


def forward_kernel(
    place, scales, hid, weight, pos, posg, tab, x, out_weight, mod,
    q_out, k_out, v_out, att, hid_out, res_out,
):
    core = place[0]
    width = x.shape[1]
    hidden = hid[...]
    onehot = onehot_of(jnp.concatenate([pos[core], posg[core]], axis=1))
    ones = segment_matrix()
    masks = head_masks()
    heads = len(masks)
    spread = stacked(masks, jnp.ones((LANES, LANES), BF))
    steps = width // LANES
    weight.need(0)
    for j in range(1, steps):
        weight.start(j)
    tab[...]
    for j in range(steps):
        here = slice(j * LANES, (j + 1) * LANES)
        if j == 1:
            for i in (out_weight, x, mod):
                i.start(0)
            weight[...]
            for out in (q_out, k_out, v_out):
                out.send(0)
        q, k, v = [
            nn(hidden, weight.ref[:, i * width + j * LANES : i * width + (j + 1) * LANES])
            for i in range(3)
        ]
        v = v.astype(BF)
        q_out[:, here] = q
        k_out[:, here] = k
        v_out[:, here] = v
        tabs = tables_of(onehot, tab.ref, j * LANES)
        root = root_of(scales, j)
        qr = spin(q * (lax.rsqrt(segment_sum(q * q, ones) + EPS) * root), tabs, 1.0).astype(BF)
        kr = spin(k * (lax.rsqrt(segment_sum(k * k, ones) + EPS) * root), tabs, 1.0).astype(BF)
        expo = abreast(jnp.exp(nt(stacked(masks, qr), kr)).astype(BF), heads)
        total = (nn(expo, stacked(masks, v)) / nn(expo, spread)).astype(BF)
        att[:, here] = total
    for out in (q_out, k_out, v_out, att):
        out.send()
    residual = x[...].astype(F32) + nn(att[...], out_weight[...])
    res_out[...] = residual
    unit, _ = normed(residual)
    hid_out[...] = (unit * (1.0 + mod[...])).astype(BF)


def dealt(values, high, bit, axis):
    size = values.shape[1] // (2 * high)
    kept, sent = [], []
    for cell in range(2 * high):
        if not cell & axis:
            zero = values[:, cell * size : (cell + 1) * size]
            unit = values[:, (cell + axis) * size : (cell + axis + 1) * size]
            kept.append(jnp.where(bit == 0, zero, unit))
            sent.append(jnp.where(bit == 0, unit, zero))
    return jnp.concatenate(kept, axis=1), jnp.concatenate(sent, axis=1)


def feed_kernel(
    high, place, codes, losses, hid, up, og, down, ogs, res, mod,
    gu_a, gu_g, act, rlow_out, cots, mixed_out, mgrad_out, grad_ref, mix_ref,
):
    core, one, two = place[0], place[1], place[2]
    ff = up.shape[1] // 2
    block = ff // 4
    unit_cols = ff // (2 * high)
    half = high // 2
    scale = losses[codes[core]]
    order = (0, 2, 1, 3)
    hidden = hid[...]
    up.need(0)
    down.start(0)
    og.start(0)

    def gates(b):
        a = nn(hidden, up.ref[:, b * block : (b + 1) * block])
        return a, nn(hidden, up.ref[:, ff + b * block : ff + (b + 1) * block])

    def finish(b, a, g, first):
        here = slice(b * block, (b + 1) * block)
        there = slice(ff + b * block, ff + (b + 1) * block)
        phi = 0.5 + 0.5 * lax.erf(g * (1.0 / math.sqrt(2.0)))
        gelu = g * phi
        active = (a * gelu).astype(BF)
        slope = a * (phi + g * (jnp.exp(-0.5 * g * g) * (1.0 / math.sqrt(2.0 * math.pi))))
        act[jnp.where(core == b // 2, 0, 1), :, (b % 2) * block : (b % 2 + 1) * block] = active
        act_grad = nt(cot, down.ref[here])
        a_grad = (act_grad * gelu).astype(BF)
        g_grad = (act_grad * slope).astype(BF)
        for c in range(block // unit_cols):
            cell = b * (block // unit_cols) + c
            cols = slice(c * unit_cols, (c + 1) * unit_cols)
            z, y, x = cell // 4, cell // 2 % 2, cell % 2
            at = (2 * z + y) * unit_cols
            gu_a[jnp.where(one == x, 0, 1), :, at : at + unit_cols] = a_grad[:, cols]
            at = (2 * z + x) * unit_cols
            gu_g[jnp.where(two == y, 0, 1), :, at : at + unit_cols] = g_grad[:, cols]
        mixed = nn(active, down.ref[here])
        grad = nt(a_grad, up.ref[:, here]) + nt(g_grad, up.ref[:, there])
        mix_ref[...] = mixed if first else mix_ref[...] + mixed
        grad_ref[...] = grad if first else grad_ref[...] + grad

    gate = gates(order[0])
    cot = (og[...].astype(F32) * scale).astype(BF)
    cots[0] = cot
    down.need(0)
    up.start(1)
    finish(order[0], *gate, True)
    up.need(1)
    for i in (up, down, ogs, res, mod):
        i.start_all()
    finish(order[1], *gates(order[1]), False)
    for i in (up, down, ogs, res, mod):
        i[...]
    if high == 4:
        gu_a.send(0)
        gu_a.send(2)
        act.send(0)
    cots[1] = (ogs[...].astype(F32) * losses[codes[1 - core]]).astype(BF)
    cots.send()
    later = gates(order[2])
    finish(order[2], *later, False)
    finish(order[3], *gates(order[3]), False)
    for i in range(4):
        gu_a.send(i)
    gu_g.send(0)
    act.send()
    residual = res[...]
    unit, size = normed(residual)
    into, mgrad = norm_back(unit, size, mod[...], grad_ref[...])
    mgrad_out[...] = mgrad
    total = og[...].astype(F32) * scale + into
    low = total.astype(BF)
    rlow_out[...] = low
    middle, end = low.shape[1] // 2, ff // 2
    for out, values, bit, axis in ((gu_a, low[:, :middle], one, 1), (gu_g, low[:, middle:], two, 2)):
        kept, sent = dealt(values, high, bit, axis)
        out[0, :, end:] = kept
        out[1, :, end:] = sent
        out.send()
    rlow_out.send()
    mixed_out[...] = (residual + mix_ref[...]).astype(BF)


def backward_kernel(
    high, place, scales, rlow, weight, q_in, k_in, v_in, pos, posg, tab, qkv, x, mod, row_two, cond,
    cells_a, cells_g, rows_out, cond_out, scale_out, tgrad_out, qkv_out,
):
    core, one, two = place[0], place[1], place[2]
    width = x.shape[1]
    onehot = onehot_of(jnp.concatenate([pos[core], posg[core]], axis=1))
    ones = segment_matrix()
    masks = head_masks()
    heads = len(masks)
    low = rlow[...]
    for j in range(width // LANES):
        here = slice(j * LANES, (j + 1) * LANES)
        if j == 0:
            for i in (weight, q_in, k_in, v_in, tab):
                i.need(0)
                i.start_all()
        if j == 1:
            for i in (qkv, x, mod, row_two, cond):
                i.start_all()
            for i in (weight, q_in, k_in, v_in, tab):
                i[...]
        grad = nt(low, weight.ref[here]).astype(BF)
        tabs = tables_of(onehot, tab.ref, j * LANES)
        root = root_of(scales, j)
        q, k, v = q_in.ref[:, here], k_in.ref[:, here], v_in.ref[:, here]
        q_inv = lax.rsqrt(segment_sum(q * q, ones) + EPS)
        k_inv = lax.rsqrt(segment_sum(k * k, ones) + EPS)
        q_scale, k_scale = q_inv * root, k_inv * root
        qr = spin(q * q_scale, tabs, 1.0).astype(BF)
        kr = spin(k * k_scale, tabs, 1.0).astype(BF)
        q_heads, g_heads = stacked(masks, qr), stacked(masks, grad)
        expo = jnp.exp(nt(kr, q_heads))
        prob = expo * (1.0 / jnp.sum(expo, axis=0, keepdims=True))
        weighted = prob * nt(v, g_heads)
        sgrad = (weighted - prob * jnp.sum(weighted, axis=0, keepdims=True)).astype(BF)
        dv = nn(prob.astype(BF), g_heads).astype(BF)
        dk = spin(nn(sgrad, q_heads), tabs, -1.0)
        size = qr.shape[0]
        turned = jnp.concatenate(
            [sgrad[:, i * size : (i + 1) * size] for i in range(heads)], axis=0
        )
        dq = spin(tn(turned, stacked(masks, kr)), tabs, -1.0)
        q_dot, k_dot = dq * q, dk * k
        scale_out[:, here] = jnp.sum(q_dot * q_scale + k_dot * k_scale, axis=0, keepdims=True)
        gq = (q_scale * (dq - q * (segment_sum(q_dot, ones) * (q_inv * q_inv)))).astype(BF)
        gk = (k_scale * (dk - k * (segment_sum(k_dot, ones) * (k_inv * k_inv)))).astype(BF)
        for i, part in enumerate((gq, gk, dv)):
            qkv_out[:, i * width + j * LANES : i * width + (j + 1) * LANES] = part
    every = cond[...].astype(F32)
    cond_out[...] = jnp.where(core == 0, every[0:1], every[1:2])
    middle = qkv_out.shape[1] // 2
    for out, at, bit, axis in ((cells_a, 0, one, 1), (cells_g, middle, two, 2)):
        kept, sent = dealt(qkv_out[:, at : at + middle], high, bit, axis)
        out[0] = kept
        out[1] = sent
        out.send()
    unit, size = normed(x[...].astype(F32))
    into, mgrad = norm_back(unit, size, mod[...], nt(qkv_out[...], qkv[...]))
    tgrad_out[...] = low.astype(F32) + into
    for i, row in enumerate((mgrad, row_two[...])):
        kept, sent = dealt(row, high // 2, place[3], 1)
        rows_out[0, :, i * kept.shape[1] : (i + 1) * kept.shape[1]] = kept
        rows_out[1, :, i * kept.shape[1] : (i + 1) * kept.shape[1]] = sent


def down_weight_kernel(place, cols_in, rows_in, out_a, out_b):
    parts, size, half = out_a.ref.shape[1:]
    for j in range(2 * parts):
        total = tn(cols_in[:, j * size : (j + 1) * size], rows_in[...]).astype(BF)
        slot = jnp.where(place[3] == j % 2, 0, 1)
        out_a[slot, j // 2] = total[:, :half]
        out_b[slot, j // 2] = total[:, half:]
        if j % 2:
            out_a.send(j // 2)
            out_b.send(j // 2)


def gate_weight_kernel(cuts, place, *refs):
    one, two = place[1], place[2]
    out_a, out_g = refs[4 * len(cuts) :]
    ins_a, ins_g = refs[: 2 * len(cuts)], refs[2 * len(cuts) : 4 * len(cuts)]
    for ins, out, mine in ((ins_a, out_a, two), (ins_g, out_g, one)):
        if out is out_a:
            for i in ins_a:
                i[...]
            for i in ins_g:
                i.start_all()
        for z in range(out_a.ref.shape[1]):
            start = 0
            for p, size in enumerate(cuts):
                cols_in, rows_in = ins[2 * p : 2 * p + 2]
                total = tn(cols_in[:, 2 * z * size : 2 * (z + 1) * size], rows_in[...]).astype(BF)
                for i in range(2):
                    out[jnp.where(mine == i, 0, 1), z, start : start + size] = total[
                        i * size : (i + 1) * size
                    ]
                start += size
            out.send(z)


def combine_kernel(counts, place, *refs):
    sent_out, kept_out = refs[sum(counts) :]
    first = at = 0
    for count in counts:
        terms = refs[at : at + count]
        at += count
        total = sum(t[...].astype(F32) for t in terms).astype(BF)
        size = total.shape[1]
        sent_out[first : first + size] = total[0]
        kept_out[first : first + size] = total[1]
        first += size


def combine(place, which, groups):
    def term(array):
        outer, _, rows, lanes = array.shape

        def plan(bit):
            return [[(0, (slice(None), 1 - bit), (0,)), (0, (slice(None), bit), (1,))]]

        return In(array, shape=(2, outer, rows, lanes), plan=plan, which=which)

    ins = [term(a) for group in groups for a in group]
    outer = sum(group[0].shape[0] for group in groups)
    rows, lanes = groups[0][0].shape[2:]
    return call(
        functools.partial(combine_kernel, [len(group) for group in groups]),
        [place],
        ins,
        [Out((outer, rows, lanes), BF)] * 2,
    )


def shards(n, tokens, condition, positions, weight_codes, loss_table, out_grad, mod_attn,
           qkv_weight, attn_scale, out_weight, mod_ff, up_weight, down_weight):
    images, part, width = tokens.shape
    rows = images * part
    half = width // 2
    heads = attn_scale.shape[0]
    ff = 2 * down_weight.shape[0]
    low = 1 if n <= 16 else n // 8
    high = n // (4 * low)
    me = lax.axis_index("dp")
    core = lax.axis_index("seq")
    one = (me // low) % 2
    two = (me // (2 * low)) % 2
    three = (me // (4 * low)) % 2
    bit_strides = [low, 2 * low, 4 * low]
    bit_strides += [1 << i for i in range(n.bit_length() - 1) if 1 << i not in bit_strides]
    place = jnp.stack([core] + [(me // b) % 2 for b in bit_strides]).astype(jnp.int32)

    def swap(values):
        return lax.ppermute(values, "seq", [(0, 1), (1, 0)])

    def cross(values, stride):
        return lax.ppermute(
            values, "dp", [(i, i + stride - 2 * stride * ((i // stride) % 2)) for i in range(n)]
        )

    def pick(values, index, axis=0):
        return lax.dynamic_index_in_dim(values, index, axis, keepdims=False)

    def tie(*values):
        return lax.optimization_barrier(values)

    first = swap(tokens), swap(mod_attn), swap(mod_ff), swap(positions)
    tokens_got, mod_attn_got, mod_ff_got, pos_got, qkv_w, out_w = tie(
        *first, qkv_weight, out_weight
    )
    qkv_got, out_got = swap(qkv_w), swap(out_w)
    hidden_one, h1, mod_one, mod_two = call(
        norm_kernel,
        [place],
        [image(tokens, tokens_got), In(condition), by_rows(mod_attn, mod_attn_got)]
        + [image(tokens, tokens_got, False), by_rows(mod_ff, mod_ff_got)],
        [Out((rows, width), BF), Out((rows, width), BF), Out((1, width), F32)]
        + [Out((1, width), F32)],
    )
    qkv_got, out_got, hidden_one, og_w, up_w, down_w = tie(
        qkv_got, out_got, hidden_one, out_grad, up_weight, down_weight
    )
    og_got, up_got, down_got = swap(og_w), swap(up_w), swap(down_w)
    h1_one, h1_two = cross(h1, low), cross(h1, 2 * low)

    table = In(jnp.asarray(angle_constants(heads)))
    pos_in = [In(positions), In(pos_got)]
    q_raw, k_raw, value, both, res = call(
        forward_kernel,
        [place, attn_scale],
        [In(hidden_one), by_rows(qkv_weight, qkv_got, 3, LANES)]
        + pos_in
        + [table, image(tokens, tokens_got, late=True)]
        + [by_rows(out_weight, out_got, late=True), In(mod_two, late=True)],
        [Out((rows, width), dtype, 1, width // LANES) for dtype in (F32, F32, BF)]
        + [Out((rows, width), BF, into={0: ("both", width)})]
        + [Out((rows, width), BF, into={0: ("both", 0)}), Out((rows, width), F32)],
    )
    both, h1_one, h1_two = tie(both, h1_one, h1_two)
    both_one, both_two, both_sib = cross(both, low), cross(both, 2 * low), swap(both)

    block = ff // 4
    wide = ff // 2 + width // 4
    gate = call(
        functools.partial(feed_kernel, high),
        [place, weight_codes, loss_table],
        [pile((both, 0), width=width), by_rows_order(up_weight, up_got, 2, block, (0, 2, 1, 3))]
        + [image(out_grad, og_got, late=True), by_row_blocks(down_weight, down_got, block, True)]
        + [image(out_grad, og_got, False, True), In(res, late=True), In(mod_two, late=True)],
        [Out((rows, wide), BF, 2, into={0: ("pack", 0)}, cuts=[*range(0, ff // 2 + 1, ff // 8), wide])]
        + [Out((rows, wide), BF, 2, into={0: ("pack", wide)}, cuts=[0, ff // 2, wide])]
        + [Out((rows, ff // 2), BF, 2, 2, into={1: ("pack", 2 * wide)})]
        + [Out((rows, width), BF), Out((rows, width), BF, 2), Out((rows, width), BF)]
        + [Out((1, width), F32)],
        [pltpu.VMEM((rows, width), F32)] * 2,
    )
    pack, send_a, send_g, act_own, res_low, cot, cot_sib, *rest = gate
    mixed_mine, mod_two_grad = rest
    send_a, send_g, pack, res_low, both_one, both_two, both_sib = tie(
        send_a, send_g, pack, res_low, both_one, both_two, both_sib
    )
    pair_a, pair_g = cross(send_a, low), cross(send_g, 2 * low)
    pack_sib, both_one_sib, both_two_sib = swap(pack), swap(both_one), swap(both_two)

    third = 3 * width // 4
    cond_cols = condition.shape[1]
    keep_q, send_qa, send_qg, line_kept, line, tokens_mine = call(
        functools.partial(backward_kernel, high),
        [place, attn_scale],
        [In(res_low), by_row_blocks(out_weight, out_got, LANES)]
        + [by_pieces(a, width // LANES) for a in (q_raw, k_raw, value)]
        + pos_in
        + [table, by_rows(qkv_weight, qkv_got, late=True), image(tokens, tokens_got, True, True)]
        + [In(a, late=True) for a in (mod_one, mod_two_grad, condition)],
        [Out((rows, third), BF, 2, into={0: ("keep", 0)})]
        + [Out((rows, third), BF, 2, into={0: ("keep", third)})]
        + [Out((1, width), F32, 2, into={1: ("line", 0)})]
        + [Out((1, cond_cols), F32, into={0: ("line", width)})]
        + [Out((1, width), F32, into={0: ("line", width + cond_cols)})]
        + [Out((rows, width), F32)],
        [pltpu.VMEM((rows, 3 * width), BF)],
    )
    cot, keep_q, send_qa, send_qg, pack_sib, both_one_sib, both_two_sib = tie(
        cot, keep_q, send_qa, send_qg, pack_sib, both_one_sib, both_two_sib
    )

    def take(values, index, axis=0):
        return pick(values, index, axis).astype(F32)

    high_bits, low_bits = high.bit_length() - 1, low.bit_length() - 1
    high_strides = [4 * low << (high_bits - 1 - i) for i in range(high_bits)]
    low_strides = [1 << (low_bits - 1 - i) for i in range(low_bits)]
    line_strides, line_order = high_strides + low_strides, high_strides[::-1] + low_strides

    def hand_on(grads, rest, stride):
        bit = (me // stride) % 2
        split = grads.reshape(grads.shape[0], 2, 2, -1)
        sent = pick(split, 1 - bit, 2).reshape(grads.shape[0], -1)
        got = cross(jnp.concatenate([sent, rest], axis=1), stride)
        return pick(split, bit, 2).reshape(grads.shape[0], -1), rest, got, bit

    def taken(mine, rest, got, bit):
        mine = jnp.concatenate([mine, rest], axis=1)
        every = jnp.where(
            bit == 0,
            jnp.concatenate([mine, got], axis=0),
            jnp.concatenate([got, mine], axis=0),
        )
        wide = mine.shape[1] - rest.shape[1]
        return every[:, :wide].reshape(every.shape[0], 2, -1), every[:, wide:]

    line_steps = [s for s in (n >> (i + 1) for i in range(n.bit_length() - 1)) if s != 4 * low]
    keep_q_sib = swap(keep_q)
    pair_qa, pair_qg = cross(send_qa, low), cross(send_qg, 2 * low)

    down = call(
        down_weight_kernel,
        [place],
        [pile(cot, cot_sib), pile(act_own, (pack_sib, 2 * wide), width=ff // 2)],
        [Out((high // 2, width // high, ff // 4), BF, 2, high // 2, 0)] * 2,
    )
    line_got = cross(line, 4 * low)
    pair_a, pair_g, line_got, down[0] = tie(pair_a, pair_g, line_got, down[0])
    small = [line_kept, line[:, width:], line_got, three]
    down_got_a = cross(down[1], 4 * low)
    def rows_of(first, far, far_sib):
        return pile(
            (both, first), (both_sib, first), (far, first), (far_sib, first), width=width, halved=True
        )

    def late(value):
        value.late = True
        return value

    def gate_weight(cuts, ins_a, ins_g):
        return call(
            functools.partial(gate_weight_kernel, cuts),
            [place],
            ins_a + [late(i) for i in ins_g],
            [Out((high // 2, sum(cuts), half), BF, 2, high // 2, 0)] * 2,
        )

    pair_a_sib, pair_g_sib = swap(pair_a), swap(pair_g)
    up_parts = gate_weight(
        [ff // (2 * high)],
        [
            pile(pack, pack_sib, pair_a, pair_a_sib, width=ff // 2),
            rows_of(0, both_one, both_one_sib),
        ],
        [
            pile((pack, wide), (pack_sib, wide), pair_g, pair_g_sib, width=ff // 2),
            rows_of(0, both_two, both_two_sib),
        ],
    )
    up_parts[0], down_got_a, pair_qa, pair_qg, keep_q_sib = tie(
        up_parts[0], down_got_a, pair_qa, pair_qg, keep_q_sib
    )
    up_last = cross(up_parts[1], 2 * low), cross(up_parts[3], low)
    down_got_b = cross(down[3], 4 * low)
    def step(groups, axes, stride, lead=1):
        outer = lead << axes.index(stride)
        groups = [[v.reshape(outer, 2, -1, v.shape[-1]) for v in group] for group in groups]
        sent, kept = combine(place, 1 + bit_strides.index(stride), groups)
        return [kept, cross(sent, stride)]

    def without(axes, *strides):
        return [a for a in axes if a not in strides]

    down_axes = high_strides[:-1] + [2 * low, low] + low_strides
    down_order = [low, 2 * low] + high_strides[:-1][::-1] + low_strides
    pair_qa_sib, pair_qg_sib = swap(pair_qa), swap(pair_qg)
    at = ff // 2
    last_parts = gate_weight(
        [width // (4 * high), 3 * width // (4 * high)],
        [
            pile((pack, at), (pack_sib, at), (pair_a, at), (pair_a_sib, at), width=width // 4),
            rows_of(width, both_one, both_one_sib),
            pile(keep_q, keep_q_sib, pair_qa, pair_qa_sib, width=third),
            pile((h1, 0), (h1, half), (h1_one, 0), (h1_one, half), width=half),
        ],
        [
            pile(
                *((pack, wide + at), (pack_sib, wide + at), (pair_g, at), (pair_g_sib, at)),
                width=width // 4,
            ),
            rows_of(width, both_two, both_two_sib),
            pile((keep_q, third), (keep_q_sib, third), pair_qg, pair_qg_sib, width=third),
            pile((h1, 0), (h1, half), (h1_two, 0), (h1_two, half), width=half),
        ],
    )
    last_last = cross(last_parts[1], 2 * low), cross(last_parts[3], low)
    last_parts[0], down_got_b, small[2], *up_last = tie(
        last_parts[0], down_got_b, small[2], *up_last
    )

    def first_line(parts, got):
        if high > 2:
            groups = [[parts[2 * i], got[i]] for i in range(2)]
            return step(groups, high_strides[1:] + low_strides, line_order[0])
        groups = [[jnp.concatenate(v, axis=0) for v in ((parts[0], parts[2]), got)]]
        return step(groups, high_strides + low_strides, line_order[0])

    def rest_of(kept, got, axes, order, lead=1):
        for stride in order:
            kept, got = step([[kept, got]], axes, stride, lead)
            axes = without(axes, stride)
        return [kept, got]

    line_axes = without(high_strides + low_strides, line_order[0])

    up_line = first_line(up_parts, up_last)
    up_line[0], small[2] = tie(up_line[0], small[2])
    small = list(hand_on(*taken(*small), line_steps[0]))
    *last_last, up_line[0] = tie(*last_last, up_line[0])
    last_line = first_line(last_parts, last_last)
    down[0], last_line[0] = tie(down[0], last_line[0])
    down_line = step([[down[0], down_got_a], [down[2], down_got_b]], down_axes, down_order[0])
    up_line[1], last_line[0], small[2] = tie(up_line[1], last_line[0], small[2])
    up_line = rest_of(*up_line, line_axes, line_order[1:2])
    small = list(hand_on(*taken(*small), line_steps[1]))
    down_axes = without(down_axes, down_order[0])
    down_line[1], up_line[0] = tie(down_line[1], up_line[0])
    down_line = rest_of(*down_line, down_axes, down_order[1:2], 2)
    last_line[1], down_line[0], small[2] = tie(last_line[1], down_line[0], small[2])
    last_line = rest_of(*last_line, line_axes, line_order[1:2])
    values = tie(down_line[0], mixed_mine, tokens_mine, line_kept, line, *small[:3])
    down_line[0], mixed_mine, tokens_mine, line_kept, line = values[:5]
    small[:3] = values[5:]
    for stride in line_steps[2:]:
        small = hand_on(*taken(*small), stride)
    grads, rest = taken(*small)
    down_line = rest_of(*down_line, without(down_axes, down_order[1]), down_order[2:], 2)

    total = lambda kept, got: kept.astype(F32) + got.astype(F32)
    line_axes = without(line_axes, line_order[1])
    down_sum = total(*down_line)
    down_sum = jnp.concatenate([v.reshape(-1, ff // 4) for v in jnp.split(down_sum, 2)], axis=1)
    up_sum = total(*rest_of(*up_line, line_axes, line_order[2:])).reshape(-1, half)
    last_sum = total(*rest_of(*last_line, line_axes, line_order[2:])).reshape(-1, half)

    cond_rows = mod_attn.shape[0]
    grads = grads.reshape(grads.shape[0], -1)
    wide = grads.shape[1]
    every = jnp.concatenate([grads, rest], axis=1)
    every = jnp.concatenate([every, swap(every)], axis=0)
    cond_all = lax.dynamic_slice_in_dim(every, wide + core * cond_rows, cond_rows, 1)
    mod_attn_grad = jnp.dot(cond_all.T, every[:, : wide // 2], precision=FINEST)
    mod_ff_grad = jnp.dot(cond_all.T, every[:, wide // 2 : wide], precision=FINEST)
    lanes = jnp.sum(every[:, wide + cond_cols :].reshape(2, -1, width), axis=1)
    lanes = jnp.sum((lanes[0] + lanes[1]).reshape(heads, HEAD_DIM), axis=1)
    scale_grad = lanes / (2.0 * attn_scale)

    def row_of(parts):
        cells = parts.reshape(2, high // 2, -1)
        cells = jnp.where(three == 0, cells, cells[::-1])
        return jnp.swapaxes(cells, 0, 1).reshape(1, width)

    mods = jnp.concatenate([mod_attn, mod_ff], axis=1)
    mine = [jnp.concatenate([a, b], axis=0) for a, b in zip(*[jnp.split(v[:, :width], 2, axis=1) for v in (line_kept, line)])]
    mine = jnp.concatenate([row_of(v) for v in mine], axis=1)
    got = swap(mine)
    pair = jnp.where(
        core == 0, jnp.concatenate([mine, got], axis=0), jnp.concatenate([got, mine], axis=0)
    )
    cond_part = jnp.dot(pair, mods.astype(F32).T, precision=FINEST)
    cond_got = swap(cond_part)
    condition_grad = jnp.where(
        core == 0,
        jnp.concatenate([cond_part, cond_got], axis=1),
        jnp.concatenate([cond_got, cond_part], axis=1),
    )

    out_cols = last_sum.shape[0] // 4

    def home(values):
        got = swap(values[part:])
        own = values[:part]
        return jnp.where(core == 0, jnp.stack([own, got]), jnp.stack([got, own]))

    def turned(values):
        return values.astype(F32).T

    return (
        home(mixed_mine),
        home(tokens_mine),
        condition_grad,
        mod_attn_grad,
        turned(last_sum[out_cols:]),
        scale_grad,
        turned(last_sum[:out_cols]),
        mod_ff_grad,
        turned(up_sum),
        turned(down_sum),
    )


def solution(mesh):
    n = mesh.shape["dp"]

    def body(*args):
        return shards(n, *args)

    return jax.shard_map(
        body,
        mesh=mesh,
        in_specs=(
            P("dp", "seq", None),
            P("dp", None),
            P("dp", None, "seq"),
            P("dp"),
            P(),
            P("dp", "seq", None),
            P("seq", None),
            P("seq", None),
            P(),
            P("seq", None),
            P("seq", None),
            P("seq", None),
            P("seq", None),
        ),
        out_specs=(
            P("dp", "seq", None),
            P("dp", "seq", None),
            P("dp", None),
            P("seq", "dp"),
            P("seq", "dp"),
            P(),
            P("seq", "dp"),
            P("seq", "dp"),
            P("seq", "dp"),
            P("seq", "dp"),
        ),
        check_vma=False,
    )
```

```python
import functools
import math

import jax
import jax.numpy as jnp
import ml_dtypes
import numpy as np
from jax import lax
from jax.experimental import pallas as pl
from jax.experimental.pallas import tpu as pltpu
from jax.sharding import PartitionSpec as P

HEAD_DIM = 64
GRID = 16
EPS = 1e-06
BF = jnp.bfloat16
F32 = jnp.float32
FINEST = lax.Precision.HIGHEST
LANES = 256
VMEM = 63 * 1024 * 1024


def nn(a, b):
    return lax.dot_general(a, b, (((1,), (0,)), ((), ())), preferred_element_type=F32)


def nt(a, b):
    return lax.dot_general(a, b, (((1,), (1,)), ((), ())), preferred_element_type=F32)


def tn(a, b):
    return lax.dot_general(a, b, (((0,), (0,)), ((), ())), preferred_element_type=F32)


def angle_constants(heads):
    quarter = HEAD_DIM // 8
    counter = np.arange(quarter)[None, :] * heads + np.arange(heads)[:, None]
    freq = (math.pi * np.power(10.0, counter / (heads * quarter))).astype(np.float32)
    coords = ((2.0 * np.arange(GRID) + 1.0) / GRID - 1.0).astype(np.float32)
    angles = (coords[:, None, None] * freq[None]).astype(np.float32).astype(np.float64)
    cos, sin = np.cos(angles), np.sin(angles)
    table = np.zeros((3, 2, GRID, heads, HEAD_DIM))
    q = quarter
    for part in range(2):
        lo = part * q
        table[0, part, :, :, lo : lo + q] = cos
        table[0, part, :, :, 2 * q + lo : 3 * q + lo] = cos
        table[1, part, :, :, lo : lo + q] = -sin
        table[2, part, :, :, 2 * q + lo : 3 * q + lo] = sin
    table[0, 0, :, :, 4 * q :] = 1.0
    rest = table.reshape(3, 2 * GRID, heads * HEAD_DIM).astype(np.float32)
    terms = []
    for _ in range(3):
        terms.append(rest.astype(ml_dtypes.bfloat16))
        rest = rest - terms[-1].astype(np.float32)
    return np.concatenate(terms, axis=1)


def segment_matrix():
    rows = lax.broadcasted_iota(jnp.int32, (LANES, LANES), 0) // HEAD_DIM
    cols = lax.broadcasted_iota(jnp.int32, (LANES, LANES), 1) // HEAD_DIM
    return (rows == cols).astype(F32).astype(BF)


def segment_sum(values, ones):
    high = values.astype(BF)
    low = (values - high.astype(F32)).astype(BF)
    return nn(high, ones) + nn(low, ones)


def onehot_of(places):
    cells = lax.broadcasted_iota(jnp.int32, (GRID, places.shape[1]), 0)
    hot = [(places[i : i + 1] == cells).astype(F32) for i in range(2)]
    return jnp.concatenate(hot * 3, axis=0).astype(BF)


def tables_of(onehot, tab_ref, at):
    return [tn(onehot, tab_ref[i, :, at : at + LANES]) for i in range(3)]


def spin(values, tabs, sign):
    cos, first, second = tabs
    q = HEAD_DIM // 4
    turned = pltpu.roll(values, LANES - q, 1) * first + pltpu.roll(values, q, 1) * second
    return values * cos + sign * turned


def head_masks():
    lane = lax.broadcasted_iota(jnp.int32, (1, LANES), 1) // HEAD_DIM
    return [lane == h for h in range(LANES // HEAD_DIM)]


def root_of(scale_ref, group):
    masks = head_masks()
    value = jnp.zeros((1, LANES), F32)
    for h, mask in enumerate(masks):
        value = jnp.where(mask, scale_ref[group * len(masks) + h], value)
    return jnp.sqrt(value)


def normed(values):
    scale = lax.rsqrt(jnp.mean(values * values, axis=-1, keepdims=True) + EPS)
    return values * scale, scale


def norm_back(unit, scale, mod, grad):
    inner = grad * (1.0 + mod)
    into = scale * (inner - unit * jnp.mean(inner * unit, axis=-1, keepdims=True))
    return into, jnp.sum(grad * unit, axis=0, keepdims=True)


def half_of(core, values):
    half = values.shape[1] // 2
    return jnp.where(core == 0, values[:, :half], values[:, half:])


def stacked(masks, values):
    zero = jnp.zeros_like(values)
    return jnp.concatenate([jnp.where(mask, values, zero) for mask in masks], axis=0)


def abreast(values, count):
    size = values.shape[0] // count
    return jnp.concatenate([values[i * size : (i + 1) * size] for i in range(count)], axis=1)


def struct(shape, dtype):
    return jax.ShapeDtypeStruct(shape, dtype)


class In:
    def __init__(self, *arrays, shape=None, plan=None, late=False, which=0):
        self.which = which
        self.arrays, self.shape, self.late = arrays, shape or arrays[0].shape, late
        whole = tuple(slice(None) for _ in self.shape)
        self.plan = plan or (lambda core: [[(0, whole, whole)]])


class Out:
    def __init__(self, shape, dtype, count=1, pieces=1, axis=1, into=(), cuts=None):
        self.struct, self.count, self.axis = struct(shape, dtype), count, axis
        self.cuts = cuts or [shape[axis] * i // pieces for i in range(pieces + 1)]
        self.pieces = len(self.cuts) - 1
        self.into = dict(into)

    def where(self, piece):
        if self.pieces == 1:
            return ...
        return (slice(None),) * self.axis + (slice(self.cuts[piece], self.cuts[piece + 1]),)


class Held:
    def __init__(self, ref, pieces):
        self.ref, self.shape, self.pieces = ref, ref.shape, pieces
        self.started, self.waited = set(), set()

    def start(self, piece):
        if piece < len(self.pieces) and piece not in self.started:
            self.started.add(piece)
            for copy in self.pieces[piece]:
                copy.start()

    def need(self, piece):
        self.start(piece)
        if piece not in self.waited:
            self.waited.add(piece)
            for copy in self.pieces[piece]:
                copy.wait()

    def start_all(self):
        for piece in range(len(self.pieces)):
            self.start(piece)

    def __getitem__(self, where):
        for piece in range(len(self.pieces)):
            self.need(piece)
        return self.ref[where]


class Made:
    def __init__(self, ref, copies):
        self.ref, self.copies, self.sent = ref, copies, set()

    def __setitem__(self, where, values):
        self.ref[where] = values

    def __getitem__(self, where):
        return self.ref[where]

    def send(self, piece=None):
        for i in range(len(self.copies)) if piece is None else (piece,):
            if i not in self.sent:
                self.sent.add(i)
                for copy in self.copies[i]:
                    copy.start()


def call(kernel, tables, inputs, outputs, scratch=()):
    arrays = [a for i in inputs for a in i.arrays]
    names, structs = [], []
    for i, o in enumerate(outputs):
        for k in range(o.count):
            name, column = o.into.get(k, ((i, k), 0))
            if name not in names:
                names.append(name)
                structs.append(o.struct)
            at = names.index(name)
            wide = max(structs[at].shape[-1], column + o.struct.shape[-1])
            structs[at] = struct((*o.struct.shape[:-1], wide), o.struct.dtype)

    def body(*refs):
        refs = list(refs)

        def some(count):
            taken = refs[:count]
            del refs[:count]
            return taken

        scalars, sources, targets = some(len(tables)), some(len(arrays)), some(len(structs))
        held, made = some(len(inputs)), some(len(outputs))
        in_sems, out_sems = some(len(inputs)), some(1)[0]
        extra = refs
        ins, outs = [], []
        for i, ref, sems in zip(inputs, held, in_sems):
            from_refs = [sources.pop(0) for _ in i.arrays]
            pieces, count = [], 0
            for piece in i.plan(scalars[0][i.which]):
                copies = []
                for which, a, b in piece:
                    copies.append(
                        pltpu.make_async_copy(from_refs[which].at[a], ref.at[b], sems.at[count])
                    )
                    count += 1
                pieces.append(copies)
            ins.append(Held(ref, pieces))
        for i, given in zip(ins, inputs):
            if not given.late:
                i.start(0)
        count = 0
        for o, ref in zip(outputs, made):
            copies = [[] for _ in range(o.pieces)]
            for k in range(o.count):
                name, column = o.into.get(k, ((len(outs), k), 0))
                target, source = targets[names.index(name)], ref if o.count == 1 else ref.at[k]
                if k in o.into:
                    target = target.at[:, column : column + o.struct.shape[-1]]
                for p in range(o.pieces):
                    where = o.where(p)
                    copies[p].append(
                        pltpu.make_async_copy(source.at[where], target.at[where], out_sems.at[count])
                    )
                    count += 1
            outs.append(Made(ref, copies))
        kernel(*scalars, *ins, *outs, *extra)
        for o in outs:
            o.send()
        for i in ins:
            for piece in range(len(i.pieces)):
                i.need(piece)
        for o in outs:
            for piece in o.copies:
                for copy in piece:
                    copy.wait()

    results = pl.pallas_call(
        body,
        out_shape=structs,
        in_specs=[pl.BlockSpec(memory_space=pltpu.SMEM)] * len(tables)
        + [pl.BlockSpec(memory_space=pltpu.HBM)] * len(arrays),
        out_specs=[pl.BlockSpec(memory_space=pltpu.HBM)] * len(structs),
        scratch_shapes=[pltpu.VMEM(i.shape, i.arrays[0].dtype) for i in inputs]
        + [
            pltpu.VMEM(o.struct.shape if o.count == 1 else (o.count, *o.struct.shape), o.struct.dtype)
            for o in outputs
        ]
        + [pltpu.SemaphoreType.DMA((sum(len(p) for p in i.plan(0)),)) for i in inputs]
        + [pltpu.SemaphoreType.DMA((sum(o.count * o.pieces for o in outputs),))]
        + list(scratch),
        compiler_params=pltpu.CompilerParams(vmem_limit_bytes=VMEM),
    )(*tables, *arrays)
    return list(results)


def at_half(core, which, size):
    part = core if which == 0 else 1 - core
    return pl.ds(pl.multiple_of(part * size, size), size)


def by_rows(own, got, parts=1, block=None, late=False):
    rows, cols = own.shape
    block = block or cols // parts

    def plan(core):
        for j in range(cols // parts // block):
            piece = []
            for p in range(parts):
                where = slice(p * (cols // parts) + j * block, p * (cols // parts) + (j + 1) * block)
                for k in range(2):
                    piece.append((k, (slice(None), where), (at_half(core, k, rows), where)))
            yield piece

    return In(own, got, shape=(2 * rows, cols), plan=plan, late=late)


def by_pieces(array, pieces, late=False):
    size = array.shape[-1] // pieces
    wheres = [
        (slice(None),) * (len(array.shape) - 1) + (slice(p * size, (p + 1) * size),)
        for p in range(pieces)
    ]
    return In(array, plan=lambda core: [[(0, where, where)] for where in wheres], late=late)


def by_rows_order(own, got, parts, block, order):
    made = by_rows(own, got, parts, block)
    pieces = made.plan

    def plan(core):
        every = list(pieces(core))
        return [every[i] for i in order]

    made.plan = plan
    return made


def by_row_blocks(own, got, block, late=False):
    rows, cols = own.shape

    def plan(core):
        for j in range(rows // block):
            piece = []
            for k in range(2):
                part = core if k == 0 else 1 - core
                there = pl.ds(pl.multiple_of(part * rows + j * block, block), block)
                piece.append((k, (slice(j * block, (j + 1) * block),), (there,)))
            yield piece

    return In(own, got, shape=(2 * rows, cols), plan=plan, late=late)


def image(own, got, mine=True, late=False):
    part, width = own.shape[1:]

    def plan(core):
        which = core if mine else 1 - core
        first, second = (0, 1) if mine else (1, 0)
        return [
            [
                (first, (which,), (slice(0, part),)),
                (second, (which,), (slice(part, 2 * part),)),
            ]
        ]

    return In(own, got, shape=(2 * part, width), plan=plan, late=late)


def pile(*arrays, width=None, pieces=1, halved=False, late=False):
    arrays = [a if isinstance(a, tuple) else (a, 0) for a in arrays]
    rows, cols = arrays[0][0].shape
    cols = (width or cols) // (2 if halved else 1)
    size = cols // pieces

    def plan(core):
        for p in range(pieces):
            there = slice(p * size, (p + 1) * size)
            piece = []
            for i, (_, first) in enumerate(arrays):
                at = first + p * size
                here = slice(at, at + size)
                if halved:
                    here = pl.ds(pl.multiple_of(core * cols + at, 128), size)
                piece.append((i, (slice(None), here), (slice(i * rows, (i + 1) * rows), there)))
            yield piece

    return In(*[a for a, _ in arrays], shape=(len(arrays) * rows, cols), plan=plan, late=late)


def norm_kernel(place, x, cond, mod, xs, mod_ff, hid_out, h1, row_one, row_two):
    core = place[0]
    rows = nn(cond[...], mod[...])
    first, second = rows[0:1], rows[1:2]
    row, row_sib = jnp.where(core == 0, first, second), jnp.where(core == 0, second, first)
    row_one[...] = row
    unit, _ = normed(x[...].astype(F32))
    hidden = (unit * (1.0 + row)).astype(BF)
    hid_out[...] = hidden
    hid_out.send()
    half = hidden.shape[1] // 2
    h1[:, :half] = half_of(core, hidden)
    unit, _ = normed(xs[...].astype(F32))
    h1[:, half:] = half_of(core, (unit * (1.0 + row_sib)).astype(BF))
    h1.send()
    rows = nn(cond[...], mod_ff[...])
    row_two[...] = jnp.where(core == 0, rows[0:1], rows[1:2])


def forward_kernel(
    place, scales, hid, weight, pos, posg, tab, x, out_weight, mod,
    q_out, k_out, v_out, att, hid_out, res_out,
):
    core = place[0]
    width = x.shape[1]
    hidden = hid[...]
    onehot = onehot_of(jnp.concatenate([pos[core], posg[core]], axis=1))
    ones = segment_matrix()
    masks = head_masks()
    heads = len(masks)
    spread = stacked(masks, jnp.ones((LANES, LANES), BF))
    steps = width // LANES
    weight.need(0)
    for j in range(1, steps):
        weight.start(j)
    tab[...]
    for j in range(steps):
        here = slice(j * LANES, (j + 1) * LANES)
        if j == 1:
            for i in (out_weight, x, mod):
                i.start(0)
            weight[...]
            for out in (q_out, k_out, v_out):
                out.send(0)
        q, k, v = [
            nn(hidden, weight.ref[:, i * width + j * LANES : i * width + (j + 1) * LANES])
            for i in range(3)
        ]
        v = v.astype(BF)
        q_out[:, here] = q
        k_out[:, here] = k
        v_out[:, here] = v
        tabs = tables_of(onehot, tab.ref, j * LANES)
        root = root_of(scales, j)
        qr = spin(q * (lax.rsqrt(segment_sum(q * q, ones) + EPS) * root), tabs, 1.0).astype(BF)
        kr = spin(k * (lax.rsqrt(segment_sum(k * k, ones) + EPS) * root), tabs, 1.0).astype(BF)
        expo = abreast(jnp.exp(nt(stacked(masks, qr), kr)).astype(BF), heads)
        total = (nn(expo, stacked(masks, v)) / nn(expo, spread)).astype(BF)
        att[:, here] = total
    for out in (q_out, k_out, v_out, att):
        out.send()
    residual = x[...].astype(F32) + nn(att[...], out_weight[...])
    res_out[...] = residual
    unit, _ = normed(residual)
    hid_out[...] = (unit * (1.0 + mod[...])).astype(BF)


def dealt(values, high, bit, axis):
    size = values.shape[1] // (2 * high)
    kept, sent = [], []
    for cell in range(2 * high):
        if not cell & axis:
            zero = values[:, cell * size : (cell + 1) * size]
            unit = values[:, (cell + axis) * size : (cell + axis + 1) * size]
            kept.append(jnp.where(bit == 0, zero, unit))
            sent.append(jnp.where(bit == 0, unit, zero))
    return jnp.concatenate(kept, axis=1), jnp.concatenate(sent, axis=1)


def feed_kernel(
    high, place, codes, losses, hid, up, og, down, ogs, res, mod,
    gu_a, gu_g, act, rlow_out, cots, mixed_out, mgrad_out, grad_ref, mix_ref,
):
    core, one, two = place[0], place[1], place[2]
    ff = up.shape[1] // 2
    block = ff // 4
    unit_cols = ff // (2 * high)
    half = high // 2
    scale = losses[codes[core]]
    order = (0, 2, 1, 3)
    hidden = hid[...]
    up.need(0)
    down.start(0)
    og.start(0)

    def gates(b):
        a = nn(hidden, up.ref[:, b * block : (b + 1) * block])
        return a, nn(hidden, up.ref[:, ff + b * block : ff + (b + 1) * block])

    def finish(b, a, g, first):
        here = slice(b * block, (b + 1) * block)
        there = slice(ff + b * block, ff + (b + 1) * block)
        phi = 0.5 + 0.5 * lax.erf(g * (1.0 / math.sqrt(2.0)))
        gelu = g * phi
        active = (a * gelu).astype(BF)
        slope = a * (phi + g * (jnp.exp(-0.5 * g * g) * (1.0 / math.sqrt(2.0 * math.pi))))
        act[jnp.where(core == b // 2, 0, 1), :, (b % 2) * block : (b % 2 + 1) * block] = active
        act_grad = nt(cot, down.ref[here])
        a_grad = (act_grad * gelu).astype(BF)
        g_grad = (act_grad * slope).astype(BF)
        for c in range(block // unit_cols):
            cell = b * (block // unit_cols) + c
            cols = slice(c * unit_cols, (c + 1) * unit_cols)
            z, y, x = cell // 4, cell // 2 % 2, cell % 2
            at = (2 * z + y) * unit_cols
            gu_a[jnp.where(one == x, 0, 1), :, at : at + unit_cols] = a_grad[:, cols]
            at = (2 * z + x) * unit_cols
            gu_g[jnp.where(two == y, 0, 1), :, at : at + unit_cols] = g_grad[:, cols]
        mixed = nn(active, down.ref[here])
        grad = nt(a_grad, up.ref[:, here]) + nt(g_grad, up.ref[:, there])
        mix_ref[...] = mixed if first else mix_ref[...] + mixed
        grad_ref[...] = grad if first else grad_ref[...] + grad

    gate = gates(order[0])
    cot = (og[...].astype(F32) * scale).astype(BF)
    cots[0] = cot
    down.need(0)
    up.start(1)
    finish(order[0], *gate, True)
    up.need(1)
    for i in (up, down, ogs, res, mod):
        i.start_all()
    finish(order[1], *gates(order[1]), False)
    for i in (up, down, ogs, res, mod):
        i[...]
    if high == 4:
        gu_a.send(0)
        gu_a.send(2)
        act.send(0)
    cots[1] = (ogs[...].astype(F32) * losses[codes[1 - core]]).astype(BF)
    cots.send()
    later = gates(order[2])
    finish(order[2], *later, False)
    finish(order[3], *gates(order[3]), False)
    for i in range(4):
        gu_a.send(i)
    gu_g.send(0)
    act.send()
    residual = res[...]
    unit, size = normed(residual)
    into, mgrad = norm_back(unit, size, mod[...], grad_ref[...])
    mgrad_out[...] = mgrad
    total = og[...].astype(F32) * scale + into
    low = total.astype(BF)
    rlow_out[...] = low
    middle, end = low.shape[1] // 2, ff // 2
    for out, values, bit, axis in ((gu_a, low[:, :middle], one, 1), (gu_g, low[:, middle:], two, 2)):
        kept, sent = dealt(values, high, bit, axis)
        out[0, :, end:] = kept
        out[1, :, end:] = sent
        out.send()
    rlow_out.send()
    mixed_out[...] = (residual + mix_ref[...]).astype(BF)


def backward_kernel(
    high, place, scales, rlow, weight, q_in, k_in, v_in, pos, posg, tab, qkv, x, mod, row_two, cond,
    cells_a, cells_g, rows_out, cond_out, scale_out, tgrad_out, qkv_out,
):
    core, one, two = place[0], place[1], place[2]
    width = x.shape[1]
    onehot = onehot_of(jnp.concatenate([pos[core], posg[core]], axis=1))
    ones = segment_matrix()
    masks = head_masks()
    heads = len(masks)
    low = rlow[...]
    for j in range(width // LANES):
        here = slice(j * LANES, (j + 1) * LANES)
        if j == 0:
            for i in (weight, q_in, k_in, v_in, tab):
                i.start_all()
            for i in (weight, q_in, k_in, v_in, tab):
                i.need(0)
        if j == 1:
            for i in (qkv, x, mod, row_two, cond):
                i.start_all()
            for i in (weight, q_in, k_in, v_in, tab):
                i[...]
        grad = nt(low, weight.ref[here]).astype(BF)
        tabs = tables_of(onehot, tab.ref, j * LANES)
        root = root_of(scales, j)
        q, k, v = q_in.ref[:, here], k_in.ref[:, here], v_in.ref[:, here]
        q_inv = lax.rsqrt(segment_sum(q * q, ones) + EPS)
        k_inv = lax.rsqrt(segment_sum(k * k, ones) + EPS)
        q_scale, k_scale = q_inv * root, k_inv * root
        qr = spin(q * q_scale, tabs, 1.0).astype(BF)
        kr = spin(k * k_scale, tabs, 1.0).astype(BF)
        q_heads, g_heads = stacked(masks, qr), stacked(masks, grad)
        expo = jnp.exp(nt(kr, q_heads))
        prob = expo * (1.0 / jnp.sum(expo, axis=0, keepdims=True))
        weighted = prob * nt(v, g_heads)
        sgrad = (weighted - prob * jnp.sum(weighted, axis=0, keepdims=True)).astype(BF)
        dv = nn(prob.astype(BF), g_heads).astype(BF)
        dk = spin(nn(sgrad, q_heads), tabs, -1.0)
        size = qr.shape[0]
        turned = jnp.concatenate(
            [sgrad[:, i * size : (i + 1) * size] for i in range(heads)], axis=0
        )
        dq = spin(tn(turned, stacked(masks, kr)), tabs, -1.0)
        q_dot, k_dot = dq * q, dk * k
        scale_out[:, here] = jnp.sum(q_dot * q_scale + k_dot * k_scale, axis=0, keepdims=True)
        gq = (q_scale * (dq - q * (segment_sum(q_dot, ones) * (q_inv * q_inv)))).astype(BF)
        gk = (k_scale * (dk - k * (segment_sum(k_dot, ones) * (k_inv * k_inv)))).astype(BF)
        for i, part in enumerate((gq, gk, dv)):
            qkv_out[:, i * width + j * LANES : i * width + (j + 1) * LANES] = part
    every = cond[...].astype(F32)
    cond_out[...] = jnp.where(core == 0, every[0:1], every[1:2])
    middle = qkv_out.shape[1] // 2
    for out, at, bit, axis in ((cells_a, 0, one, 1), (cells_g, middle, two, 2)):
        kept, sent = dealt(qkv_out[:, at : at + middle], high, bit, axis)
        out[0] = kept
        out[1] = sent
        out.send()
    unit, size = normed(x[...].astype(F32))
    into, mgrad = norm_back(unit, size, mod[...], nt(qkv_out[...], qkv[...]))
    tgrad_out[...] = low.astype(F32) + into
    for i, row in enumerate((mgrad, row_two[...])):
        kept, sent = dealt(row, high // 2, place[3], 1)
        rows_out[0, :, i * kept.shape[1] : (i + 1) * kept.shape[1]] = kept
        rows_out[1, :, i * kept.shape[1] : (i + 1) * kept.shape[1]] = sent


def down_weight_kernel(place, cols_in, rows_in, out_a, out_b):
    parts, size, half = out_a.ref.shape[1:]
    for j in range(2 * parts):
        total = tn(cols_in[:, j * size : (j + 1) * size], rows_in[...]).astype(BF)
        slot = jnp.where(place[3] == j % 2, 0, 1)
        out_a[slot, j // 2] = total[:, :half]
        out_b[slot, j // 2] = total[:, half:]
        if j % 2:
            out_a.send(j // 2)
            out_b.send(j // 2)


def gate_weight_kernel(cuts, place, *refs):
    one, two = place[1], place[2]
    out_a, out_g = refs[4 * len(cuts) :]
    ins_a, ins_g = refs[: 2 * len(cuts)], refs[2 * len(cuts) : 4 * len(cuts)]
    for ins, out, mine in ((ins_a, out_a, two), (ins_g, out_g, one)):
        if out is out_a:
            for i in ins_a:
                i[...]
            for i in ins_g:
                i.start_all()
        for z in range(out_a.ref.shape[1]):
            start = 0
            for p, size in enumerate(cuts):
                cols_in, rows_in = ins[2 * p : 2 * p + 2]
                total = tn(cols_in[:, 2 * z * size : 2 * (z + 1) * size], rows_in[...]).astype(BF)
                for i in range(2):
                    out[jnp.where(mine == i, 0, 1), z, start : start + size] = total[
                        i * size : (i + 1) * size
                    ]
                start += size
            out.send(z)


def combine_kernel(counts, place, *refs):
    sent_out, kept_out = refs[sum(counts) :]
    first = at = 0
    for count in counts:
        terms = refs[at : at + count]
        at += count
        total = sum(t[...].astype(F32) for t in terms).astype(BF)
        size = total.shape[1]
        sent_out[first : first + size] = total[0]
        kept_out[first : first + size] = total[1]
        first += size


def combine(place, which, groups):
    def term(array):
        outer, _, rows, lanes = array.shape

        def plan(bit):
            return [[(0, (slice(None), 1 - bit), (0,)), (0, (slice(None), bit), (1,))]]

        return In(array, shape=(2, outer, rows, lanes), plan=plan, which=which)

    ins = [term(a) for group in groups for a in group]
    outer = sum(group[0].shape[0] for group in groups)
    rows, lanes = groups[0][0].shape[2:]
    return call(
        functools.partial(combine_kernel, [len(group) for group in groups]),
        [place],
        ins,
        [Out((outer, rows, lanes), BF)] * 2,
    )


def shards(n, tokens, condition, positions, weight_codes, loss_table, out_grad, mod_attn,
           qkv_weight, attn_scale, out_weight, mod_ff, up_weight, down_weight):
    images, part, width = tokens.shape
    rows = images * part
    half = width // 2
    heads = attn_scale.shape[0]
    ff = 2 * down_weight.shape[0]
    low = 1 if n <= 16 else n // 8
    high = n // (4 * low)
    me = lax.axis_index("dp")
    core = lax.axis_index("seq")
    one = (me // low) % 2
    two = (me // (2 * low)) % 2
    three = (me // (4 * low)) % 2
    bit_strides = [low, 2 * low, 4 * low]
    bit_strides += [1 << i for i in range(n.bit_length() - 1) if 1 << i not in bit_strides]
    place = jnp.stack([core] + [(me // b) % 2 for b in bit_strides]).astype(jnp.int32)

    def swap(values):
        return lax.ppermute(values, "seq", [(0, 1), (1, 0)])

    def cross(values, stride):
        return lax.ppermute(
            values, "dp", [(i, i + stride - 2 * stride * ((i // stride) % 2)) for i in range(n)]
        )

    def pick(values, index, axis=0):
        return lax.dynamic_index_in_dim(values, index, axis, keepdims=False)

    def tie(*values):
        return lax.optimization_barrier(values)

    first = swap(tokens), swap(mod_attn), swap(mod_ff), swap(positions)
    tokens_got, mod_attn_got, mod_ff_got, pos_got, qkv_w, out_w = tie(
        *first, qkv_weight, out_weight
    )
    qkv_got, out_got = swap(qkv_w), swap(out_w)
    hidden_one, h1, mod_one, mod_two = call(
        norm_kernel,
        [place],
        [image(tokens, tokens_got), In(condition), by_rows(mod_attn, mod_attn_got)]
        + [image(tokens, tokens_got, False), by_rows(mod_ff, mod_ff_got)],
        [Out((rows, width), BF), Out((rows, width), BF), Out((1, width), F32)]
        + [Out((1, width), F32)],
    )
    qkv_got, out_got, hidden_one, og_w, up_w, down_w = tie(
        qkv_got, out_got, hidden_one, out_grad, up_weight, down_weight
    )
    og_got, up_got, down_got = swap(og_w), swap(up_w), swap(down_w)
    h1_one, h1_two = cross(h1, low), cross(h1, 2 * low)

    table = In(jnp.asarray(angle_constants(heads)))
    pos_in = [In(positions), In(pos_got)]
    q_raw, k_raw, value, both, res = call(
        forward_kernel,
        [place, attn_scale],
        [In(hidden_one), by_rows(qkv_weight, qkv_got, 3, LANES)]
        + pos_in
        + [table, image(tokens, tokens_got, late=True)]
        + [by_rows(out_weight, out_got, late=True), In(mod_two, late=True)],
        [Out((rows, width), dtype, 1, width // LANES) for dtype in (F32, F32, BF)]
        + [Out((rows, width), BF, into={0: ("both", width)})]
        + [Out((rows, width), BF, into={0: ("both", 0)}), Out((rows, width), F32)],
    )
    both, h1_one, h1_two = tie(both, h1_one, h1_two)
    both_one, both_two, both_sib = cross(both, low), cross(both, 2 * low), swap(both)

    block = ff // 4
    wide = ff // 2 + width // 4
    gate = call(
        functools.partial(feed_kernel, high),
        [place, weight_codes, loss_table],
        [pile((both, 0), width=width), by_rows_order(up_weight, up_got, 2, block, (0, 2, 1, 3))]
        + [image(out_grad, og_got, late=True), by_row_blocks(down_weight, down_got, block, True)]
        + [image(out_grad, og_got, False, True), In(res, late=True), In(mod_two, late=True)],
        [Out((rows, wide), BF, 2, into={0: ("pack", 0)}, cuts=[*range(0, ff // 2 + 1, ff // 8), wide])]
        + [Out((rows, wide), BF, 2, into={0: ("pack", wide)}, cuts=[0, ff // 2, wide])]
        + [Out((rows, ff // 2), BF, 2, 2, into={1: ("pack", 2 * wide)})]
        + [Out((rows, width), BF), Out((rows, width), BF, 2), Out((rows, width), BF)]
        + [Out((1, width), F32)],
        [pltpu.VMEM((rows, width), F32)] * 2,
    )
    pack, send_a, send_g, act_own, res_low, cot, cot_sib, *rest = gate
    mixed_mine, mod_two_grad = rest
    send_a, send_g, pack, res_low, both_one, both_two, both_sib = tie(
        send_a, send_g, pack, res_low, both_one, both_two, both_sib
    )
    pair_a, pair_g = cross(send_a, low), cross(send_g, 2 * low)
    pack_sib, both_one_sib, both_two_sib = swap(pack), swap(both_one), swap(both_two)

    third = 3 * width // 4
    cond_cols = condition.shape[1]
    keep_q, send_qa, send_qg, line_kept, line, tokens_mine = call(
        functools.partial(backward_kernel, high),
        [place, attn_scale],
        [In(res_low), by_row_blocks(out_weight, out_got, LANES)]
        + [by_pieces(a, width // LANES) for a in (q_raw, k_raw, value)]
        + pos_in
        + [table, by_rows(qkv_weight, qkv_got, late=True), image(tokens, tokens_got, True, True)]
        + [In(a, late=True) for a in (mod_one, mod_two_grad, condition)],
        [Out((rows, third), BF, 2, into={0: ("keep", 0)})]
        + [Out((rows, third), BF, 2, into={0: ("keep", third)})]
        + [Out((1, width), F32, 2, into={1: ("line", 0)})]
        + [Out((1, cond_cols), F32, into={0: ("line", width)})]
        + [Out((1, width), F32, into={0: ("line", width + cond_cols)})]
        + [Out((rows, width), F32)],
        [pltpu.VMEM((rows, 3 * width), BF)],
    )
    cot, keep_q, send_qa, send_qg, pack_sib, both_one_sib, both_two_sib = tie(
        cot, keep_q, send_qa, send_qg, pack_sib, both_one_sib, both_two_sib
    )

    def take(values, index, axis=0):
        return pick(values, index, axis).astype(F32)

    high_bits, low_bits = high.bit_length() - 1, low.bit_length() - 1
    high_strides = [4 * low << (high_bits - 1 - i) for i in range(high_bits)]
    low_strides = [1 << (low_bits - 1 - i) for i in range(low_bits)]
    line_strides, line_order = high_strides + low_strides, high_strides[::-1] + low_strides

    def hand_on(grads, rest, stride):
        bit = (me // stride) % 2
        split = grads.reshape(grads.shape[0], 2, 2, -1)
        sent = pick(split, 1 - bit, 2).reshape(grads.shape[0], -1)
        got = cross(jnp.concatenate([sent, rest], axis=1), stride)
        return pick(split, bit, 2).reshape(grads.shape[0], -1), rest, got, bit

    def taken(mine, rest, got, bit):
        mine = jnp.concatenate([mine, rest], axis=1)
        every = jnp.where(
            bit == 0,
            jnp.concatenate([mine, got], axis=0),
            jnp.concatenate([got, mine], axis=0),
        )
        wide = mine.shape[1] - rest.shape[1]
        return every[:, :wide].reshape(every.shape[0], 2, -1), every[:, wide:]

    line_steps = [s for s in (n >> (i + 1) for i in range(n.bit_length() - 1)) if s != 4 * low]
    keep_q_sib = swap(keep_q)
    pair_qa, pair_qg = cross(send_qa, low), cross(send_qg, 2 * low)

    down = call(
        down_weight_kernel,
        [place],
        [pile(cot, cot_sib), pile(act_own, (pack_sib, 2 * wide), width=ff // 2)],
        [Out((high // 2, width // high, ff // 4), BF, 2, high // 2, 0)] * 2,
    )
    line_got = cross(line, 4 * low)
    pair_a, pair_g, line_got, down[0] = tie(pair_a, pair_g, line_got, down[0])
    small = [line_kept, line[:, width:], line_got, three]
    down_got_a = cross(down[1], 4 * low)
    def rows_of(first, far, far_sib):
        return pile(
            (both, first), (both_sib, first), (far, first), (far_sib, first), width=width, halved=True
        )

    def late(value):
        return value

    def gate_weight(cuts, ins_a, ins_g):
        return call(
            functools.partial(gate_weight_kernel, cuts),
            [place],
            ins_a + [late(i) for i in ins_g],
            [Out((high // 2, sum(cuts), half), BF, 2, high // 2, 0)] * 2,
        )

    pair_a_sib, pair_g_sib = swap(pair_a), swap(pair_g)
    up_parts = gate_weight(
        [ff // (2 * high)],
        [
            pile(pack, pack_sib, pair_a, pair_a_sib, width=ff // 2),
            rows_of(0, both_one, both_one_sib),
        ],
        [
            pile((pack, wide), (pack_sib, wide), pair_g, pair_g_sib, width=ff // 2),
            rows_of(0, both_two, both_two_sib),
        ],
    )
    up_parts[0], down_got_a, pair_qa, pair_qg, keep_q_sib = tie(
        up_parts[0], down_got_a, pair_qa, pair_qg, keep_q_sib
    )
    up_last = cross(up_parts[1], 2 * low), cross(up_parts[3], low)
    down_got_b = cross(down[3], 4 * low)
    def step(groups, axes, stride, lead=1):
        outer = lead << axes.index(stride)
        groups = [[v.reshape(outer, 2, -1, v.shape[-1]) for v in group] for group in groups]
        sent, kept = combine(place, 1 + bit_strides.index(stride), groups)
        return [kept, cross(sent, stride)]

    def without(axes, *strides):
        return [a for a in axes if a not in strides]

    down_axes = high_strides[:-1] + [2 * low, low] + low_strides
    down_order = [low, 2 * low] + high_strides[:-1][::-1] + low_strides
    pair_qa_sib, pair_qg_sib = swap(pair_qa), swap(pair_qg)
    at = ff // 2
    last_parts = gate_weight(
        [width // (4 * high), 3 * width // (4 * high)],
        [
            pile((pack, at), (pack_sib, at), (pair_a, at), (pair_a_sib, at), width=width // 4),
            rows_of(width, both_one, both_one_sib),
            pile(keep_q, keep_q_sib, pair_qa, pair_qa_sib, width=third),
            pile((h1, 0), (h1, half), (h1_one, 0), (h1_one, half), width=half),
        ],
        [
            pile(
                *((pack, wide + at), (pack_sib, wide + at), (pair_g, at), (pair_g_sib, at)),
                width=width // 4,
            ),
            rows_of(width, both_two, both_two_sib),
            pile((keep_q, third), (keep_q_sib, third), pair_qg, pair_qg_sib, width=third),
            pile((h1, 0), (h1, half), (h1_two, 0), (h1_two, half), width=half),
        ],
    )
    last_last = cross(last_parts[1], 2 * low), cross(last_parts[3], low)
    last_parts[0], down_got_b, small[2], *up_last = tie(
        last_parts[0], down_got_b, small[2], *up_last
    )

    def first_line(parts, got):
        if high > 2:
            groups = [[parts[2 * i], got[i]] for i in range(2)]
            return step(groups, high_strides[1:] + low_strides, line_order[0])
        groups = [[jnp.concatenate(v, axis=0) for v in ((parts[0], parts[2]), got)]]
        return step(groups, high_strides + low_strides, line_order[0])

    def rest_of(kept, got, axes, order, lead=1):
        for stride in order:
            kept, got = step([[kept, got]], axes, stride, lead)
            axes = without(axes, stride)
        return [kept, got]

    line_axes = without(high_strides + low_strides, line_order[0])

    up_line = first_line(up_parts, up_last)
    up_line[0], small[2] = tie(up_line[0], small[2])
    small = list(hand_on(*taken(*small), line_steps[0]))
    *last_last, up_line[0] = tie(*last_last, up_line[0])
    last_line = first_line(last_parts, last_last)
    down[0], last_line[0] = tie(down[0], last_line[0])
    down_line = step([[down[0], down_got_a], [down[2], down_got_b]], down_axes, down_order[0])
    up_line[1], last_line[0], small[2] = tie(up_line[1], last_line[0], small[2])
    up_line = rest_of(*up_line, line_axes, line_order[1:2])
    small = list(hand_on(*taken(*small), line_steps[1]))
    down_axes = without(down_axes, down_order[0])
    down_line[1], up_line[0] = tie(down_line[1], up_line[0])
    down_line = rest_of(*down_line, down_axes, down_order[1:2], 2)
    last_line[1], down_line[0], small[2] = tie(last_line[1], down_line[0], small[2])
    last_line = rest_of(*last_line, line_axes, line_order[1:2])
    values = tie(down_line[0], mixed_mine, tokens_mine, line_kept, line, *small[:3])
    down_line[0], mixed_mine, tokens_mine, line_kept, line = values[:5]
    small[:3] = values[5:]
    for stride in line_steps[2:]:
        small = hand_on(*taken(*small), stride)
    grads, rest = taken(*small)
    down_line = rest_of(*down_line, without(down_axes, down_order[1]), down_order[2:], 2)
    up_line[1], last_line[1], down_line[0] = tie(up_line[1], last_line[1], down_line[0])

    total = lambda kept, got: kept.astype(F32) + got.astype(F32)
    line_axes = without(line_axes, line_order[1])
    down_sum = total(*down_line)
    down_sum = jnp.concatenate([v.reshape(-1, ff // 4) for v in jnp.split(down_sum, 2)], axis=1)
    up_sum = total(*rest_of(*up_line, line_axes, line_order[2:])).reshape(-1, half)
    last_sum = total(*rest_of(*last_line, line_axes, line_order[2:])).reshape(-1, half)

    cond_rows = mod_attn.shape[0]
    grads = grads.reshape(grads.shape[0], -1)
    wide = grads.shape[1]
    every = jnp.concatenate([grads, rest], axis=1)
    every = jnp.concatenate([every, swap(every)], axis=0)
    cond_all = lax.dynamic_slice_in_dim(every, wide + core * cond_rows, cond_rows, 1)
    mod_attn_grad = jnp.dot(cond_all.T, every[:, : wide // 2], precision=FINEST)
    mod_ff_grad = jnp.dot(cond_all.T, every[:, wide // 2 : wide], precision=FINEST)
    lanes = jnp.sum(every[:, wide + cond_cols :].reshape(2, -1, width), axis=1)
    lanes = jnp.sum((lanes[0] + lanes[1]).reshape(heads, HEAD_DIM), axis=1)
    scale_grad = lanes / (2.0 * attn_scale)

    def row_of(parts):
        cells = parts.reshape(2, high // 2, -1)
        cells = jnp.where(three == 0, cells, cells[::-1])
        return jnp.swapaxes(cells, 0, 1).reshape(1, width)

    mods = jnp.concatenate([mod_attn, mod_ff], axis=1)
    mine = [jnp.concatenate([a, b], axis=0) for a, b in zip(*[jnp.split(v[:, :width], 2, axis=1) for v in (line_kept, line)])]
    mine = jnp.concatenate([row_of(v) for v in mine], axis=1)
    got = swap(mine)
    pair = jnp.where(
        core == 0, jnp.concatenate([mine, got], axis=0), jnp.concatenate([got, mine], axis=0)
    )
    cond_part = jnp.dot(pair, mods.astype(F32).T, precision=FINEST)
    cond_got = swap(cond_part)
    condition_grad = jnp.where(
        core == 0,
        jnp.concatenate([cond_part, cond_got], axis=1),
        jnp.concatenate([cond_got, cond_part], axis=1),
    )

    out_cols = last_sum.shape[0] // 4

    def home(values):
        got = swap(values[part:])
        own = values[:part]
        return jnp.where(core == 0, jnp.stack([own, got]), jnp.stack([got, own]))

    def turned(values):
        return values.astype(F32).T

    return (
        home(mixed_mine),
        home(tokens_mine),
        condition_grad,
        mod_attn_grad,
        turned(last_sum[out_cols:]),
        scale_grad,
        turned(last_sum[:out_cols]),
        mod_ff_grad,
        turned(up_sum),
        turned(down_sum),
    )


def solution(mesh):
    n = mesh.shape["dp"]

    def body(*args):
        return shards(n, *args)

    return jax.shard_map(
        body,
        mesh=mesh,
        in_specs=(
            P("dp", "seq", None),
            P("dp", None),
            P("dp", None, "seq"),
            P("dp"),
            P(),
            P("dp", "seq", None),
            P("seq", None),
            P("seq", None),
            P(),
            P("seq", None),
            P("seq", None),
            P("seq", None),
            P("seq", None),
        ),
        out_specs=(
            P("dp", "seq", None),
            P("dp", "seq", None),
            P("dp", None),
            P("seq", "dp"),
            P("seq", "dp"),
            P(),
            P("seq", "dp"),
            P("seq", "dp"),
            P("seq", "dp"),
            P("seq", "dp"),
        ),
        check_vma=False,
    )
```

```python
import functools
import math

import jax
import jax.numpy as jnp
import ml_dtypes
import numpy as np
from jax import lax
from jax.experimental import pallas as pl
from jax.experimental.pallas import tpu as pltpu
from jax.sharding import PartitionSpec as P

HEAD_DIM = 64
GRID = 16
EPS = 1e-06
BF = jnp.bfloat16
F32 = jnp.float32
FINEST = lax.Precision.HIGHEST
LANES = 256
VMEM = 63 * 1024 * 1024


def nn(a, b):
    return lax.dot_general(a, b, (((1,), (0,)), ((), ())), preferred_element_type=F32)


def nt(a, b):
    return lax.dot_general(a, b, (((1,), (1,)), ((), ())), preferred_element_type=F32)


def tn(a, b):
    return lax.dot_general(a, b, (((0,), (0,)), ((), ())), preferred_element_type=F32)


def angle_constants(heads):
    quarter = HEAD_DIM // 8
    counter = np.arange(quarter)[None, :] * heads + np.arange(heads)[:, None]
    freq = (math.pi * np.power(10.0, counter / (heads * quarter))).astype(np.float32)
    coords = ((2.0 * np.arange(GRID) + 1.0) / GRID - 1.0).astype(np.float32)
    angles = (coords[:, None, None] * freq[None]).astype(np.float32).astype(np.float64)
    cos, sin = np.cos(angles), np.sin(angles)
    table = np.zeros((3, 2, GRID, heads, HEAD_DIM))
    q = quarter
    for part in range(2):
        lo = part * q
        table[0, part, :, :, lo : lo + q] = cos
        table[0, part, :, :, 2 * q + lo : 3 * q + lo] = cos
        table[1, part, :, :, lo : lo + q] = -sin
        table[2, part, :, :, 2 * q + lo : 3 * q + lo] = sin
    table[0, 0, :, :, 4 * q :] = 1.0
    rest = table.reshape(3, 2 * GRID, heads * HEAD_DIM).astype(np.float32)
    terms = []
    for _ in range(3):
        terms.append(rest.astype(ml_dtypes.bfloat16))
        rest = rest - terms[-1].astype(np.float32)
    return np.concatenate(terms, axis=1)


def segment_matrix():
    rows = lax.broadcasted_iota(jnp.int32, (LANES, LANES), 0) // HEAD_DIM
    cols = lax.broadcasted_iota(jnp.int32, (LANES, LANES), 1) // HEAD_DIM
    return (rows == cols).astype(F32).astype(BF)


def segment_sum(values, ones):
    high = values.astype(BF)
    low = (values - high.astype(F32)).astype(BF)
    return nn(high, ones) + nn(low, ones)


def onehot_of(places):
    cells = lax.broadcasted_iota(jnp.int32, (GRID, places.shape[1]), 0)
    hot = [(places[i : i + 1] == cells).astype(F32) for i in range(2)]
    return jnp.concatenate(hot * 3, axis=0).astype(BF)


def tables_of(onehot, tab_ref, at):
    return [tn(onehot, tab_ref[i, :, at : at + LANES]) for i in range(3)]


def spin(values, tabs, sign):
    cos, first, second = tabs
    q = HEAD_DIM // 4
    turned = pltpu.roll(values, LANES - q, 1) * first + pltpu.roll(values, q, 1) * second
    return values * cos + sign * turned


def head_masks():
    lane = lax.broadcasted_iota(jnp.int32, (1, LANES), 1) // HEAD_DIM
    return [lane == h for h in range(LANES // HEAD_DIM)]


def root_of(scale_ref, group):
    masks = head_masks()
    value = jnp.zeros((1, LANES), F32)
    for h, mask in enumerate(masks):
        value = jnp.where(mask, scale_ref[group * len(masks) + h], value)
    return jnp.sqrt(value)


def normed(values):
    scale = lax.rsqrt(jnp.mean(values * values, axis=-1, keepdims=True) + EPS)
    return values * scale, scale


def norm_back(unit, scale, mod, grad):
    inner = grad * (1.0 + mod)
    into = scale * (inner - unit * jnp.mean(inner * unit, axis=-1, keepdims=True))
    return into, jnp.sum(grad * unit, axis=0, keepdims=True)


def half_of(core, values):
    half = values.shape[1] // 2
    return jnp.where(core == 0, values[:, :half], values[:, half:])


def stacked(masks, values):
    zero = jnp.zeros_like(values)
    return jnp.concatenate([jnp.where(mask, values, zero) for mask in masks], axis=0)


def abreast(values, count):
    size = values.shape[0] // count
    return jnp.concatenate([values[i * size : (i + 1) * size] for i in range(count)], axis=1)


def struct(shape, dtype):
    return jax.ShapeDtypeStruct(shape, dtype)


class In:
    def __init__(self, *arrays, shape=None, plan=None, late=False, which=0):
        self.which = which
        self.arrays, self.shape, self.late = arrays, shape or arrays[0].shape, late
        whole = tuple(slice(None) for _ in self.shape)
        self.plan = plan or (lambda core: [[(0, whole, whole)]])


class Out:
    def __init__(self, shape, dtype, count=1, pieces=1, axis=1, into=(), cuts=None):
        self.struct, self.count, self.axis = struct(shape, dtype), count, axis
        self.cuts = cuts or [shape[axis] * i // pieces for i in range(pieces + 1)]
        self.pieces = len(self.cuts) - 1
        self.into = dict(into)

    def where(self, piece):
        if self.pieces == 1:
            return ...
        return (slice(None),) * self.axis + (slice(self.cuts[piece], self.cuts[piece + 1]),)


class Held:
    def __init__(self, ref, pieces):
        self.ref, self.shape, self.pieces = ref, ref.shape, pieces
        self.started, self.waited = set(), set()

    def start(self, piece):
        if piece < len(self.pieces) and piece not in self.started:
            self.started.add(piece)
            for copy in self.pieces[piece]:
                copy.start()

    def need(self, piece):
        self.start(piece)
        if piece not in self.waited:
            self.waited.add(piece)
            for copy in self.pieces[piece]:
                copy.wait()

    def start_all(self):
        for piece in range(len(self.pieces)):
            self.start(piece)

    def __getitem__(self, where):
        for piece in range(len(self.pieces)):
            self.need(piece)
        return self.ref[where]


class Made:
    def __init__(self, ref, copies):
        self.ref, self.copies, self.sent = ref, copies, set()

    def __setitem__(self, where, values):
        self.ref[where] = values

    def __getitem__(self, where):
        return self.ref[where]

    def send(self, piece=None):
        for i in range(len(self.copies)) if piece is None else (piece,):
            if i not in self.sent:
                self.sent.add(i)
                for copy in self.copies[i]:
                    copy.start()


def call(kernel, tables, inputs, outputs, scratch=()):
    arrays = [a for i in inputs for a in i.arrays]
    names, structs = [], []
    for i, o in enumerate(outputs):
        for k in range(o.count):
            name, column = o.into.get(k, ((i, k), 0))
            if name not in names:
                names.append(name)
                structs.append(o.struct)
            at = names.index(name)
            wide = max(structs[at].shape[-1], column + o.struct.shape[-1])
            structs[at] = struct((*o.struct.shape[:-1], wide), o.struct.dtype)

    def body(*refs):
        refs = list(refs)

        def some(count):
            taken = refs[:count]
            del refs[:count]
            return taken

        scalars, sources, targets = some(len(tables)), some(len(arrays)), some(len(structs))
        held, made = some(len(inputs)), some(len(outputs))
        in_sems, out_sems = some(len(inputs)), some(1)[0]
        extra = refs
        ins, outs = [], []
        for i, ref, sems in zip(inputs, held, in_sems):
            from_refs = [sources.pop(0) for _ in i.arrays]
            pieces, count = [], 0
            for piece in i.plan(scalars[0][i.which]):
                copies = []
                for which, a, b in piece:
                    copies.append(
                        pltpu.make_async_copy(from_refs[which].at[a], ref.at[b], sems.at[count])
                    )
                    count += 1
                pieces.append(copies)
            ins.append(Held(ref, pieces))
        for i, given in zip(ins, inputs):
            if not given.late:
                i.start(0)
        count = 0
        for o, ref in zip(outputs, made):
            copies = [[] for _ in range(o.pieces)]
            for k in range(o.count):
                name, column = o.into.get(k, ((len(outs), k), 0))
                target, source = targets[names.index(name)], ref if o.count == 1 else ref.at[k]
                if k in o.into:
                    target = target.at[:, column : column + o.struct.shape[-1]]
                for p in range(o.pieces):
                    where = o.where(p)
                    copies[p].append(
                        pltpu.make_async_copy(source.at[where], target.at[where], out_sems.at[count])
                    )
                    count += 1
            outs.append(Made(ref, copies))
        kernel(*scalars, *ins, *outs, *extra)
        for o in outs:
            o.send()
        for i in ins:
            for piece in range(len(i.pieces)):
                i.need(piece)
        for o in outs:
            for piece in o.copies:
                for copy in piece:
                    copy.wait()

    results = pl.pallas_call(
        body,
        out_shape=structs,
        in_specs=[pl.BlockSpec(memory_space=pltpu.SMEM)] * len(tables)
        + [pl.BlockSpec(memory_space=pltpu.HBM)] * len(arrays),
        out_specs=[pl.BlockSpec(memory_space=pltpu.HBM)] * len(structs),
        scratch_shapes=[pltpu.VMEM(i.shape, i.arrays[0].dtype) for i in inputs]
        + [
            pltpu.VMEM(o.struct.shape if o.count == 1 else (o.count, *o.struct.shape), o.struct.dtype)
            for o in outputs
        ]
        + [pltpu.SemaphoreType.DMA((sum(len(p) for p in i.plan(0)),)) for i in inputs]
        + [pltpu.SemaphoreType.DMA((sum(o.count * o.pieces for o in outputs),))]
        + list(scratch),
        compiler_params=pltpu.CompilerParams(vmem_limit_bytes=VMEM),
    )(*tables, *arrays)
    return list(results)


def at_half(core, which, size):
    part = core if which == 0 else 1 - core
    return pl.ds(pl.multiple_of(part * size, size), size)


def by_rows(own, got, parts=1, block=None, late=False):
    rows, cols = own.shape
    block = block or cols // parts

    def plan(core):
        for j in range(cols // parts // block):
            piece = []
            for p in range(parts):
                where = slice(p * (cols // parts) + j * block, p * (cols // parts) + (j + 1) * block)
                for k in range(2):
                    piece.append((k, (slice(None), where), (at_half(core, k, rows), where)))
            yield piece

    return In(own, got, shape=(2 * rows, cols), plan=plan, late=late)


def by_pieces(array, pieces, late=False):
    size = array.shape[-1] // pieces
    wheres = [
        (slice(None),) * (len(array.shape) - 1) + (slice(p * size, (p + 1) * size),)
        for p in range(pieces)
    ]
    return In(array, plan=lambda core: [[(0, where, where)] for where in wheres], late=late)


def by_rows_order(own, got, parts, block, order):
    made = by_rows(own, got, parts, block)
    pieces = made.plan

    def plan(core):
        every = list(pieces(core))
        return [every[i] for i in order]

    made.plan = plan
    return made


def by_row_blocks(own, got, block, late=False):
    rows, cols = own.shape

    def plan(core):
        for j in range(rows // block):
            piece = []
            for k in range(2):
                part = core if k == 0 else 1 - core
                there = pl.ds(pl.multiple_of(part * rows + j * block, block), block)
                piece.append((k, (slice(j * block, (j + 1) * block),), (there,)))
            yield piece

    return In(own, got, shape=(2 * rows, cols), plan=plan, late=late)


def image(own, got, mine=True, late=False):
    part, width = own.shape[1:]

    def plan(core):
        which = core if mine else 1 - core
        first, second = (0, 1) if mine else (1, 0)
        return [
            [
                (first, (which,), (slice(0, part),)),
                (second, (which,), (slice(part, 2 * part),)),
            ]
        ]

    return In(own, got, shape=(2 * part, width), plan=plan, late=late)


def pile(*arrays, width=None, pieces=1, halved=False, late=False):
    arrays = [a if isinstance(a, tuple) else (a, 0) for a in arrays]
    rows, cols = arrays[0][0].shape
    cols = (width or cols) // (2 if halved else 1)
    size = cols // pieces

    def plan(core):
        for p in range(pieces):
            there = slice(p * size, (p + 1) * size)
            piece = []
            for i, (_, first) in enumerate(arrays):
                at = first + p * size
                here = slice(at, at + size)
                if halved:
                    here = pl.ds(pl.multiple_of(core * cols + at, 128), size)
                piece.append((i, (slice(None), here), (slice(i * rows, (i + 1) * rows), there)))
            yield piece

    return In(*[a for a, _ in arrays], shape=(len(arrays) * rows, cols), plan=plan, late=late)


def norm_kernel(place, x, cond, mod, xs, mod_ff, hid_out, h1, row_one, row_two):
    core = place[0]
    rows = nn(cond[...], mod[...])
    first, second = rows[0:1], rows[1:2]
    row, row_sib = jnp.where(core == 0, first, second), jnp.where(core == 0, second, first)
    row_one[...] = row
    unit, _ = normed(x[...].astype(F32))
    hidden = (unit * (1.0 + row)).astype(BF)
    hid_out[...] = hidden
    hid_out.send()
    half = hidden.shape[1] // 2
    h1[:, :half] = half_of(core, hidden)
    unit, _ = normed(xs[...].astype(F32))
    h1[:, half:] = half_of(core, (unit * (1.0 + row_sib)).astype(BF))
    h1.send()
    rows = nn(cond[...], mod_ff[...])
    row_two[...] = jnp.where(core == 0, rows[0:1], rows[1:2])


def forward_kernel(
    place, scales, hid, weight, pos, posg, tab, x, out_weight, mod,
    q_out, k_out, v_out, att, hid_out, res_out,
):
    core = place[0]
    width = x.shape[1]
    hidden = hid[...]
    onehot = onehot_of(jnp.concatenate([pos[core], posg[core]], axis=1))
    ones = segment_matrix()
    masks = head_masks()
    heads = len(masks)
    spread = stacked(masks, jnp.ones((LANES, LANES), BF))
    steps = width // LANES
    weight.need(0)
    for j in range(1, steps):
        weight.start(j)
    tab[...]
    for j in range(steps):
        here = slice(j * LANES, (j + 1) * LANES)
        if j == 1:
            for i in (out_weight, x, mod):
                i.start(0)
            weight[...]
            for out in (q_out, k_out, v_out):
                out.send(0)
        q, k, v = [
            nn(hidden, weight.ref[:, i * width + j * LANES : i * width + (j + 1) * LANES])
            for i in range(3)
        ]
        v = v.astype(BF)
        q_out[:, here] = q
        k_out[:, here] = k
        v_out[:, here] = v
        tabs = tables_of(onehot, tab.ref, j * LANES)
        root = root_of(scales, j)
        qr = spin(q * (lax.rsqrt(segment_sum(q * q, ones) + EPS) * root), tabs, 1.0).astype(BF)
        kr = spin(k * (lax.rsqrt(segment_sum(k * k, ones) + EPS) * root), tabs, 1.0).astype(BF)
        expo = abreast(jnp.exp(nt(stacked(masks, qr), kr)).astype(BF), heads)
        total = (nn(expo, stacked(masks, v)) / nn(expo, spread)).astype(BF)
        att[:, here] = total
    for out in (q_out, k_out, v_out, att):
        out.send()
    residual = x[...].astype(F32) + nn(att[...], out_weight[...])
    res_out[...] = residual
    unit, _ = normed(residual)
    hid_out[...] = (unit * (1.0 + mod[...])).astype(BF)


def dealt(values, high, bit, axis):
    size = values.shape[1] // (2 * high)
    kept, sent = [], []
    for cell in range(2 * high):
        if not cell & axis:
            zero = values[:, cell * size : (cell + 1) * size]
            unit = values[:, (cell + axis) * size : (cell + axis + 1) * size]
            kept.append(jnp.where(bit == 0, zero, unit))
            sent.append(jnp.where(bit == 0, unit, zero))
    return jnp.concatenate(kept, axis=1), jnp.concatenate(sent, axis=1)


def feed_kernel(
    high, place, codes, losses, hid, up, og, down, ogs, res, mod,
    gu_a, gu_g, act, rlow_out, cots, mixed_out, mgrad_out, grad_ref, mix_ref,
):
    core, one, two = place[0], place[1], place[2]
    ff = up.shape[1] // 2
    block = ff // 4
    unit_cols = ff // (2 * high)
    half = high // 2
    scale = losses[codes[core]]
    order = (0, 2, 1, 3)
    hidden = hid[...]
    up.need(0)
    down.start(0)
    og.start(0)

    def gates(b):
        a = nn(hidden, up.ref[:, b * block : (b + 1) * block])
        return a, nn(hidden, up.ref[:, ff + b * block : ff + (b + 1) * block])

    def finish(b, a, g, first):
        here = slice(b * block, (b + 1) * block)
        there = slice(ff + b * block, ff + (b + 1) * block)
        phi = 0.5 + 0.5 * lax.erf(g * (1.0 / math.sqrt(2.0)))
        gelu = g * phi
        active = (a * gelu).astype(BF)
        slope = a * (phi + g * (jnp.exp(-0.5 * g * g) * (1.0 / math.sqrt(2.0 * math.pi))))
        act[jnp.where(core == b // 2, 0, 1), :, (b % 2) * block : (b % 2 + 1) * block] = active
        act_grad = nt(cot, down.ref[here])
        a_grad = (act_grad * gelu).astype(BF)
        g_grad = (act_grad * slope).astype(BF)
        for c in range(block // unit_cols):
            cell = b * (block // unit_cols) + c
            cols = slice(c * unit_cols, (c + 1) * unit_cols)
            z, y, x = cell // 4, cell // 2 % 2, cell % 2
            at = (2 * z + y) * unit_cols
            gu_a[jnp.where(one == x, 0, 1), :, at : at + unit_cols] = a_grad[:, cols]
            at = (2 * z + x) * unit_cols
            gu_g[jnp.where(two == y, 0, 1), :, at : at + unit_cols] = g_grad[:, cols]
        mixed = nn(active, down.ref[here])
        grad = nt(a_grad, up.ref[:, here]) + nt(g_grad, up.ref[:, there])
        mix_ref[...] = mixed if first else mix_ref[...] + mixed
        grad_ref[...] = grad if first else grad_ref[...] + grad

    gate = gates(order[0])
    cot = (og[...].astype(F32) * scale).astype(BF)
    cots[0] = cot
    down.need(0)
    up.start(1)
    finish(order[0], *gate, True)
    up.need(1)
    for i in (up, down, ogs, res, mod):
        i.start_all()
    finish(order[1], *gates(order[1]), False)
    for i in (up, down, ogs, res, mod):
        i[...]
    if high == 4:
        gu_a.send(0)
        gu_a.send(2)
        act.send(0)
    cots[1] = (ogs[...].astype(F32) * losses[codes[1 - core]]).astype(BF)
    cots.send()
    later = gates(order[2])
    finish(order[2], *later, False)
    finish(order[3], *gates(order[3]), False)
    for i in range(4):
        gu_a.send(i)
    gu_g.send(0)
    act.send()
    residual = res[...]
    unit, size = normed(residual)
    into, mgrad = norm_back(unit, size, mod[...], grad_ref[...])
    mgrad_out[...] = mgrad
    total = og[...].astype(F32) * scale + into
    low = total.astype(BF)
    rlow_out[...] = low
    middle, end = low.shape[1] // 2, ff // 2
    for out, values, bit, axis in ((gu_a, low[:, :middle], one, 1), (gu_g, low[:, middle:], two, 2)):
        kept, sent = dealt(values, high, bit, axis)
        out[0, :, end:] = kept
        out[1, :, end:] = sent
        out.send()
    rlow_out.send()
    mixed_out[...] = (residual + mix_ref[...]).astype(BF)


def backward_kernel(
    high, place, scales, rlow, weight, q_in, k_in, v_in, pos, posg, tab, qkv, x, mod, row_two, cond,
    cells_a, cells_g, rows_out, cond_out, scale_out, tgrad_out, qkv_out,
):
    core, one, two = place[0], place[1], place[2]
    width = x.shape[1]
    onehot = onehot_of(jnp.concatenate([pos[core], posg[core]], axis=1))
    ones = segment_matrix()
    masks = head_masks()
    heads = len(masks)
    low = rlow[...]
    for j in range(width // LANES):
        here = slice(j * LANES, (j + 1) * LANES)
        if j == 0:
            for i in (weight, q_in, k_in, v_in, tab):
                i.start_all()
            for i in (weight, q_in, k_in, v_in, tab):
                i.need(0)
        if j == 1:
            for i in (qkv, x, mod, row_two, cond):
                i.start_all()
            for i in (weight, q_in, k_in, v_in, tab):
                i[...]
        grad = nt(low, weight.ref[here]).astype(BF)
        tabs = tables_of(onehot, tab.ref, j * LANES)
        root = root_of(scales, j)
        q, k, v = q_in.ref[:, here], k_in.ref[:, here], v_in.ref[:, here]
        q_inv = lax.rsqrt(segment_sum(q * q, ones) + EPS)
        k_inv = lax.rsqrt(segment_sum(k * k, ones) + EPS)
        q_scale, k_scale = q_inv * root, k_inv * root
        qr = spin(q * q_scale, tabs, 1.0).astype(BF)
        kr = spin(k * k_scale, tabs, 1.0).astype(BF)
        q_heads, g_heads = stacked(masks, qr), stacked(masks, grad)
        expo = jnp.exp(nt(kr, q_heads))
        prob = expo * (1.0 / jnp.sum(expo, axis=0, keepdims=True))
        weighted = prob * nt(v, g_heads)
        sgrad = (weighted - prob * jnp.sum(weighted, axis=0, keepdims=True)).astype(BF)
        dv = nn(prob.astype(BF), g_heads).astype(BF)
        dk = spin(nn(sgrad, q_heads), tabs, -1.0)
        size = qr.shape[0]
        turned = jnp.concatenate(
            [sgrad[:, i * size : (i + 1) * size] for i in range(heads)], axis=0
        )
        dq = spin(tn(turned, stacked(masks, kr)), tabs, -1.0)
        q_dot, k_dot = dq * q, dk * k
        scale_out[:, here] = jnp.sum(q_dot * q_scale + k_dot * k_scale, axis=0, keepdims=True)
        gq = (q_scale * (dq - q * (segment_sum(q_dot, ones) * (q_inv * q_inv)))).astype(BF)
        gk = (k_scale * (dk - k * (segment_sum(k_dot, ones) * (k_inv * k_inv)))).astype(BF)
        for i, part in enumerate((gq, gk, dv)):
            qkv_out[:, i * width + j * LANES : i * width + (j + 1) * LANES] = part
    every = cond[...].astype(F32)
    cond_out[...] = jnp.where(core == 0, every[0:1], every[1:2])
    middle = qkv_out.shape[1] // 2
    for out, at, bit, axis in ((cells_a, 0, one, 1), (cells_g, middle, two, 2)):
        kept, sent = dealt(qkv_out[:, at : at + middle], high, bit, axis)
        out[0] = kept
        out[1] = sent
        out.send()
    unit, size = normed(x[...].astype(F32))
    into, mgrad = norm_back(unit, size, mod[...], nt(qkv_out[...], qkv[...]))
    tgrad_out[...] = low.astype(F32) + into
    for i, row in enumerate((mgrad, row_two[...])):
        kept, sent = dealt(row, high // 2, place[3], 1)
        rows_out[0, :, i * kept.shape[1] : (i + 1) * kept.shape[1]] = kept
        rows_out[1, :, i * kept.shape[1] : (i + 1) * kept.shape[1]] = sent


def down_weight_kernel(place, cols_in, rows_in, out_a, out_b):
    parts, size, half = out_a.ref.shape[1:]
    for j in range(2 * parts):
        total = tn(cols_in[:, j * size : (j + 1) * size], rows_in[...]).astype(BF)
        slot = jnp.where(place[3] == j % 2, 0, 1)
        out_a[slot, j // 2] = total[:, :half]
        out_b[slot, j // 2] = total[:, half:]
        if j % 2:
            out_a.send(j // 2)
            out_b.send(j // 2)


def gate_weight_kernel(cuts, place, *refs):
    one, two = place[1], place[2]
    out_a, out_g = refs[4 * len(cuts) :]
    ins_a, ins_g = refs[: 2 * len(cuts)], refs[2 * len(cuts) : 4 * len(cuts)]
    for ins, out, mine in ((ins_a, out_a, two), (ins_g, out_g, one)):
        if out is out_a:
            for i in ins_a:
                i[...]
            for i in ins_g:
                i.start_all()
        for z in range(out_a.ref.shape[1]):
            start = 0
            for p, size in enumerate(cuts):
                cols_in, rows_in = ins[2 * p : 2 * p + 2]
                total = tn(cols_in[:, 2 * z * size : 2 * (z + 1) * size], rows_in[...]).astype(BF)
                for i in range(2):
                    out[jnp.where(mine == i, 0, 1), z, start : start + size] = total[
                        i * size : (i + 1) * size
                    ]
                start += size
            out.send(z)


def combine_kernel(counts, place, *refs):
    sent_out, kept_out = refs[sum(counts) :]
    first = at = 0
    for count in counts:
        terms = refs[at : at + count]
        at += count
        total = sum(t[...].astype(F32) for t in terms).astype(BF)
        size = total.shape[1]
        sent_out[first : first + size] = total[0]
        kept_out[first : first + size] = total[1]
        first += size


def combine(place, which, groups):
    def term(array):
        outer, _, rows, lanes = array.shape

        def plan(bit):
            return [[(0, (slice(None), 1 - bit), (0,)), (0, (slice(None), bit), (1,))]]

        return In(array, shape=(2, outer, rows, lanes), plan=plan, which=which)

    ins = [term(a) for group in groups for a in group]
    outer = sum(group[0].shape[0] for group in groups)
    rows, lanes = groups[0][0].shape[2:]
    return call(
        functools.partial(combine_kernel, [len(group) for group in groups]),
        [place],
        ins,
        [Out((outer, rows, lanes), BF)] * 2,
    )


def shards(n, tokens, condition, positions, weight_codes, loss_table, out_grad, mod_attn,
           qkv_weight, attn_scale, out_weight, mod_ff, up_weight, down_weight):
    images, part, width = tokens.shape
    rows = images * part
    half = width // 2
    heads = attn_scale.shape[0]
    ff = 2 * down_weight.shape[0]
    low = 1 if n <= 16 else n // 8
    high = n // (4 * low)
    me = lax.axis_index("dp")
    core = lax.axis_index("seq")
    one = (me // low) % 2
    two = (me // (2 * low)) % 2
    three = (me // (4 * low)) % 2
    bit_strides = [low, 2 * low, 4 * low]
    bit_strides += [1 << i for i in range(n.bit_length() - 1) if 1 << i not in bit_strides]
    place = jnp.stack([core] + [(me // b) % 2 for b in bit_strides]).astype(jnp.int32)

    def swap(values):
        return lax.ppermute(values, "seq", [(0, 1), (1, 0)])

    def cross(values, stride):
        return lax.ppermute(
            values, "dp", [(i, i + stride - 2 * stride * ((i // stride) % 2)) for i in range(n)]
        )

    def pick(values, index, axis=0):
        return lax.dynamic_index_in_dim(values, index, axis, keepdims=False)

    def tie(*values):
        return lax.optimization_barrier(values)

    first = swap(tokens), swap(mod_attn), swap(mod_ff), swap(positions)
    tokens_got, mod_attn_got, mod_ff_got, pos_got, qkv_w, out_w = tie(
        *first, qkv_weight, out_weight
    )
    qkv_got, out_got = swap(qkv_w), swap(out_w)
    hidden_one, h1, mod_one, mod_two = call(
        norm_kernel,
        [place],
        [image(tokens, tokens_got), In(condition), by_rows(mod_attn, mod_attn_got)]
        + [image(tokens, tokens_got, False), by_rows(mod_ff, mod_ff_got)],
        [Out((rows, width), BF), Out((rows, width), BF), Out((1, width), F32)]
        + [Out((1, width), F32)],
    )
    qkv_got, out_got, hidden_one, og_w, up_w, down_w = tie(
        qkv_got, out_got, hidden_one, out_grad, up_weight, down_weight
    )
    og_got, up_got, down_got = swap(og_w), swap(up_w), swap(down_w)
    h1_one, h1_two = cross(h1, low), cross(h1, 2 * low)

    table = In(jnp.asarray(angle_constants(heads)))
    pos_in = [In(positions), In(pos_got)]
    q_raw, k_raw, value, both, res = call(
        forward_kernel,
        [place, attn_scale],
        [In(hidden_one), by_rows(qkv_weight, qkv_got, 3, LANES)]
        + pos_in
        + [table, image(tokens, tokens_got, late=True)]
        + [by_rows(out_weight, out_got, late=True), In(mod_two, late=True)],
        [Out((rows, width), dtype, 1, width // LANES) for dtype in (F32, F32, BF)]
        + [Out((rows, width), BF, into={0: ("both", width)})]
        + [Out((rows, width), BF, into={0: ("both", 0)}), Out((rows, width), F32)],
    )
    both, h1_one, h1_two = tie(both, h1_one, h1_two)
    both_one, both_two, both_sib = cross(both, low), cross(both, 2 * low), swap(both)

    block = ff // 4
    wide = ff // 2 + width // 4
    gate = call(
        functools.partial(feed_kernel, high),
        [place, weight_codes, loss_table],
        [pile((both, 0), width=width), by_rows_order(up_weight, up_got, 2, block, (0, 2, 1, 3))]
        + [image(out_grad, og_got, late=True), by_row_blocks(down_weight, down_got, block, True)]
        + [image(out_grad, og_got, False, True), In(res, late=True), In(mod_two, late=True)],
        [Out((rows, wide), BF, 2, into={0: ("pack", 0)}, cuts=[*range(0, ff // 2 + 1, ff // 8), wide])]
        + [Out((rows, wide), BF, 2, into={0: ("pack", wide)}, cuts=[0, ff // 2, wide])]
        + [Out((rows, ff // 2), BF, 2, 2, into={1: ("pack", 2 * wide)})]
        + [Out((rows, width), BF), Out((rows, width), BF, 2), Out((rows, width), BF)]
        + [Out((1, width), F32)],
        [pltpu.VMEM((rows, width), F32)] * 2,
    )
    pack, send_a, send_g, act_own, res_low, cot, cot_sib, *rest = gate
    mixed_mine, mod_two_grad = rest
    send_a, send_g, pack, res_low, both_one, both_two, both_sib = tie(
        send_a, send_g, pack, res_low, both_one, both_two, both_sib
    )
    pair_a, pair_g = cross(send_a, low), cross(send_g, 2 * low)
    pack_sib, both_one_sib, both_two_sib = swap(pack), swap(both_one), swap(both_two)

    third = 3 * width // 4
    cond_cols = condition.shape[1]
    keep_q, send_qa, send_qg, line_kept, line, tokens_mine = call(
        functools.partial(backward_kernel, high),
        [place, attn_scale],
        [In(res_low), by_row_blocks(out_weight, out_got, LANES)]
        + [by_pieces(a, width // LANES) for a in (q_raw, k_raw, value)]
        + pos_in
        + [table, by_rows(qkv_weight, qkv_got, late=True), image(tokens, tokens_got, True, True)]
        + [In(a, late=True) for a in (mod_one, mod_two_grad, condition)],
        [Out((rows, third), BF, 2, into={0: ("keep", 0)})]
        + [Out((rows, third), BF, 2, into={0: ("keep", third)})]
        + [Out((1, width), F32, 2, into={1: ("line", 0)})]
        + [Out((1, cond_cols), F32, into={0: ("line", width)})]
        + [Out((1, width), F32, into={0: ("line", width + cond_cols)})]
        + [Out((rows, width), F32)],
        [pltpu.VMEM((rows, 3 * width), BF)],
    )
    cot, keep_q, send_qa, send_qg, pack_sib, both_one_sib, both_two_sib = tie(
        cot, keep_q, send_qa, send_qg, pack_sib, both_one_sib, both_two_sib
    )

    def take(values, index, axis=0):
        return pick(values, index, axis).astype(F32)

    high_bits, low_bits = high.bit_length() - 1, low.bit_length() - 1
    high_strides = [4 * low << (high_bits - 1 - i) for i in range(high_bits)]
    low_strides = [1 << (low_bits - 1 - i) for i in range(low_bits)]
    line_strides, line_order = high_strides + low_strides, high_strides[::-1] + low_strides

    def hand_on(grads, rest, stride):
        bit = (me // stride) % 2
        split = grads.reshape(grads.shape[0], 2, 2, -1)
        sent = pick(split, 1 - bit, 2).reshape(grads.shape[0], -1)
        got = cross(jnp.concatenate([sent, rest], axis=1), stride)
        return pick(split, bit, 2).reshape(grads.shape[0], -1), rest, got, bit

    def taken(mine, rest, got, bit):
        mine = jnp.concatenate([mine, rest], axis=1)
        every = jnp.where(
            bit == 0,
            jnp.concatenate([mine, got], axis=0),
            jnp.concatenate([got, mine], axis=0),
        )
        wide = mine.shape[1] - rest.shape[1]
        return every[:, :wide].reshape(every.shape[0], 2, -1), every[:, wide:]

    line_steps = [s for s in (n >> (i + 1) for i in range(n.bit_length() - 1)) if s != 4 * low]
    keep_q_sib = swap(keep_q)
    pair_qa, pair_qg = cross(send_qa, low), cross(send_qg, 2 * low)

    down = call(
        down_weight_kernel,
        [place],
        [pile(cot, cot_sib), pile(act_own, (pack_sib, 2 * wide), width=ff // 2)],
        [Out((high // 2, width // high, ff // 4), BF, 2, high // 2, 0)] * 2,
    )
    line_got = cross(line, 4 * low)
    pair_a, pair_g, line_got, down[0] = tie(pair_a, pair_g, line_got, down[0])
    small = [line_kept, line[:, width:], line_got, three]
    down_got_a = cross(down[1], 4 * low)
    def rows_of(first, far, far_sib):
        return pile(
            (both, first), (both_sib, first), (far, first), (far_sib, first), width=width, halved=True
        )

    def late(value):
        return value

    def gate_weight(cuts, ins_a, ins_g):
        return call(
            functools.partial(gate_weight_kernel, cuts),
            [place],
            ins_a + [late(i) for i in ins_g],
            [Out((high // 2, sum(cuts), half), BF, 2, high // 2, 0)] * 2,
        )

    pair_a_sib, pair_g_sib = swap(pair_a), swap(pair_g)
    up_parts = gate_weight(
        [ff // (2 * high)],
        [
            pile(pack, pack_sib, pair_a, pair_a_sib, width=ff // 2),
            rows_of(0, both_one, both_one_sib),
        ],
        [
            pile((pack, wide), (pack_sib, wide), pair_g, pair_g_sib, width=ff // 2),
            rows_of(0, both_two, both_two_sib),
        ],
    )
    up_parts[0], down_got_a, pair_qa, pair_qg, keep_q_sib = tie(
        up_parts[0], down_got_a, pair_qa, pair_qg, keep_q_sib
    )
    up_last = cross(up_parts[1], 2 * low), cross(up_parts[3], low)
    down_got_b = cross(down[3], 4 * low)
    def step(groups, axes, stride, lead=1):
        outer = lead << axes.index(stride)
        groups = [[v.reshape(outer, 2, -1, v.shape[-1]) for v in group] for group in groups]
        sent, kept = combine(place, 1 + bit_strides.index(stride), groups)
        return [kept, cross(sent, stride)]

    def without(axes, *strides):
        return [a for a in axes if a not in strides]

    down_axes = high_strides[:-1] + [2 * low, low] + low_strides
    down_order = [low, 2 * low] + high_strides[:-1][::-1] + low_strides
    pair_qa_sib, pair_qg_sib = swap(pair_qa), swap(pair_qg)
    at = ff // 2
    last_parts = gate_weight(
        [width // (4 * high), 3 * width // (4 * high)],
        [
            pile((pack, at), (pack_sib, at), (pair_a, at), (pair_a_sib, at), width=width // 4),
            rows_of(width, both_one, both_one_sib),
            pile(keep_q, keep_q_sib, pair_qa, pair_qa_sib, width=third),
            pile((h1, 0), (h1, half), (h1_one, 0), (h1_one, half), width=half),
        ],
        [
            pile(
                *((pack, wide + at), (pack_sib, wide + at), (pair_g, at), (pair_g_sib, at)),
                width=width // 4,
            ),
            rows_of(width, both_two, both_two_sib),
            pile((keep_q, third), (keep_q_sib, third), pair_qg, pair_qg_sib, width=third),
            pile((h1, 0), (h1, half), (h1_two, 0), (h1_two, half), width=half),
        ],
    )
    last_last = cross(last_parts[1], 2 * low), cross(last_parts[3], low)
    last_parts[0], down_got_b, small[2], *up_last = tie(
        last_parts[0], down_got_b, small[2], *up_last
    )

    def first_line(parts, got):
        if high > 2:
            groups = [[parts[2 * i], got[i]] for i in range(2)]
            return step(groups, high_strides[1:] + low_strides, line_order[0])
        groups = [[jnp.concatenate(v, axis=0) for v in ((parts[0], parts[2]), got)]]
        return step(groups, high_strides + low_strides, line_order[0])

    def rest_of(kept, got, axes, order, lead=1):
        for stride in order:
            kept, got = step([[kept, got]], axes, stride, lead)
            axes = without(axes, stride)
        return [kept, got]

    line_axes = without(high_strides + low_strides, line_order[0])

    up_line = first_line(up_parts, up_last)
    up_line[0], small[2] = tie(up_line[0], small[2])
    small = list(hand_on(*taken(*small), line_steps[0]))
    *last_last, up_line[0] = tie(*last_last, up_line[0])
    last_line = first_line(last_parts, last_last)
    down[0], last_line[0] = tie(down[0], last_line[0])
    down_line = step([[down[0], down_got_a], [down[2], down_got_b]], down_axes, down_order[0])
    up_line[1], last_line[0], small[2] = tie(up_line[1], last_line[0], small[2])
    up_line = rest_of(*up_line, line_axes, line_order[1:2])
    small = list(hand_on(*taken(*small), line_steps[1]))
    down_axes = without(down_axes, down_order[0])
    down_line[1], up_line[0] = tie(down_line[1], up_line[0])
    down_line = rest_of(*down_line, down_axes, down_order[1:2], 2)
    last_line[1], down_line[0], small[2] = tie(last_line[1], down_line[0], small[2])
    last_line = rest_of(*last_line, line_axes, line_order[1:2])
    values = tie(down_line[0], mixed_mine, tokens_mine, line_kept, line)
    down_line[0], mixed_mine, tokens_mine, line_kept, line = values
    down_line = rest_of(*down_line, without(down_axes, down_order[1]), down_order[2:], 2)
    up_line[1], last_line[1], down_line[0], *small[:3] = tie(
        up_line[1], last_line[1], down_line[0], *small[:3]
    )
    for stride in line_steps[2:]:
        small = hand_on(*taken(*small), stride)
    grads, rest = taken(*small)

    total = lambda kept, got: kept.astype(F32) + got.astype(F32)
    line_axes = without(line_axes, line_order[1])
    down_sum = total(*down_line)
    down_sum = jnp.concatenate([v.reshape(-1, ff // 4) for v in jnp.split(down_sum, 2)], axis=1)
    up_sum = total(*rest_of(*up_line, line_axes, line_order[2:])).reshape(-1, half)
    last_sum = total(*rest_of(*last_line, line_axes, line_order[2:])).reshape(-1, half)

    cond_rows = mod_attn.shape[0]
    grads = grads.reshape(grads.shape[0], -1)
    wide = grads.shape[1]
    every = jnp.concatenate([grads, rest], axis=1)
    every = jnp.concatenate([every, swap(every)], axis=0)
    cond_all = lax.dynamic_slice_in_dim(every, wide + core * cond_rows, cond_rows, 1)
    mod_attn_grad = jnp.dot(cond_all.T, every[:, : wide // 2], precision=FINEST)
    mod_ff_grad = jnp.dot(cond_all.T, every[:, wide // 2 : wide], precision=FINEST)
    lanes = jnp.sum(every[:, wide + cond_cols :].reshape(2, -1, width), axis=1)
    lanes = jnp.sum((lanes[0] + lanes[1]).reshape(heads, HEAD_DIM), axis=1)
    scale_grad = lanes / (2.0 * attn_scale)

    def row_of(parts):
        cells = parts.reshape(2, high // 2, -1)
        cells = jnp.where(three == 0, cells, cells[::-1])
        return jnp.swapaxes(cells, 0, 1).reshape(1, width)

    mods = jnp.concatenate([mod_attn, mod_ff], axis=1)
    mine = [jnp.concatenate([a, b], axis=0) for a, b in zip(*[jnp.split(v[:, :width], 2, axis=1) for v in (line_kept, line)])]
    mine = jnp.concatenate([row_of(v) for v in mine], axis=1)
    got = swap(mine)
    pair = jnp.where(
        core == 0, jnp.concatenate([mine, got], axis=0), jnp.concatenate([got, mine], axis=0)
    )
    cond_part = jnp.dot(pair, mods.astype(F32).T, precision=FINEST)
    cond_got = swap(cond_part)
    condition_grad = jnp.where(
        core == 0,
        jnp.concatenate([cond_part, cond_got], axis=1),
        jnp.concatenate([cond_got, cond_part], axis=1),
    )

    out_cols = last_sum.shape[0] // 4

    def home(values):
        got = swap(values[part:])
        own = values[:part]
        return jnp.where(core == 0, jnp.stack([own, got]), jnp.stack([got, own]))

    def turned(values):
        return values.astype(F32).T

    return (
        home(mixed_mine),
        home(tokens_mine),
        condition_grad,
        mod_attn_grad,
        turned(last_sum[out_cols:]),
        scale_grad,
        turned(last_sum[:out_cols]),
        mod_ff_grad,
        turned(up_sum),
        turned(down_sum),
    )


def solution(mesh):
    n = mesh.shape["dp"]

    def body(*args):
        return shards(n, *args)

    return jax.shard_map(
        body,
        mesh=mesh,
        in_specs=(
            P("dp", "seq", None),
            P("dp", None),
            P("dp", None, "seq"),
            P("dp"),
            P(),
            P("dp", "seq", None),
            P("seq", None),
            P("seq", None),
            P(),
            P("seq", None),
            P("seq", None),
            P("seq", None),
            P("seq", None),
        ),
        out_specs=(
            P("dp", "seq", None),
            P("dp", "seq", None),
            P("dp", None),
            P("seq", "dp"),
            P("seq", "dp"),
            P(),
            P("seq", "dp"),
            P("seq", "dp"),
            P("seq", "dp"),
            P("seq", "dp"),
        ),
        check_vma=False,
    )
```

```python
import functools
import math

import jax
import jax.numpy as jnp
import ml_dtypes
import numpy as np
from jax import lax
from jax.experimental import pallas as pl
from jax.experimental.pallas import tpu as pltpu
from jax.sharding import PartitionSpec as P

HEAD_DIM = 64
GRID = 16
EPS = 1e-06
BF = jnp.bfloat16
F32 = jnp.float32
FINEST = lax.Precision.HIGHEST
LANES = 256
VMEM = 63 * 1024 * 1024


def nn(a, b):
    return lax.dot_general(a, b, (((1,), (0,)), ((), ())), preferred_element_type=F32)


def nt(a, b):
    return lax.dot_general(a, b, (((1,), (1,)), ((), ())), preferred_element_type=F32)


def tn(a, b):
    return lax.dot_general(a, b, (((0,), (0,)), ((), ())), preferred_element_type=F32)


def angle_constants(heads):
    quarter = HEAD_DIM // 8
    counter = np.arange(quarter)[None, :] * heads + np.arange(heads)[:, None]
    freq = (math.pi * np.power(10.0, counter / (heads * quarter))).astype(np.float32)
    coords = ((2.0 * np.arange(GRID) + 1.0) / GRID - 1.0).astype(np.float32)
    angles = (coords[:, None, None] * freq[None]).astype(np.float32).astype(np.float64)
    cos, sin = np.cos(angles), np.sin(angles)
    table = np.zeros((3, 2, GRID, heads, HEAD_DIM))
    q = quarter
    for part in range(2):
        lo = part * q
        table[0, part, :, :, lo : lo + q] = cos
        table[0, part, :, :, 2 * q + lo : 3 * q + lo] = cos
        table[1, part, :, :, lo : lo + q] = -sin
        table[2, part, :, :, 2 * q + lo : 3 * q + lo] = sin
    table[0, 0, :, :, 4 * q :] = 1.0
    rest = table.reshape(3, 2 * GRID, heads * HEAD_DIM).astype(np.float32)
    terms = []
    for _ in range(3):
        terms.append(rest.astype(ml_dtypes.bfloat16))
        rest = rest - terms[-1].astype(np.float32)
    return np.concatenate(terms, axis=1)


def segment_matrix():
    rows = lax.broadcasted_iota(jnp.int32, (LANES, LANES), 0) // HEAD_DIM
    cols = lax.broadcasted_iota(jnp.int32, (LANES, LANES), 1) // HEAD_DIM
    return (rows == cols).astype(F32).astype(BF)


def segment_sum(values, ones):
    high = values.astype(BF)
    low = (values - high.astype(F32)).astype(BF)
    return nn(high, ones) + nn(low, ones)


def onehot_of(places):
    cells = lax.broadcasted_iota(jnp.int32, (GRID, places.shape[1]), 0)
    hot = [(places[i : i + 1] == cells).astype(F32) for i in range(2)]
    return jnp.concatenate(hot * 3, axis=0).astype(BF)


def tables_of(onehot, tab_ref, at):
    return [tn(onehot, tab_ref[i, :, at : at + LANES]) for i in range(3)]


def spin(values, tabs, sign):
    cos, first, second = tabs
    q = HEAD_DIM // 4
    turned = pltpu.roll(values, LANES - q, 1) * first + pltpu.roll(values, q, 1) * second
    return values * cos + sign * turned


def head_masks():
    lane = lax.broadcasted_iota(jnp.int32, (1, LANES), 1) // HEAD_DIM
    return [lane == h for h in range(LANES // HEAD_DIM)]


def root_of(scale_ref, group):
    masks = head_masks()
    value = jnp.zeros((1, LANES), F32)
    for h, mask in enumerate(masks):
        value = jnp.where(mask, scale_ref[group * len(masks) + h], value)
    return jnp.sqrt(value)


def normed(values):
    scale = lax.rsqrt(jnp.mean(values * values, axis=-1, keepdims=True) + EPS)
    return values * scale, scale


def norm_back(unit, scale, mod, grad):
    inner = grad * (1.0 + mod)
    into = scale * (inner - unit * jnp.mean(inner * unit, axis=-1, keepdims=True))
    return into, jnp.sum(grad * unit, axis=0, keepdims=True)


def half_of(core, values):
    half = values.shape[1] // 2
    return jnp.where(core == 0, values[:, :half], values[:, half:])


def stacked(masks, values):
    zero = jnp.zeros_like(values)
    return jnp.concatenate([jnp.where(mask, values, zero) for mask in masks], axis=0)


def abreast(values, count):
    size = values.shape[0] // count
    return jnp.concatenate([values[i * size : (i + 1) * size] for i in range(count)], axis=1)


def struct(shape, dtype):
    return jax.ShapeDtypeStruct(shape, dtype)


class In:
    def __init__(self, *arrays, shape=None, plan=None, late=False, which=0):
        self.which = which
        self.arrays, self.shape, self.late = arrays, shape or arrays[0].shape, late
        whole = tuple(slice(None) for _ in self.shape)
        self.plan = plan or (lambda core: [[(0, whole, whole)]])


class Out:
    def __init__(self, shape, dtype, count=1, pieces=1, axis=1, into=(), cuts=None):
        self.struct, self.count, self.axis = struct(shape, dtype), count, axis
        self.cuts = cuts or [shape[axis] * i // pieces for i in range(pieces + 1)]
        self.pieces = len(self.cuts) - 1
        self.into = dict(into)

    def where(self, piece):
        if self.pieces == 1:
            return ...
        return (slice(None),) * self.axis + (slice(self.cuts[piece], self.cuts[piece + 1]),)


class Held:
    def __init__(self, ref, pieces):
        self.ref, self.shape, self.pieces = ref, ref.shape, pieces
        self.started, self.waited = set(), set()

    def start(self, piece):
        if piece < len(self.pieces) and piece not in self.started:
            self.started.add(piece)
            for copy in self.pieces[piece]:
                copy.start()

    def need(self, piece):
        self.start(piece)
        if piece not in self.waited:
            self.waited.add(piece)
            for copy in self.pieces[piece]:
                copy.wait()

    def start_all(self):
        for piece in range(len(self.pieces)):
            self.start(piece)

    def __getitem__(self, where):
        for piece in range(len(self.pieces)):
            self.need(piece)
        return self.ref[where]


class Made:
    def __init__(self, ref, copies):
        self.ref, self.copies, self.sent = ref, copies, set()

    def __setitem__(self, where, values):
        self.ref[where] = values

    def __getitem__(self, where):
        return self.ref[where]

    def send(self, piece=None):
        for i in range(len(self.copies)) if piece is None else (piece,):
            if i not in self.sent:
                self.sent.add(i)
                for copy in self.copies[i]:
                    copy.start()


def call(kernel, tables, inputs, outputs, scratch=()):
    arrays = [a for i in inputs for a in i.arrays]
    names, structs = [], []
    for i, o in enumerate(outputs):
        for k in range(o.count):
            name, column = o.into.get(k, ((i, k), 0))
            if name not in names:
                names.append(name)
                structs.append(o.struct)
            at = names.index(name)
            wide = max(structs[at].shape[-1], column + o.struct.shape[-1])
            structs[at] = struct((*o.struct.shape[:-1], wide), o.struct.dtype)

    def body(*refs):
        refs = list(refs)

        def some(count):
            taken = refs[:count]
            del refs[:count]
            return taken

        scalars, sources, targets = some(len(tables)), some(len(arrays)), some(len(structs))
        held, made = some(len(inputs)), some(len(outputs))
        in_sems, out_sems = some(len(inputs)), some(1)[0]
        extra = refs
        ins, outs = [], []
        for i, ref, sems in zip(inputs, held, in_sems):
            from_refs = [sources.pop(0) for _ in i.arrays]
            pieces, count = [], 0
            for piece in i.plan(scalars[0][i.which]):
                copies = []
                for which, a, b in piece:
                    copies.append(
                        pltpu.make_async_copy(from_refs[which].at[a], ref.at[b], sems.at[count])
                    )
                    count += 1
                pieces.append(copies)
            ins.append(Held(ref, pieces))
        for i, given in zip(ins, inputs):
            if not given.late:
                i.start(0)
        count = 0
        for o, ref in zip(outputs, made):
            copies = [[] for _ in range(o.pieces)]
            for k in range(o.count):
                name, column = o.into.get(k, ((len(outs), k), 0))
                target, source = targets[names.index(name)], ref if o.count == 1 else ref.at[k]
                if k in o.into:
                    target = target.at[:, column : column + o.struct.shape[-1]]
                for p in range(o.pieces):
                    where = o.where(p)
                    copies[p].append(
                        pltpu.make_async_copy(source.at[where], target.at[where], out_sems.at[count])
                    )
                    count += 1
            outs.append(Made(ref, copies))
        kernel(*scalars, *ins, *outs, *extra)
        for o in outs:
            o.send()
        for i in ins:
            for piece in range(len(i.pieces)):
                i.need(piece)
        for o in outs:
            for piece in o.copies:
                for copy in piece:
                    copy.wait()

    results = pl.pallas_call(
        body,
        out_shape=structs,
        in_specs=[pl.BlockSpec(memory_space=pltpu.SMEM)] * len(tables)
        + [pl.BlockSpec(memory_space=pltpu.HBM)] * len(arrays),
        out_specs=[pl.BlockSpec(memory_space=pltpu.HBM)] * len(structs),
        scratch_shapes=[pltpu.VMEM(i.shape, i.arrays[0].dtype) for i in inputs]
        + [
            pltpu.VMEM(o.struct.shape if o.count == 1 else (o.count, *o.struct.shape), o.struct.dtype)
            for o in outputs
        ]
        + [pltpu.SemaphoreType.DMA((sum(len(p) for p in i.plan(0)),)) for i in inputs]
        + [pltpu.SemaphoreType.DMA((sum(o.count * o.pieces for o in outputs),))]
        + list(scratch),
        compiler_params=pltpu.CompilerParams(vmem_limit_bytes=VMEM),
    )(*tables, *arrays)
    return list(results)


def at_half(core, which, size):
    part = core if which == 0 else 1 - core
    return pl.ds(pl.multiple_of(part * size, size), size)


def by_rows(own, got, parts=1, block=None, late=False):
    rows, cols = own.shape
    block = block or cols // parts

    def plan(core):
        for j in range(cols // parts // block):
            piece = []
            for p in range(parts):
                where = slice(p * (cols // parts) + j * block, p * (cols // parts) + (j + 1) * block)
                for k in range(2):
                    piece.append((k, (slice(None), where), (at_half(core, k, rows), where)))
            yield piece

    return In(own, got, shape=(2 * rows, cols), plan=plan, late=late)


def by_pieces(array, pieces, late=False):
    size = array.shape[-1] // pieces
    wheres = [
        (slice(None),) * (len(array.shape) - 1) + (slice(p * size, (p + 1) * size),)
        for p in range(pieces)
    ]
    return In(array, plan=lambda core: [[(0, where, where)] for where in wheres], late=late)


def by_rows_order(own, got, parts, block, order):
    made = by_rows(own, got, parts, block)
    pieces = made.plan

    def plan(core):
        every = list(pieces(core))
        return [every[i] for i in order]

    made.plan = plan
    return made


def by_row_blocks(own, got, block, late=False):
    rows, cols = own.shape

    def plan(core):
        for j in range(rows // block):
            piece = []
            for k in range(2):
                part = core if k == 0 else 1 - core
                there = pl.ds(pl.multiple_of(part * rows + j * block, block), block)
                piece.append((k, (slice(j * block, (j + 1) * block),), (there,)))
            yield piece

    return In(own, got, shape=(2 * rows, cols), plan=plan, late=late)


def image(own, got, mine=True, late=False):
    part, width = own.shape[1:]

    def plan(core):
        which = core if mine else 1 - core
        first, second = (0, 1) if mine else (1, 0)
        return [
            [
                (first, (which,), (slice(0, part),)),
                (second, (which,), (slice(part, 2 * part),)),
            ]
        ]

    return In(own, got, shape=(2 * part, width), plan=plan, late=late)


def pile(*arrays, width=None, pieces=1, halved=False, late=False):
    arrays = [a if isinstance(a, tuple) else (a, 0) for a in arrays]
    rows, cols = arrays[0][0].shape
    cols = (width or cols) // (2 if halved else 1)
    size = cols // pieces

    def plan(core):
        for p in range(pieces):
            there = slice(p * size, (p + 1) * size)
            piece = []
            for i, (_, first) in enumerate(arrays):
                at = first + p * size
                here = slice(at, at + size)
                if halved:
                    here = pl.ds(pl.multiple_of(core * cols + at, 128), size)
                piece.append((i, (slice(None), here), (slice(i * rows, (i + 1) * rows), there)))
            yield piece

    return In(*[a for a, _ in arrays], shape=(len(arrays) * rows, cols), plan=plan, late=late)


def norm_kernel(place, x, cond, mod, xs, mod_ff, hid_out, h1, row_one, row_two):
    core = place[0]
    rows = nn(cond[...], mod[...])
    first, second = rows[0:1], rows[1:2]
    row, row_sib = jnp.where(core == 0, first, second), jnp.where(core == 0, second, first)
    row_one[...] = row
    unit, _ = normed(x[...].astype(F32))
    hidden = (unit * (1.0 + row)).astype(BF)
    hid_out[...] = hidden
    hid_out.send()
    half = hidden.shape[1] // 2
    h1[:, :half] = half_of(core, hidden)
    unit, _ = normed(xs[...].astype(F32))
    h1[:, half:] = half_of(core, (unit * (1.0 + row_sib)).astype(BF))
    h1.send()
    rows = nn(cond[...], mod_ff[...])
    row_two[...] = jnp.where(core == 0, rows[0:1], rows[1:2])


def forward_kernel(
    place, scales, hid, weight, pos, posg, tab, x, out_weight, mod,
    q_out, k_out, v_out, att, hid_out, res_out,
):
    core = place[0]
    width = x.shape[1]
    hidden = hid[...]
    onehot = onehot_of(jnp.concatenate([pos[core], posg[core]], axis=1))
    ones = segment_matrix()
    masks = head_masks()
    heads = len(masks)
    spread = stacked(masks, jnp.ones((LANES, LANES), BF))
    steps = width // LANES
    weight.need(0)
    for j in range(1, steps):
        weight.start(j)
    tab[...]
    for j in range(steps):
        here = slice(j * LANES, (j + 1) * LANES)
        if j == 1:
            for i in (out_weight, x, mod):
                i.start(0)
            weight[...]
            for out in (q_out, k_out, v_out):
                out.send(0)
        q, k, v = [
            nn(hidden, weight.ref[:, i * width + j * LANES : i * width + (j + 1) * LANES])
            for i in range(3)
        ]
        v = v.astype(BF)
        q_out[:, here] = q
        k_out[:, here] = k
        v_out[:, here] = v
        tabs = tables_of(onehot, tab.ref, j * LANES)
        root = root_of(scales, j)
        qr = spin(q * (lax.rsqrt(segment_sum(q * q, ones) + EPS) * root), tabs, 1.0).astype(BF)
        kr = spin(k * (lax.rsqrt(segment_sum(k * k, ones) + EPS) * root), tabs, 1.0).astype(BF)
        expo = abreast(jnp.exp(nt(stacked(masks, qr), kr)).astype(BF), heads)
        total = (nn(expo, stacked(masks, v)) / nn(expo, spread)).astype(BF)
        att[:, here] = total
    for out in (q_out, k_out, v_out, att):
        out.send()
    residual = x[...].astype(F32) + nn(att[...], out_weight[...])
    res_out[...] = residual
    unit, _ = normed(residual)
    hid_out[...] = (unit * (1.0 + mod[...])).astype(BF)


def dealt(values, high, bit, axis):
    size = values.shape[1] // (2 * high)
    kept, sent = [], []
    for cell in range(2 * high):
        if not cell & axis:
            zero = values[:, cell * size : (cell + 1) * size]
            unit = values[:, (cell + axis) * size : (cell + axis + 1) * size]
            kept.append(jnp.where(bit == 0, zero, unit))
            sent.append(jnp.where(bit == 0, unit, zero))
    return jnp.concatenate(kept, axis=1), jnp.concatenate(sent, axis=1)


def feed_kernel(
    high, place, codes, losses, hid, up, og, down, ogs, res, mod,
    gu_a, gu_g, act, rlow_out, cots, mixed_out, mgrad_out, grad_ref, mix_ref,
):
    core, one, two = place[0], place[1], place[2]
    ff = up.shape[1] // 2
    block = ff // 4
    unit_cols = ff // (2 * high)
    half = high // 2
    scale = losses[codes[core]]
    order = (0, 2, 1, 3)
    hidden = hid[...]
    up.need(0)
    down.start(0)
    og.start(0)

    def gates(b):
        a = nn(hidden, up.ref[:, b * block : (b + 1) * block])
        return a, nn(hidden, up.ref[:, ff + b * block : ff + (b + 1) * block])

    def finish(b, a, g, first):
        here = slice(b * block, (b + 1) * block)
        there = slice(ff + b * block, ff + (b + 1) * block)
        phi = 0.5 + 0.5 * lax.erf(g * (1.0 / math.sqrt(2.0)))
        gelu = g * phi
        active = (a * gelu).astype(BF)
        slope = a * (phi + g * (jnp.exp(-0.5 * g * g) * (1.0 / math.sqrt(2.0 * math.pi))))
        act[jnp.where(core == b // 2, 0, 1), :, (b % 2) * block : (b % 2 + 1) * block] = active
        act_grad = nt(cot, down.ref[here])
        a_grad = (act_grad * gelu).astype(BF)
        g_grad = (act_grad * slope).astype(BF)
        for c in range(block // unit_cols):
            cell = b * (block // unit_cols) + c
            cols = slice(c * unit_cols, (c + 1) * unit_cols)
            z, y, x = cell // 4, cell // 2 % 2, cell % 2
            at = (2 * z + y) * unit_cols
            gu_a[jnp.where(one == x, 0, 1), :, at : at + unit_cols] = a_grad[:, cols]
            at = (2 * z + x) * unit_cols
            gu_g[jnp.where(two == y, 0, 1), :, at : at + unit_cols] = g_grad[:, cols]
        mixed = nn(active, down.ref[here])
        grad = nt(a_grad, up.ref[:, here]) + nt(g_grad, up.ref[:, there])
        mix_ref[...] = mixed if first else mix_ref[...] + mixed
        grad_ref[...] = grad if first else grad_ref[...] + grad

    gate = gates(order[0])
    cot = (og[...].astype(F32) * scale).astype(BF)
    cots[0] = cot
    down.need(0)
    up.start(1)
    finish(order[0], *gate, True)
    up.need(1)
    for i in (up, down, ogs, res, mod):
        i.start_all()
    finish(order[1], *gates(order[1]), False)
    for i in (up, down, ogs, res, mod):
        i[...]
    if high == 4:
        gu_a.send(0)
        gu_a.send(2)
        act.send(0)
    cots[1] = (ogs[...].astype(F32) * losses[codes[1 - core]]).astype(BF)
    cots.send()
    later = gates(order[2])
    finish(order[2], *later, False)
    finish(order[3], *gates(order[3]), False)
    for i in range(4):
        gu_a.send(i)
    gu_g.send(0)
    act.send()
    residual = res[...]
    unit, size = normed(residual)
    into, mgrad = norm_back(unit, size, mod[...], grad_ref[...])
    mgrad_out[...] = mgrad
    total = og[...].astype(F32) * scale + into
    low = total.astype(BF)
    rlow_out[...] = low
    middle, end = low.shape[1] // 2, ff // 2
    for out, values, bit, axis in ((gu_a, low[:, :middle], one, 1), (gu_g, low[:, middle:], two, 2)):
        kept, sent = dealt(values, high, bit, axis)
        out[0, :, end:] = kept
        out[1, :, end:] = sent
        out.send()
    rlow_out.send()
    mixed_out[...] = (residual + mix_ref[...]).astype(BF)


def backward_kernel(
    high, place, scales, rlow, weight, q_in, k_in, v_in, pos, posg, tab, qkv, x, mod, row_two, cond,
    cells_a, cells_g, rows_out, cond_out, scale_out, tgrad_out, qkv_out,
):
    core, one, two = place[0], place[1], place[2]
    width = x.shape[1]
    onehot = onehot_of(jnp.concatenate([pos[core], posg[core]], axis=1))
    ones = segment_matrix()
    masks = head_masks()
    heads = len(masks)
    low = rlow[...]
    for j in range(width // LANES):
        here = slice(j * LANES, (j + 1) * LANES)
        if j == 0:
            for i in (weight, q_in, k_in, v_in, tab):
                i.start_all()
            for i in (weight, q_in, k_in, v_in, tab):
                i.need(0)
        if j == 1:
            for i in (qkv, x, mod, row_two, cond):
                i.start_all()
            for i in (weight, q_in, k_in, v_in, tab):
                i[...]
        grad = nt(low, weight.ref[here]).astype(BF)
        tabs = tables_of(onehot, tab.ref, j * LANES)
        root = root_of(scales, j)
        q, k, v = q_in.ref[:, here], k_in.ref[:, here], v_in.ref[:, here]
        q_inv = lax.rsqrt(segment_sum(q * q, ones) + EPS)
        k_inv = lax.rsqrt(segment_sum(k * k, ones) + EPS)
        q_scale, k_scale = q_inv * root, k_inv * root
        qr = spin(q * q_scale, tabs, 1.0).astype(BF)
        kr = spin(k * k_scale, tabs, 1.0).astype(BF)
        q_heads, g_heads = stacked(masks, qr), stacked(masks, grad)
        expo = jnp.exp(nt(kr, q_heads))
        prob = expo * (1.0 / jnp.sum(expo, axis=0, keepdims=True))
        weighted = prob * nt(v, g_heads)
        sgrad = (weighted - prob * jnp.sum(weighted, axis=0, keepdims=True)).astype(BF)
        dv = nn(prob.astype(BF), g_heads).astype(BF)
        dk = spin(nn(sgrad, q_heads), tabs, -1.0)
        size = qr.shape[0]
        turned = jnp.concatenate(
            [sgrad[:, i * size : (i + 1) * size] for i in range(heads)], axis=0
        )
        dq = spin(tn(turned, stacked(masks, kr)), tabs, -1.0)
        q_dot, k_dot = dq * q, dk * k
        scale_out[:, here] = jnp.sum(q_dot * q_scale + k_dot * k_scale, axis=0, keepdims=True)
        gq = (q_scale * (dq - q * (segment_sum(q_dot, ones) * (q_inv * q_inv)))).astype(BF)
        gk = (k_scale * (dk - k * (segment_sum(k_dot, ones) * (k_inv * k_inv)))).astype(BF)
        for i, part in enumerate((gq, gk, dv)):
            qkv_out[:, i * width + j * LANES : i * width + (j + 1) * LANES] = part
    every = cond[...].astype(F32)
    cond_out[...] = jnp.where(core == 0, every[0:1], every[1:2])
    middle = qkv_out.shape[1] // 2
    for out, at, bit, axis in ((cells_a, 0, one, 1), (cells_g, middle, two, 2)):
        kept, sent = dealt(qkv_out[:, at : at + middle], high, bit, axis)
        out[0] = kept
        out[1] = sent
        out.send()
    unit, size = normed(x[...].astype(F32))
    into, mgrad = norm_back(unit, size, mod[...], nt(qkv_out[...], qkv[...]))
    tgrad_out[...] = low.astype(F32) + into
    for i, row in enumerate((mgrad, row_two[...])):
        kept, sent = dealt(row, high // 2, place[3], 1)
        rows_out[0, :, i * kept.shape[1] : (i + 1) * kept.shape[1]] = kept
        rows_out[1, :, i * kept.shape[1] : (i + 1) * kept.shape[1]] = sent


def down_weight_kernel(place, cols_in, rows_in, out_a, out_b):
    parts, size, half = out_a.ref.shape[1:]
    for j in range(2 * parts):
        total = tn(cols_in[:, j * size : (j + 1) * size], rows_in[...]).astype(BF)
        slot = jnp.where(place[3] == j % 2, 0, 1)
        out_a[slot, j // 2] = total[:, :half]
        out_b[slot, j // 2] = total[:, half:]
        if j % 2:
            out_a.send(j // 2)
            out_b.send(j // 2)


def gate_weight_kernel(cuts, place, *refs):
    one, two = place[1], place[2]
    out_a, out_g = refs[4 * len(cuts) :]
    ins_a, ins_g = refs[: 2 * len(cuts)], refs[2 * len(cuts) : 4 * len(cuts)]
    for ins, out, mine in ((ins_a, out_a, two), (ins_g, out_g, one)):
        if out is out_a:
            for i in ins_a:
                i[...]
            for i in ins_g:
                i.start_all()
        for z in range(out_a.ref.shape[1]):
            start = 0
            for p, size in enumerate(cuts):
                cols_in, rows_in = ins[2 * p : 2 * p + 2]
                total = tn(cols_in[:, 2 * z * size : 2 * (z + 1) * size], rows_in[...]).astype(BF)
                for i in range(2):
                    out[jnp.where(mine == i, 0, 1), z, start : start + size] = total[
                        i * size : (i + 1) * size
                    ]
                start += size
            out.send(z)


def combine_kernel(counts, place, *refs):
    sent_out, kept_out = refs[sum(counts) :]
    first = at = 0
    for count in counts:
        terms = refs[at : at + count]
        at += count
        total = sum(t[...].astype(F32) for t in terms).astype(BF)
        size = total.shape[1]
        sent_out[first : first + size] = total[0]
        kept_out[first : first + size] = total[1]
        first += size


def combine(place, which, groups):
    def term(array):
        outer, _, rows, lanes = array.shape

        def plan(bit):
            return [[(0, (slice(None), 1 - bit), (0,)), (0, (slice(None), bit), (1,))]]

        return In(array, shape=(2, outer, rows, lanes), plan=plan, which=which)

    ins = [term(a) for group in groups for a in group]
    outer = sum(group[0].shape[0] for group in groups)
    rows, lanes = groups[0][0].shape[2:]
    return call(
        functools.partial(combine_kernel, [len(group) for group in groups]),
        [place],
        ins,
        [Out((outer, rows, lanes), BF)] * 2,
    )


def shards(n, tokens, condition, positions, weight_codes, loss_table, out_grad, mod_attn,
           qkv_weight, attn_scale, out_weight, mod_ff, up_weight, down_weight):
    images, part, width = tokens.shape
    rows = images * part
    half = width // 2
    heads = attn_scale.shape[0]
    ff = 2 * down_weight.shape[0]
    low = 1 if n <= 16 else n // 8
    high = n // (4 * low)
    me = lax.axis_index("dp")
    core = lax.axis_index("seq")
    one = (me // low) % 2
    two = (me // (2 * low)) % 2
    three = (me // (4 * low)) % 2
    bit_strides = [low, 2 * low, 4 * low]
    bit_strides += [1 << i for i in range(n.bit_length() - 1) if 1 << i not in bit_strides]
    place = jnp.stack([core] + [(me // b) % 2 for b in bit_strides]).astype(jnp.int32)

    def swap(values):
        return lax.ppermute(values, "seq", [(0, 1), (1, 0)])

    def cross(values, stride):
        return lax.ppermute(
            values, "dp", [(i, i + stride - 2 * stride * ((i // stride) % 2)) for i in range(n)]
        )

    def pick(values, index, axis=0):
        return lax.dynamic_index_in_dim(values, index, axis, keepdims=False)

    def tie(*values):
        return lax.optimization_barrier(values)

    first = swap(tokens), swap(mod_attn), swap(mod_ff), swap(positions)
    tokens_got, mod_attn_got, mod_ff_got, pos_got, qkv_w, out_w = tie(
        *first, qkv_weight, out_weight
    )
    qkv_got, out_got = swap(qkv_w), swap(out_w)
    hidden_one, h1, mod_one, mod_two = call(
        norm_kernel,
        [place],
        [image(tokens, tokens_got), In(condition), by_rows(mod_attn, mod_attn_got)]
        + [image(tokens, tokens_got, False), by_rows(mod_ff, mod_ff_got)],
        [Out((rows, width), BF), Out((rows, width), BF), Out((1, width), F32)]
        + [Out((1, width), F32)],
    )
    qkv_got, out_got, hidden_one, og_w, up_w, down_w = tie(
        qkv_got, out_got, hidden_one, out_grad, up_weight, down_weight
    )
    og_got, up_got, down_got = swap(og_w), swap(up_w), swap(down_w)
    h1_one, h1_two = cross(h1, low), cross(h1, 2 * low)

    table = In(jnp.asarray(angle_constants(heads)))
    pos_in = [In(positions), In(pos_got)]
    q_raw, k_raw, value, both, res = call(
        forward_kernel,
        [place, attn_scale],
        [In(hidden_one), by_rows(qkv_weight, qkv_got, 3, LANES)]
        + pos_in
        + [table, image(tokens, tokens_got, late=True)]
        + [by_rows(out_weight, out_got, late=True), In(mod_two, late=True)],
        [Out((rows, width), dtype, 1, width // LANES) for dtype in (F32, F32, BF)]
        + [Out((rows, width), BF, into={0: ("both", width)})]
        + [Out((rows, width), BF, into={0: ("both", 0)}), Out((rows, width), F32)],
    )
    both, h1_one, h1_two = tie(both, h1_one, h1_two)
    both_one, both_two, both_sib = cross(both, low), cross(both, 2 * low), swap(both)

    block = ff // 4
    wide = ff // 2 + width // 4
    gate = call(
        functools.partial(feed_kernel, high),
        [place, weight_codes, loss_table],
        [pile((both, 0), width=width), by_rows_order(up_weight, up_got, 2, block, (0, 2, 1, 3))]
        + [image(out_grad, og_got, late=True), by_row_blocks(down_weight, down_got, block, True)]
        + [image(out_grad, og_got, False, True), In(res, late=True), In(mod_two, late=True)],
        [Out((rows, wide), BF, 2, into={0: ("pack", 0)}, cuts=[*range(0, ff // 2 + 1, ff // 8), wide])]
        + [Out((rows, wide), BF, 2, into={0: ("pack", wide)}, cuts=[0, ff // 2, wide])]
        + [Out((rows, ff // 2), BF, 2, 2, into={1: ("pack", 2 * wide)})]
        + [Out((rows, width), BF), Out((rows, width), BF, 2), Out((rows, width), BF)]
        + [Out((1, width), F32)],
        [pltpu.VMEM((rows, width), F32)] * 2,
    )
    pack, send_a, send_g, act_own, res_low, cot, cot_sib, *rest = gate
    mixed_mine, mod_two_grad = rest
    send_a, send_g, pack, res_low, both_one, both_two, both_sib = tie(
        send_a, send_g, pack, res_low, both_one, both_two, both_sib
    )
    pair_a, pair_g = cross(send_a, low), cross(send_g, 2 * low)
    pack_sib, both_one_sib, both_two_sib = swap(pack), swap(both_one), swap(both_two)

    third = 3 * width // 4
    cond_cols = condition.shape[1]
    keep_q, send_qa, send_qg, line_kept, line, tokens_mine = call(
        functools.partial(backward_kernel, high),
        [place, attn_scale],
        [In(res_low), by_row_blocks(out_weight, out_got, LANES)]
        + [by_pieces(a, width // LANES) for a in (q_raw, k_raw, value)]
        + pos_in
        + [table, by_rows(qkv_weight, qkv_got, late=True), image(tokens, tokens_got, True, True)]
        + [In(a, late=True) for a in (mod_one, mod_two_grad, condition)],
        [Out((rows, third), BF, 2, into={0: ("keep", 0)})]
        + [Out((rows, third), BF, 2, into={0: ("keep", third)})]
        + [Out((1, width), F32, 2, into={1: ("line", 0)})]
        + [Out((1, cond_cols), F32, into={0: ("line", width)})]
        + [Out((1, width), F32, into={0: ("line", width + cond_cols)})]
        + [Out((rows, width), F32)],
        [pltpu.VMEM((rows, 3 * width), BF)],
    )
    cot, keep_q, send_qa, send_qg, pack_sib, both_one_sib, both_two_sib = tie(
        cot, keep_q, send_qa, send_qg, pack_sib, both_one_sib, both_two_sib
    )

    def take(values, index, axis=0):
        return pick(values, index, axis).astype(F32)

    high_bits, low_bits = high.bit_length() - 1, low.bit_length() - 1
    high_strides = [4 * low << (high_bits - 1 - i) for i in range(high_bits)]
    low_strides = [1 << (low_bits - 1 - i) for i in range(low_bits)]
    line_strides, line_order = high_strides + low_strides, high_strides[::-1] + low_strides

    def hand_on(grads, rest, stride):
        bit = (me // stride) % 2
        split = grads.reshape(grads.shape[0], 2, 2, -1)
        sent = pick(split, 1 - bit, 2).reshape(grads.shape[0], -1)
        got = cross(jnp.concatenate([sent, rest], axis=1), stride)
        return pick(split, bit, 2).reshape(grads.shape[0], -1), rest, got, bit

    def taken(mine, rest, got, bit):
        mine = jnp.concatenate([mine, rest], axis=1)
        every = jnp.where(
            bit == 0,
            jnp.concatenate([mine, got], axis=0),
            jnp.concatenate([got, mine], axis=0),
        )
        wide = mine.shape[1] - rest.shape[1]
        return every[:, :wide].reshape(every.shape[0], 2, -1), every[:, wide:]

    line_steps = [s for s in (n >> (i + 1) for i in range(n.bit_length() - 1)) if s != 4 * low]
    keep_q_sib = swap(keep_q)
    pair_qa, pair_qg = cross(send_qa, low), cross(send_qg, 2 * low)

    down = call(
        down_weight_kernel,
        [place],
        [pile(cot, cot_sib), pile(act_own, (pack_sib, 2 * wide), width=ff // 2)],
        [Out((high // 2, width // high, ff // 4), BF, 2, high // 2, 0)] * 2,
    )
    line_got = cross(line, 4 * low)
    pair_a, pair_g, line_got, down[0] = tie(pair_a, pair_g, line_got, down[0])
    small = [line_kept, line[:, width:], line_got, three]
    down_got_a = cross(down[1], 4 * low)
    def rows_of(first, far, far_sib):
        return pile(
            (both, first), (both_sib, first), (far, first), (far_sib, first), width=width, halved=True
        )

    def late(value):
        return value

    def gate_weight(cuts, ins_a, ins_g):
        return call(
            functools.partial(gate_weight_kernel, cuts),
            [place],
            ins_a + [late(i) for i in ins_g],
            [Out((high // 2, sum(cuts), half), BF, 2, high // 2, 0)] * 2,
        )

    pair_a_sib, pair_g_sib = swap(pair_a), swap(pair_g)
    up_parts = gate_weight(
        [ff // (2 * high)],
        [
            pile(pack, pack_sib, pair_a, pair_a_sib, width=ff // 2),
            rows_of(0, both_one, both_one_sib),
        ],
        [
            pile((pack, wide), (pack_sib, wide), pair_g, pair_g_sib, width=ff // 2),
            rows_of(0, both_two, both_two_sib),
        ],
    )
    up_parts[0], down_got_a, pair_qa, pair_qg, keep_q_sib = tie(
        up_parts[0], down_got_a, pair_qa, pair_qg, keep_q_sib
    )
    up_last = cross(up_parts[1], 2 * low), cross(up_parts[3], low)
    down_got_b = cross(down[3], 4 * low)
    def step(groups, axes, stride, lead=1):
        outer = lead << axes.index(stride)
        groups = [[v.reshape(outer, 2, -1, v.shape[-1]) for v in group] for group in groups]
        sent, kept = combine(place, 1 + bit_strides.index(stride), groups)
        return [kept, cross(sent, stride)]

    def without(axes, *strides):
        return [a for a in axes if a not in strides]

    down_axes = high_strides[:-1] + [2 * low, low] + low_strides
    down_order = [low, 2 * low] + high_strides[:-1][::-1] + low_strides
    pair_qa_sib, pair_qg_sib = swap(pair_qa), swap(pair_qg)
    at = ff // 2
    last_parts = gate_weight(
        [width // (4 * high), 3 * width // (4 * high)],
        [
            pile((pack, at), (pack_sib, at), (pair_a, at), (pair_a_sib, at), width=width // 4),
            rows_of(width, both_one, both_one_sib),
            pile(keep_q, keep_q_sib, pair_qa, pair_qa_sib, width=third),
            pile((h1, 0), (h1, half), (h1_one, 0), (h1_one, half), width=half),
        ],
        [
            pile(
                *((pack, wide + at), (pack_sib, wide + at), (pair_g, at), (pair_g_sib, at)),
                width=width // 4,
            ),
            rows_of(width, both_two, both_two_sib),
            pile((keep_q, third), (keep_q_sib, third), pair_qg, pair_qg_sib, width=third),
            pile((h1, 0), (h1, half), (h1_two, 0), (h1_two, half), width=half),
        ],
    )
    last_last = cross(last_parts[1], 2 * low), cross(last_parts[3], low)
    last_parts[0], down_got_b, small[2], *up_last = tie(
        last_parts[0], down_got_b, small[2], *up_last
    )

    def first_line(parts, got):
        if high > 2:
            groups = [[parts[2 * i], got[i]] for i in range(2)]
            return step(groups, high_strides[1:] + low_strides, line_order[0])
        groups = [[jnp.concatenate(v, axis=0) for v in ((parts[0], parts[2]), got)]]
        return step(groups, high_strides + low_strides, line_order[0])

    def rest_of(kept, got, axes, order, lead=1):
        for stride in order:
            kept, got = step([[kept, got]], axes, stride, lead)
            axes = without(axes, stride)
        return [kept, got]

    line_axes = without(high_strides + low_strides, line_order[0])

    up_line = first_line(up_parts, up_last)
    up_line[0], small[2] = tie(up_line[0], small[2])
    small = list(hand_on(*taken(*small), line_steps[0]))
    *last_last, up_line[0] = tie(*last_last, up_line[0])
    last_line = first_line(last_parts, last_last)
    down[0], last_line[0] = tie(down[0], last_line[0])
    down_line = step([[down[0], down_got_a], [down[2], down_got_b]], down_axes, down_order[0])
    up_line[1], last_line[0], small[2] = tie(up_line[1], last_line[0], small[2])
    up_line = rest_of(*up_line, line_axes, line_order[1:2])
    small = list(hand_on(*taken(*small), line_steps[1]))
    down_axes = without(down_axes, down_order[0])
    down_line[1], up_line[0] = tie(down_line[1], up_line[0])
    down_line = rest_of(*down_line, down_axes, down_order[1:2], 2)
    last_line[1], down_line[0], small[2] = tie(last_line[1], down_line[0], small[2])
    last_line = rest_of(*last_line, line_axes, line_order[1:2])
    down_line[0], mixed_mine, tokens_mine = tie(down_line[0], mixed_mine, tokens_mine)
    down_line = rest_of(*down_line, without(down_axes, down_order[1]), down_order[2:], 2)
    up_line[1], last_line[1], down_line[0], line_kept, line, *small[:3] = tie(
        up_line[1], last_line[1], down_line[0], line_kept, line, *small[:3]
    )
    for stride in line_steps[2:]:
        small = hand_on(*taken(*small), stride)
    grads, rest = taken(*small)

    total = lambda kept, got: kept.astype(F32) + got.astype(F32)
    line_axes = without(line_axes, line_order[1])
    down_sum = total(*down_line)
    down_sum = jnp.concatenate([v.reshape(-1, ff // 4) for v in jnp.split(down_sum, 2)], axis=1)
    up_sum = total(*rest_of(*up_line, line_axes, line_order[2:])).reshape(-1, half)
    last_sum = total(*rest_of(*last_line, line_axes, line_order[2:])).reshape(-1, half)

    cond_rows = mod_attn.shape[0]
    grads = grads.reshape(grads.shape[0], -1)
    wide = grads.shape[1]
    every = jnp.concatenate([grads, rest], axis=1)
    every = jnp.concatenate([every, swap(every)], axis=0)
    cond_all = lax.dynamic_slice_in_dim(every, wide + core * cond_rows, cond_rows, 1)
    mod_attn_grad = jnp.dot(cond_all.T, every[:, : wide // 2], precision=FINEST)
    mod_ff_grad = jnp.dot(cond_all.T, every[:, wide // 2 : wide], precision=FINEST)
    lanes = jnp.sum(every[:, wide + cond_cols :].reshape(2, -1, width), axis=1)
    lanes = jnp.sum((lanes[0] + lanes[1]).reshape(heads, HEAD_DIM), axis=1)
    scale_grad = lanes / (2.0 * attn_scale)

    def row_of(parts):
        cells = parts.reshape(2, high // 2, -1)
        cells = jnp.where(three == 0, cells, cells[::-1])
        return jnp.swapaxes(cells, 0, 1).reshape(1, width)

    mods = jnp.concatenate([mod_attn, mod_ff], axis=1)
    mine = [jnp.concatenate([a, b], axis=0) for a, b in zip(*[jnp.split(v[:, :width], 2, axis=1) for v in (line_kept, line)])]
    mine = jnp.concatenate([row_of(v) for v in mine], axis=1)
    got = swap(mine)
    pair = jnp.where(
        core == 0, jnp.concatenate([mine, got], axis=0), jnp.concatenate([got, mine], axis=0)
    )
    cond_part = jnp.dot(pair, mods.astype(F32).T, precision=FINEST)
    cond_got = swap(cond_part)
    condition_grad = jnp.where(
        core == 0,
        jnp.concatenate([cond_part, cond_got], axis=1),
        jnp.concatenate([cond_got, cond_part], axis=1),
    )

    out_cols = last_sum.shape[0] // 4

    def home(values):
        got = swap(values[part:])
        own = values[:part]
        return jnp.where(core == 0, jnp.stack([own, got]), jnp.stack([got, own]))

    def turned(values):
        return values.astype(F32).T

    return (
        home(mixed_mine),
        home(tokens_mine),
        condition_grad,
        mod_attn_grad,
        turned(last_sum[out_cols:]),
        scale_grad,
        turned(last_sum[:out_cols]),
        mod_ff_grad,
        turned(up_sum),
        turned(down_sum),
    )


def solution(mesh):
    n = mesh.shape["dp"]

    def body(*args):
        return shards(n, *args)

    return jax.shard_map(
        body,
        mesh=mesh,
        in_specs=(
            P("dp", "seq", None),
            P("dp", None),
            P("dp", None, "seq"),
            P("dp"),
            P(),
            P("dp", "seq", None),
            P("seq", None),
            P("seq", None),
            P(),
            P("seq", None),
            P("seq", None),
            P("seq", None),
            P("seq", None),
        ),
        out_specs=(
            P("dp", "seq", None),
            P("dp", "seq", None),
            P("dp", None),
            P("seq", "dp"),
            P("seq", "dp"),
            P(),
            P("seq", "dp"),
            P("seq", "dp"),
            P("seq", "dp"),
            P("seq", "dp"),
        ),
        check_vma=False,
    )
```
